32 devices in a mesh: dp: 16 (over z, y, x), shard: 2 (over core).
Axes of the slice: x: 2, y: 2, z: 4, core: 2. Of those that a mesh axis runs over, the one named last changes fastest.
Arguments:
- features: bfloat16 [24576, 1024], P('dp'), may hold values from -6 to 6
- condition: bfloat16 [1536, 1152], P('dp'), may hold values from -6 to 6
- task_ids: int32 [1536], P('dp'), may hold values from 0 to 49, never falling along the last dimension, each value on 1 to 61 neighbouring positions
- conv_first: bfloat16 [5, 1024, 1024], P(None, 'dp', 'shard'), may hold values from -0.078125 to 0.078125
- conv_second: bfloat16 [5, 1024, 1024], P(None, 'dp', 'shard'), may hold values from -0.078125 to 0.078125
- film_weight: bfloat16 [1152, 2048], P('dp', 'shard'), may hold values from -0.1875 to 0.1875
- norm_gain_first: bfloat16 [1024], P(('dp', 'shard')), may hold values from 0.099609375 to 1.8984375
- norm_shift_first: bfloat16 [1024], P(('dp', 'shard')), may hold values from -3 to 3
- norm_gain_second: bfloat16 [1024], P(('dp', 'shard')), may hold values from 0.099609375 to 1.8984375
- norm_shift_second: bfloat16 [1024], P(('dp', 'shard')), may hold values from -3 to 3
- film_bias: bfloat16 [2048], P(('dp', 'shard')), may hold values from -3 to 3
- task_table: bfloat16 [50, 1152], replicated, may hold values from -3 to 3
- out_grad: bfloat16 [24576, 1024], P('dp'), may hold values from -6 to 6
- grad_mask: int32 [24576], P('dp'), may hold values 0 or 1
Outputs:
- block_out: bfloat16 [24576, 1024], P('dp')
- grad_features: bfloat16 [24576, 1024], P('dp')
- grad_conv_first: float32 [5, 1024, 1024], P(None, 'dp', 'shard')
- grad_conv_second: float32 [5, 1024, 1024], P(None, 'dp', 'shard')
- grad_film_weight: float32 [1152, 2048], P('dp', 'shard')
- grad_gain_first: float32 [1024], P(('dp', 'shard'))
- grad_shift_first: float32 [1024], P(('dp', 'shard'))
- grad_gain_second: float32 [1024], P(('dp', 'shard'))
- grad_shift_second: float32 [1024], P(('dp', 'shard'))
- grad_film_bias: float32 [2048], P(('dp', 'shard'))
- grad_task_table: float32 [50, 1152], replicated
The draws below stay inside these ranges and needn't reach their ends.
Inputs may be any that keep to these rules, and one draw needn't show every extreme that they name: `task_ids`: task numbers never fall along the samples; every task has one or more samples.
All inputs are finite; a program needn't handle non-finite values. No bound on the sum of `grad_mask` on one device may be relied on, other than what follows from the above.
Results may differ from the reference program's by a relative error of at most 0.0064.
Values may be sent and summed in bfloat16 or wider, within the bound.
No kernel may reach another device: no remote copies, remote signals or barrier semaphores. Data moves between devices by JAX's collectives and lax.ppermute only.
A program may use at most 256 MiB of HBM per device.

```python
import math
import jax
import jax.numpy as jnp
import numpy as np
from jax import lax

CHANNELS = 1024
CONDITION = 1152
TASKS = 50
KERNEL = 5
GROUPS = 8
HORIZON = 16
SAMPLES = 1536
FRAMES = 24576


def touch_ends(array, key, low, top_value):
    dims = array.shape
    place = [jax.random.randint(jax.random.fold_in(key, axis), (), 0, dims[axis]) for axis in range(len(dims))]
    array = array.at[tuple(place)].set(low)
    longest = dims.index(max(dims))
    place[longest] = (place[longest] + 1) % dims[longest]
    return array.at[tuple(place)].set(top_value)


def raised(values, own_key, source, target, shards_of, factor):
    def block_of(dim):
        return (jnp.arange(values.shape[dim]) // (values.shape[dim] // shards_of)).reshape((-1,) + (1,) * (values.ndim - 1 - dim))

    near = jax.random.permutation(own_key, shards_of)[block_of(target)]
    other_side = (block_of(target) + shards_of // 2) % shards_of
    return jnp.where((block_of(source) == near) | (block_of(source) == other_side), factor * values, values)


def levels(own_key, extent, shards, least, largest):
    loudness, own = 1.0, jax.random.fold_in(own_key, 6)
    for dim, parts in shards:
        draws = jnp.exp(jax.random.uniform(jax.random.fold_in(own, dim), (parts,), jnp.float32, least / len(shards), largest / len(shards)))
        loudness = loudness * jnp.repeat(draws, extent[dim] // parts).reshape([-1 if axis == dim else 1 for axis in range(len(extent))])
    return loudness


def length_profile(number_of, total, bound, lean):
    portions = [(1 << 20) // math.isqrt(standing ** lean) + 1 for standing in range(2, number_of + 1)]
    rest, counts = total - bound - (number_of - 1), [1] * (number_of - 1)
    while rest > 0:
        free = [i for i in range(number_of - 1) if counts[i] < bound]
        whole, budget = sum([portions[i] for i in free]), rest
        for i in free:
            extra = min(bound - counts[i], max(1, budget * portions[i] // whole), rest)
            counts[i] = counts[i] + extra
            rest = rest - extra
    return np.array([bound] + counts)


def uneven(key, number_of, total, most, skew):
    if number_of == 2:
        one = jax.random.randint(key, (), max(1, total - most), min(most, total - 1) + 1)
        return jnp.stack([one, total - one])
    tallies = jnp.asarray(length_profile(number_of, total, most, skew), jnp.int32)
    twos = (number_of - 1) // 2
    source_of, taker = tallies[1:1 + 2 * twos:2], tallies[2:2 + 2 * twos:2]
    margin = jnp.minimum(source_of - 1, most - taker)
    passed = jax.random.randint(jax.random.fold_in(key, 1), (twos,), 0, 1 << 20) % (margin + 1)
    tallies = tallies.at[1:1 + 2 * twos:2].set(source_of - passed).at[2:2 + 2 * twos:2].set(taker + passed)
    return tallies[jax.random.permutation(jax.random.fold_in(key, 2), number_of)]


def scatter_about(stream_key, dims, scale, bound, shards=(), held_as=jnp.bfloat16):
    entries = scale * jax.random.normal(stream_key, dims, jnp.float32)
    if shards:
        entries = entries * levels(stream_key, dims, shards, -0.22, 0.18)
    return jnp.clip(entries, -bound, bound).astype(held_as)


def heavy_noise(rng, shape, scale, most, cuts, heavy, dtype=jnp.bfloat16):
    result = scale * jax.random.normal(rng, shape, jnp.float32)
    if cuts:
        result = result * levels(rng, shape, cuts, -0.22, 0.18)
    return jnp.clip(raised(result, jax.random.fold_in(rng, 3), *heavy), -most, most).astype(dtype)


def setup_inputs(seed: int = 0) -> dict:
    key_list = jax.random.split(jax.random.key(seed), 15)
    return {
        "features": heavy_noise(key_list[0], (FRAMES, CHANNELS), 1.0, 6.0, ((0, 16),), (0, 1, 16, 2.0)),
        "condition": scatter_about(key_list[1], (SAMPLES, CONDITION), 1.0, 6.0, ((0, 16),)),
        "task_ids": jnp.searchsorted(jnp.cumsum(uneven(key_list[2], TASKS, SAMPLES, 2 * SAMPLES // TASKS, 1)), jnp.arange(SAMPLES), side="right").astype(jnp.int32),
        "conv_first": scatter_about(key_list[3], (KERNEL, CHANNELS, CHANNELS), (KERNEL * CHANNELS) ** -0.5, 0.078125, ((1, 16), (2, 2))),
        "conv_second": scatter_about(key_list[4], (KERNEL, CHANNELS, CHANNELS), (KERNEL * CHANNELS) ** -0.5, 0.078125, ((1, 16), (2, 2))),
        "film_weight": scatter_about(key_list[5], (CONDITION, 2 * CHANNELS), CONDITION ** -0.5, 0.1875, ((0, 16), (1, 2))),
        "norm_gain_first": jnp.clip(1.0 + 0.18 * jax.random.normal(key_list[6], (CHANNELS,), jnp.float32), 0.099609375, 1.8984375).astype(jnp.bfloat16),
        "norm_shift_first": scatter_about(key_list[7], (CHANNELS,), 0.5, 3.0, ((0, 32),)),
        "norm_gain_second": jnp.clip(1.0 + 0.18 * jax.random.normal(key_list[8], (CHANNELS,), jnp.float32), 0.099609375, 1.8984375).astype(jnp.bfloat16),
        "norm_shift_second": scatter_about(key_list[9], (CHANNELS,), 0.5, 3.0, ((0, 32),)),
        "film_bias": scatter_about(key_list[10], (2 * CHANNELS,), 0.5, 3.0, ((0, 32),)),
        "task_table": scatter_about(key_list[11], (TASKS, CONDITION), 0.5, 3.0),
        "out_grad": scatter_about(key_list[12], (FRAMES, CHANNELS), 1.0, 6.0, ((0, 16),)),
        "grad_mask": touch_ends((jax.random.randint(key_list[13], (FRAMES,), 0, 4) < 3).astype(jnp.int32), jax.random.fold_in(key_list[13], 1), 0, 1),
    }


@jax.custom_vjp
def low(v):
    return lax.optimization_barrier(v.astype(jnp.bfloat16)).astype(jnp.float32)

@jax.custom_vjp
def low_back(v):
    return v

def low_keep(v):
    return (low(v), None)

def low_pass(kept, grad):
    return (grad,)

def back_keep(v):
    return (v, None)

def back_low(kept, grad):
    return (low(grad),)
low.defvjp(low_keep, low_pass)
low_back.defvjp(back_keep, back_low)

def mish_act(values):
    return values * jnp.tanh(jax.nn.softplus(values))

def shifted(values, offset):
    horizon = values.shape[1]
    half_kernel = KERNEL // 2
    padded = jnp.pad(values, ((0, 0), (half_kernel, half_kernel), (0, 0)))
    return lax.slice_in_dim(padded, half_kernel + offset, half_kernel + offset + horizon, axis=1)

def conv_apply(values, weight):
    half_kernel = KERNEL // 2
    columns = jnp.concatenate([shifted(values, offset - half_kernel) for offset in range(KERNEL)], axis=2)
    flat_weight = weight.reshape(KERNEL * CHANNELS, CHANNELS)
    return jnp.einsum('sha,ao->sho', columns, flat_weight, precision=lax.Precision.HIGHEST)

def group_norm(activations, gain, shift):
    samples = activations.shape[0]
    grouped = activations.reshape(samples, HORIZON, GROUPS, CHANNELS // GROUPS)
    centre = grouped - lax.optimization_barrier(jnp.mean(grouped, axis=(1, 3), keepdims=True))
    spread = lax.rsqrt(lax.optimization_barrier(jnp.mean(centre * centre, axis=(1, 3), keepdims=True)) + 1e-05)
    unit = (centre * spread).reshape(activations.shape)
    return unit * gain + shift

def block_forward(weights_f32, feat_block, cond_block, task_block):
    conv_a, conv_b, film_w, gain_a, shift_a, gain_b, shift_b, film_b, table = weights_f32
    samples = cond_block.shape[0]
    inputs = feat_block.reshape(samples, HORIZON, CHANNELS)
    first_conv = low_back(conv_apply(low(inputs), low(conv_a)))
    mixed_a = mish_act(group_norm(first_conv, gain_a, shift_a))
    onehot = (task_block[:, None] == jnp.arange(TASKS)[None, :]).astype(jnp.float32)
    cond_in = cond_block + jnp.dot(onehot, table, precision=lax.Precision.HIGHEST)
    embedded = low(mish_act(cond_in))
    film_out = low_back(jnp.dot(embedded, low(film_w), precision=lax.Precision.HIGHEST)) + film_b
    lifted = low(film_out[:, None, :CHANNELS] * mixed_a + film_out[:, None, CHANNELS:])
    second_conv = low_back(conv_apply(lifted, low(conv_b)))
    mixed_b = mish_act(group_norm(second_conv, gain_b, shift_b))
    return (inputs + mixed_b).reshape(samples * HORIZON, CHANNELS)

def reference(features, condition, task_ids, conv_first, conv_second, film_weight, norm_gain_first, norm_shift_first, norm_gain_second, norm_shift_second, film_bias, task_table, out_grad, grad_mask):
    per_block = min(SAMPLES, 256)
    block_count = SAMPLES // per_block
    reshaped = features.astype(jnp.float32).reshape(block_count, per_block * HORIZON, CHANNELS)
    cond_blocks = condition.astype(jnp.float32).reshape(block_count, per_block, CONDITION)
    task_blocks = task_ids.reshape(block_count, per_block)
    weights_f32 = tuple((member.astype(jnp.float32) for member in (conv_first, conv_second, film_weight, norm_gain_first, norm_shift_first, norm_gain_second, norm_shift_second, film_bias, task_table)))

    def forward_all(feat_all, weight_all):

        def per_piece(pieces):
            return block_forward(weight_all, pieces[0], pieces[1], pieces[2])
        return lax.map(jax.checkpoint(per_piece), (feat_all, cond_blocks, task_blocks))
    output, pullback = jax.vjp(forward_all, reshaped, weights_f32)
    upstream = out_grad.astype(jnp.float32) * grad_mask.astype(jnp.float32)[:, None]
    grad_feat, grad_weights = pullback(upstream.reshape(block_count, per_block * HORIZON, CHANNELS))
    return (output.reshape(FRAMES, CHANNELS).astype(jnp.bfloat16), grad_feat.reshape(FRAMES, CHANNELS).astype(jnp.bfloat16), grad_weights[0], grad_weights[1], grad_weights[2], grad_weights[3], grad_weights[4], grad_weights[5], grad_weights[6], grad_weights[7], grad_weights[8])
```

```python
import functools

import jax
import jax.numpy as jnp
from jax import lax
from jax.experimental import pallas as pl
from jax.experimental.pallas import tpu as pltpu
from jax.sharding import PartitionSpec as P

KERNEL = 5
HALF = KERNEL // 2
HORIZON = 16
GROUP = 128
EPSILON = 1e-05
BLOCK = 16
VMEM_LIMIT = 48 * 1024 * 1024
f32 = jnp.float32
bf16 = jnp.bfloat16


def mish_parts(v):
    w = jnp.exp(jnp.minimum(v, 20.0))
    n = w * (w + 2.0)
    r = 1.0 / (n + 2.0)
    return w, r, n * r


def mish_act(v):
    return v * mish_parts(v)[2]


def mish_slope(v):
    w, r, t = mish_parts(v)
    return t + v * (4.0 * w * (1.0 + w)) * (r * r)


def digits(count):
    bits = count.bit_length() - 1
    small = bits // 3
    return (1 << (bits - 2 * small), 1 << small, 1 << small)


def coordinates(index, sizes):
    _, ny, nx = sizes
    return (index // (ny * nx), (index // nx) % ny, index % nx)


def flat(position, sizes):
    _, ny, nx = sizes
    return (position[0] * ny + position[1]) * nx + position[2]


def move(value, sizes, axis, by):
    count = sizes[0] * sizes[1] * sizes[2]
    pairs = []
    for source in range(count):
        position = list(coordinates(source, sizes))
        position[axis] = (position[axis] + by) % sizes[axis]
        pairs.append((source, flat(position, sizes)))
    return lax.ppermute(value, "dp", pairs)


def swap(value, by):
    count = lax.axis_size("shard")
    return lax.ppermute(value, "shard", [(i, (i + by) % count) for i in range(count)])


def around(value):
    return [value] + [swap(value, r) for r in range(1, lax.axis_size("shard"))]


def gather_pieces(own, cut, sizes):
    nz, ny, nx = sizes
    lines = [own] + [move(own, sizes, 0, r) for r in range(1, nz)]
    first = jnp.stack([line[:cut] for line in lines])
    second = jnp.stack([line[cut:] for line in lines])
    first_x = [first] + [move(first, sizes, 2, r) for r in range(1, nx)]
    second_y = [second] + [move(second, sizes, 1, r) for r in range(1, ny)]
    first_all = [[part] + [move(part, sizes, 1, r) for r in range(1, ny)] for part in first_x]
    by_y = [[part] + [move(part, sizes, 2, r) for r in range(1, nx)] for part in second_y]
    second_all = [[by_y[dy][dx] for dy in range(ny)] for dx in range(nx)]
    return first_all, second_all


def scatter_first(keep, sends, sizes):
    got = [move(part, sizes, 1, dy + 1) for dy, part in enumerate(sends)]
    sums = [keep[dx] + sum(part[dx].astype(f32) for part in got) for dx in range(sizes[2])]
    return sums[0] + sum(
        move(sums[dx].astype(bf16), sizes, 2, dx).astype(f32) for dx in range(1, sizes[2])
    )


def scatter_second(keep, sends, sizes):
    got = [move(part, sizes, 2, dx + 1) for dx, part in enumerate(sends)]
    sums = [keep[dy] + sum(part[dy].astype(f32) for part in got) for dy in range(sizes[1])]
    return sums[0] + sum(
        move(sums[dy].astype(bf16), sizes, 1, dy).astype(f32) for dy in range(1, sizes[1])
    )


def scatter_lines(first, second, sizes):
    def whole(r):
        return jnp.concatenate([first[r], second[r]], axis=0)

    total = whole(0)
    for r in range(1, sizes[0]):
        total = total + move(whole(r).astype(bf16), sizes, 0, r).astype(f32)
    return total


def cost(flops, bytes_accessed, transcendentals=0):
    return pl.CostEstimate(
        flops=int(flops), bytes_accessed=int(bytes_accessed), transcendentals=int(transcendentals)
    )


def params(dims):
    return pltpu.CompilerParams(
        dimension_semantics=("arbitrary",) * dims, vmem_limit_bytes=VMEM_LIMIT
    )


def regroup_matrix(masked=None):
    side = BLOCK * HORIZON
    row = lax.broadcasted_iota(jnp.int32, (side, side), 0)
    column = lax.broadcasted_iota(jnp.int32, (side, side), 1)
    picked = column == (row % BLOCK) * HORIZON + row // BLOCK
    value = picked.astype(f32)
    if masked is not None:
        value = value * masked
    return value.astype(bf16)


def to_time_body(features_ref, grads_ref, mask_ref, features_out, grads_out):
    channels = features_ref.shape[1]
    moved = jnp.dot(regroup_matrix(), features_ref[...], preferred_element_type=f32)
    features_out[...] = moved.astype(bf16).reshape(HORIZON, BLOCK, channels)
    moved = jnp.dot(
        regroup_matrix(mask_ref[0].astype(f32)), grads_ref[...], preferred_element_type=f32
    )
    grads_out[...] = moved.astype(bf16).reshape(HORIZON, BLOCK, channels)


def to_time(features, grads, mask):
    frames, channels = features.shape
    samples = frames // HORIZON
    steps = samples // BLOCK
    side = BLOCK * HORIZON
    rows = pl.BlockSpec((side, channels), lambda b: (b, 0))
    out = pl.BlockSpec((HORIZON, BLOCK, channels), lambda b: (0, b, 0))
    shape = jax.ShapeDtypeStruct((HORIZON, samples, channels), bf16)
    return pl.pallas_call(
        to_time_body,
        grid=(steps,),
        in_specs=[rows, rows, pl.BlockSpec((1, 1, side), lambda b: (b, 0, 0))],
        out_specs=[out, out],
        out_shape=[shape, shape],
        compiler_params=params(1),
        cost_estimate=cost(4 * frames * side * channels, 8 * frames * channels),
        name="to_time",
    )(features, grads, mask.reshape(steps, 1, side))


def from_time_body(place_ref, *refs):
    pieces, out = refs[:-1], refs[-1]
    count, width = len(pieces), pieces[0].shape[2]
    for r, piece in enumerate(pieces):
        rows = piece[...].reshape(HORIZON * BLOCK, width)
        moved = jnp.dot(regroup_matrix(), rows, preferred_element_type=f32).astype(bf16)
        column = pl.multiple_of(((place_ref[3] + count - r) % count) * width, width)
        out[:, pl.ds(column, width)] = moved


def from_time(place, pieces):
    horizon, samples, width = pieces[0].shape
    channels = width * len(pieces)
    frames = horizon * samples
    return pl.pallas_call(
        from_time_body,
        grid_spec=pltpu.PrefetchScalarGridSpec(
            num_scalar_prefetch=1,
            grid=(samples // BLOCK,),
            in_specs=[pl.BlockSpec((HORIZON, BLOCK, width), lambda b, _: (0, b, 0))] * len(pieces),
            out_specs=pl.BlockSpec((HORIZON * BLOCK, channels), lambda b, _: (b, 0)),
        ),
        out_shape=jax.ShapeDtypeStruct((frames, channels), bf16),
        compiler_params=params(1),
        cost_estimate=cost(2 * frames * 256 * channels, 4 * frames * channels),
        name="from_time",
    )(place, *pieces)


def turn_body(sizes, rows, place_ref, *refs):
    pieces, out = refs[:-1], refs[-1]
    count, width = len(pieces), pieces[0].shape[2]
    nz, ny, nx = sizes
    for r, piece in enumerate(pieces):
        shard = (place_ref[3] + count - r) % count
        for tile in range(width // GROUP):
            block = piece[:, :, tile * GROUP : (tile + 1) * GROUP]
            turned = block.reshape(-1, GROUP).T
            for j in range(GROUP // rows):
                owner = shard * (width // rows) + tile * (GROUP // rows) + j
                oz, oy, ox = coordinates(owner, sizes)
                dz = (oz - place_ref[0] + nz) % nz
                dy = (oy - place_ref[1] + ny) % ny
                dx = (ox - place_ref[2] + nx) % nx
                out[pl.ds((dx * ny + dy) * nz + dz, 1)] = turned[j * rows : (j + 1) * rows][None]


def turn(place, pieces, sizes):
    horizon, samples, width = pieces[0].shape
    count = sizes[0] * sizes[1] * sizes[2]
    channels = width * len(pieces)
    rows = channels // count
    frames = horizon * samples
    return pl.pallas_call(
        functools.partial(turn_body, sizes, rows),
        in_specs=[pl.BlockSpec(memory_space=pltpu.SMEM)]
        + [pl.BlockSpec(memory_space=pltpu.VMEM)] * len(pieces),
        out_specs=pl.BlockSpec(memory_space=pltpu.VMEM),
        out_shape=jax.ShapeDtypeStruct((count, rows, frames), bf16),
        compiler_params=pltpu.CompilerParams(vmem_limit_bytes=VMEM_LIMIT),
        cost_estimate=cost(0, 4 * frames * channels),
        name="turn",
    )(place, *pieces)


def zero_ends(padded):
    rows, channels = padded.shape
    edge = rows * HALF // (HORIZON + 2 * HALF)
    zeros = jnp.zeros((edge, channels), padded.dtype)
    padded[:edge] = zeros
    padded[rows - edge :] = zeros


def weight_copies(sizes, cut, place_ref, firsts, seconds, weight, sems):
    nz, ny, nx = sizes
    rows = firsts[0].shape[2]
    copies = []
    for start, taps, pieces in ((0, cut, firsts), (cut, KERNEL - cut, seconds)):
        for dx in range(nx):
            for dy in range(ny):
                for r in range(nz):
                    owner = flat(
                        (
                            (place_ref[0] - r + nz) % nz,
                            (place_ref[1] - dy + ny) % ny,
                            (place_ref[2] - dx + nx) % nx,
                        ),
                        sizes,
                    )
                    at = pl.ds(pl.multiple_of(owner * rows, rows), rows)
                    copies.append(
                        pltpu.make_async_copy(
                            pieces[dx * ny + dy].at[r],
                            weight.at[pl.ds(start, taps), at, :],
                            sems.at[len(copies)],
                        )
                    )
    return copies


def column_copies(place_ref, pieces, target, sems, first_sem):
    count, width = len(pieces), pieces[0].shape[-1]
    copies = []
    for r, piece in enumerate(pieces):
        column = pl.multiple_of(((place_ref[3] + count - r) % count) * width, width)
        copies.append(
            pltpu.make_async_copy(
                piece, target.at[..., pl.ds(column, width)], sems.at[first_sem + r]
            )
        )
    return copies


def blocks_of(samples, body):
    def step(b, carry):
        body(pl.ds(pl.multiple_of(b * BLOCK, BLOCK), BLOCK))
        return carry

    lax.fori_loop(0, samples // BLOCK, step, 0)


def group_mean(value):
    return jnp.sum(jnp.sum(value, axis=0), axis=1, keepdims=True)[None] / (HORIZON * GROUP)


def norm_of(a):
    centre = a - group_mean(a)
    spread = lax.rsqrt(group_mean(centre * centre) + EPSILON)
    return centre * spread, spread


def norm_back(h, unit, spread):
    return spread * (h - group_mean(h) - unit * group_mean(h * unit))


def conv_front(sizes, cut, place_ref, inputs, firsts, seconds, quarters, padded, weight, acc, sems):
    n, k = pl.program_id(0), pl.program_id(1)
    samples = acc.shape[1]
    tile = acc.shape[2]
    frames = HORIZON * samples
    height = weight.shape[1] // len(quarters)

    def out_copies():
        count = len(quarters)
        base = len(firsts) * sizes[0] * 2 + len(inputs)
        return [
            pltpu.make_async_copy(
                weight.at[:, pl.ds(pl.multiple_of(((place_ref[3] + r) % count) * height, height), height), :],
                quarter,
                sems.at[base + r],
            )
            for r, quarter in enumerate(quarters)
        ]

    @pl.when((n == 0) & (k == 0))
    def _():
        copies = weight_copies(sizes, cut, place_ref, firsts, seconds, weight, sems)
        copies += column_copies(
            place_ref, inputs, padded.at[pl.ds(HALF * samples, frames)], sems, len(copies)
        )
        for copy in copies:
            copy.start()
        zero_ends(padded)
        for copy in copies:
            copy.wait()
        for copy in out_copies():
            copy.start()

    rows = padded[pl.ds(pl.multiple_of(k * samples, BLOCK), frames), :]
    columns = weight[k, :, pl.ds(pl.multiple_of(n * tile, tile), tile)]
    part = jnp.dot(rows, columns, preferred_element_type=f32).reshape(acc.shape)

    @pl.when(k == 0)
    def _():
        acc[...] = part

    @pl.when(k > 0)
    def _():
        acc[...] += part

    @pl.when((n == pl.num_programs(0) - 1) & (k == KERNEL - 1))
    def _():
        for copy in out_copies():
            copy.wait()


def first_body(sizes, cut, shards, place_ref, *refs):
    count = sizes[1] * sizes[2]
    inputs, firsts, seconds = refs[:1], refs[1 : 1 + count], refs[1 + count : 1 + 2 * count]
    scale, shifting, gain, shift = refs[1 + 2 * count : 5 + 2 * count]
    unit_out, spread_out, lifted_out = refs[5 + 2 * count : 8 + 2 * count]
    quarters = refs[8 + 2 * count : 8 + 2 * count + shards]
    padded, weight, acc, sems = refs[8 + 2 * count + shards :]
    conv_front(sizes, cut, place_ref, inputs, firsts, seconds, quarters, padded, weight, acc, sems)

    @pl.when(pl.program_id(1) == KERNEL - 1)
    def _():
        for group in range(acc.shape[2] // GROUP):
            lanes = pl.ds(group * GROUP, GROUP)

            def body(at, group=group, lanes=lanes):
                unit, spread = norm_of(acc[:, at, lanes])
                unit_out[:, at, lanes] = unit
                spread_out[group, at, :] = jnp.broadcast_to(spread[0], (BLOCK, GROUP))
                mixed = mish_act(unit * gain[:, lanes][None] + shift[:, lanes][None])
                lifted = scale[at, lanes][None] * mixed + shifting[at, lanes][None]
                lifted_out[:, at, lanes] = lifted.astype(bf16)

            blocks_of(acc.shape[1], body)


def second_body(sizes, cut, shards, place_ref, *refs):
    count = sizes[1] * sizes[2]
    inputs, refs = refs[:shards], refs[shards:]
    firsts, seconds = refs[:count], refs[count : 2 * count]
    features, upstream, gain, shift = refs[2 * count : 4 + 2 * count]
    block_out, grad_out, sums_out = refs[4 + 2 * count : 7 + 2 * count]
    quarters = refs[7 + 2 * count : 7 + 2 * count + shards]
    padded, weight, acc, sems = refs[7 + 2 * count + shards :]
    conv_front(sizes, cut, place_ref, inputs, firsts, seconds, quarters, padded, weight, acc, sems)

    @pl.when(pl.program_id(1) == KERNEL - 1)
    def _():
        sums_out[...] = jnp.zeros_like(sums_out)
        for group in range(acc.shape[2] // GROUP):
            lanes = pl.ds(group * GROUP, GROUP)

            def body(at, lanes=lanes):
                unit, spread = norm_of(acc[:, at, lanes])
                gain_here = gain[:, lanes][None]
                normed = unit * gain_here + shift[:, lanes][None]
                w, r, t = mish_parts(normed)
                block = features[:, at, lanes].astype(f32) + normed * t
                block_out[:, at, lanes] = block.astype(bf16)
                slope = t + normed * (4.0 * w * (1.0 + w)) * (r * r)
                grad = upstream[:, at, lanes].astype(f32) * slope
                sums_out[0:1, lanes] += jnp.sum(jnp.sum(grad * unit, axis=0), axis=0, keepdims=True)
                sums_out[1:2, lanes] += jnp.sum(jnp.sum(grad, axis=0), axis=0, keepdims=True)
                grad_out[:, at, lanes] = norm_back(grad * gain_here, unit, spread).astype(bf16)

            blocks_of(acc.shape[1], body)


def conv_call(body, name, place, sizes, cut, inputs, pieces, extras, extra_specs, outs, out_specs):
    shards = lax.axis_size("shard")
    horizon, samples, _ = inputs[0].shape
    channels = inputs[0].shape[2] * len(inputs)
    frames = horizon * samples
    firsts = [part for row in pieces[0] for part in row]
    seconds = [part for row in pieces[1] for part in row]
    width = firsts[0].shape[3]
    tile = min(256, width)
    inputs = [part.reshape(frames, part.shape[2]) for part in inputs]
    quarter = jax.ShapeDtypeStruct((KERNEL, width, width), bf16)
    anywhere = pl.BlockSpec(memory_space=pl.ANY)
    copies = 2 * len(firsts) * sizes[0] + len(inputs) + shards
    return pl.pallas_call(
        functools.partial(body, sizes, cut, shards),
        grid_spec=pltpu.PrefetchScalarGridSpec(
            num_scalar_prefetch=1,
            grid=(width // tile, KERNEL),
            in_specs=[anywhere] * (len(inputs) + 2 * len(firsts)) + extra_specs,
            out_specs=out_specs + [anywhere] * shards,
            scratch_shapes=[
                pltpu.VMEM(((HORIZON + 2 * HALF) * samples, channels), bf16),
                pltpu.VMEM((KERNEL, channels, width), bf16),
                pltpu.VMEM((HORIZON, samples, tile), f32),
                pltpu.SemaphoreType.DMA((copies,)),
            ],
        ),
        out_shape=outs + [quarter] * shards,
        compiler_params=params(2),
        cost_estimate=cost(
            2 * KERNEL * frames * channels * width, 24 * frames * width + 10 * channels * width
        ),
        name=name,
    )(place, *inputs, *firsts, *seconds, *extras)


def back_front(place_ref, grads, quarters, padded, weight, acc, sems):
    n, k = pl.program_id(0), pl.program_id(1)
    samples = acc.shape[1]
    tile = acc.shape[2]
    frames = HORIZON * samples

    @pl.when((n == 0) & (k == 0))
    def _():
        copies = column_copies(
            place_ref, grads, padded.at[pl.ds(HALF * samples, frames)], sems, 0
        )
        copies += column_copies(place_ref, quarters, weight, sems, len(copies))
        for copy in copies:
            copy.start()
        zero_ends(padded)
        for copy in copies:
            copy.wait()

    rows = padded[pl.ds(pl.multiple_of((KERNEL - 1 - k) * samples, BLOCK), frames), :]
    own = weight[k, pl.ds(pl.multiple_of(n * tile, tile), tile), :]
    part = lax.dot_general(rows, own, (((1,), (1,)), ((), ())), preferred_element_type=f32)
    part = part.reshape(acc.shape)

    @pl.when(k == 0)
    def _():
        acc[...] = part

    @pl.when(k > 0)
    def _():
        acc[...] += part


def lifted_back_body(shards, place_ref, *refs):
    grads, quarters, refs = refs[:shards], refs[shards : 2 * shards], refs[2 * shards :]
    unit_in, spread_in, scale, gain, shift = refs[:5]
    grad_out, film_out, sums_out = refs[5:8]
    padded, weight, acc, sems = refs[8:]
    back_front(place_ref, grads, quarters, padded, weight, acc, sems)

    @pl.when(pl.program_id(1) == KERNEL - 1)
    def _():
        sums_out[...] = jnp.zeros_like(sums_out)
        for group in range(acc.shape[2] // GROUP):
            lanes = pl.ds(group * GROUP, GROUP)

            def body(at, group=group, lanes=lanes):
                grad_lifted = acc[:, at, lanes]
                unit = unit_in[:, at, lanes]
                spread = spread_in[group, at, :][None]
                gain_here = gain[:, lanes][None]
                normed = unit * gain_here + shift[:, lanes][None]
                w, r, t = mish_parts(normed)
                film_out[0, at, lanes] = jnp.sum(grad_lifted * (normed * t), axis=0)
                film_out[1, at, lanes] = jnp.sum(grad_lifted, axis=0)
                slope = t + normed * (4.0 * w * (1.0 + w)) * (r * r)
                grad = grad_lifted * scale[at, lanes][None] * slope
                sums_out[0:1, lanes] += jnp.sum(jnp.sum(grad * unit, axis=0), axis=0, keepdims=True)
                sums_out[1:2, lanes] += jnp.sum(jnp.sum(grad, axis=0), axis=0, keepdims=True)
                grad_out[:, at, lanes] = norm_back(grad * gain_here, unit, spread).astype(bf16)

            blocks_of(acc.shape[1], body)


def features_back_body(shards, place_ref, *refs):
    grads, quarters, refs = refs[:shards], refs[shards : 2 * shards], refs[2 * shards :]
    upstream, grad_out, padded, weight, acc, sems = refs
    back_front(place_ref, grads, quarters, padded, weight, acc, sems)

    @pl.when(pl.program_id(1) == KERNEL - 1)
    def _():
        grad_out[...] = (acc[...] + upstream[...].astype(f32)).astype(bf16)


def back_call(body, name, place, grads, quarters, extras, extra_specs, outs, out_specs):
    shards = len(grads)
    horizon, samples, width = grads[0].shape
    channels = width * shards
    frames = horizon * samples
    tile = min(256, width)
    grads = [part.reshape(frames, width) for part in grads]
    anywhere = pl.BlockSpec(memory_space=pl.ANY)
    return pl.pallas_call(
        functools.partial(body, shards),
        grid_spec=pltpu.PrefetchScalarGridSpec(
            num_scalar_prefetch=1,
            grid=(width // tile, KERNEL),
            in_specs=[anywhere] * (2 * shards) + extra_specs,
            out_specs=out_specs,
            scratch_shapes=[
                pltpu.VMEM(((HORIZON + 2 * HALF) * samples, channels), bf16),
                pltpu.VMEM((KERNEL, width, channels), bf16),
                pltpu.VMEM((HORIZON, samples, tile), f32),
                pltpu.SemaphoreType.DMA((2 * shards,)),
            ],
        ),
        out_shape=outs,
        compiler_params=params(2),
        cost_estimate=cost(
            2 * KERNEL * frames * channels * width, 24 * frames * width + 10 * channels * width
        ),
        name=name,
    )(place, *grads, *quarters, *extras)


def weight_grad_body(sizes, start, along_y, turned, grads, *refs):
    nz, ny, nx = sizes
    padded = refs[-1]
    keep, sends = refs[0], refs[1:-1]
    rows = turned.shape[1]
    frames = turned.shape[2]
    samples = frames // HORIZON
    k = pl.program_id(0)

    @pl.when(k == 0)
    def _():
        zero_ends(padded)
        padded[HALF * samples : HALF * samples + frames, :] = grads[...]

    at = pl.multiple_of((KERNEL - 1 - start - k) * samples, BLOCK)
    lifted = turned[...].reshape(-1, frames)
    part = jnp.dot(lifted, padded[pl.ds(at, frames), :], preferred_element_type=f32)
    part = part.reshape(nx, ny, nz, 1, rows, part.shape[1])
    if along_y:
        keep[...] = part[:, 0]
        for dy, send in enumerate(sends):
            send[...] = part[:, dy + 1].astype(bf16)
    else:
        keep[...] = part[0]
        for dx, send in enumerate(sends):
            send[...] = part[dx + 1].astype(bf16)


def weight_grad(turned, grads, sizes, start, stop, along_y):
    nz, ny, nx = sizes
    count, rows, frames = turned.shape
    horizon, samples, width = grads.shape
    kept, sent = (nx, ny) if along_y else (ny, nx)
    block = pl.BlockSpec((kept, nz, 1, rows, width), lambda k: (0, 0, k, 0, 0))
    shape = (kept, nz, stop - start, rows, width)
    whole = pl.BlockSpec(memory_space=pltpu.VMEM)
    result = pl.pallas_call(
        functools.partial(weight_grad_body, sizes, start, along_y),
        grid=(stop - start,),
        in_specs=[whole, whole],
        out_specs=[block] * sent,
        out_shape=[jax.ShapeDtypeStruct(shape, f32)]
        + [jax.ShapeDtypeStruct(shape, bf16)] * (sent - 1),
        scratch_shapes=[pltpu.VMEM(((HORIZON + 2 * HALF) * samples, width), bf16)],
        compiler_params=params(1),
        cost_estimate=cost(
            2 * (stop - start) * count * rows * frames * width,
            2 * count * rows * frames + 6 * (stop - start) * count * rows * width,
        ),
        name="weight_grad",
    )(turned, grads.reshape(frames, width))
    return result[0], list(result[1:])


def conv_weight_grad(turned, grads, sizes, cut):
    first = scatter_first(*weight_grad(turned, grads, sizes, 0, cut, True), sizes)
    second = scatter_second(*weight_grad(turned, grads, sizes, cut, KERNEL, False), sizes)
    return scatter_lines(first, second, sizes)


def local(
    features,
    condition,
    task_ids,
    conv_first,
    conv_second,
    film_weight,
    norm_gain_first,
    norm_shift_first,
    norm_gain_second,
    norm_shift_second,
    film_bias,
    task_table,
    out_grad,
    grad_mask,
):
    count, shards = lax.axis_size("dp"), lax.axis_size("shard")
    sizes = digits(count)
    nz, ny, nx = sizes
    me, own = lax.axis_index("dp"), lax.axis_index("shard")
    position = coordinates(me, sizes)
    place = jnp.stack([position[0], position[1], position[2], own]).astype(jnp.int32)
    samples = condition.shape[0]
    channels = features.shape[1]
    width = channels // shards
    tile = min(256, width)
    film_rows, film_width = film_weight.shape

    def own_columns(value, each):
        return lax.dynamic_slice_in_dim(value, own * each, each, value.ndim - 1)

    vectors = jnp.concatenate(
        [norm_gain_first, norm_shift_first, norm_gain_second, norm_shift_second, film_bias]
    )
    each = norm_gain_first.shape[0]
    block = jnp.pad(vectors, (0, 2048 - vectors.shape[0])).reshape(16, 128)
    everyone = lax.all_gather(block, ("dp", "shard"), axis=0, tiled=False).astype(f32)
    everyone = everyone.reshape(count * shards, 2048)
    gain_a, shift_a, gain_b, shift_b = [
        own_columns(everyone[:, i * each : (i + 1) * each].reshape(1, -1), width) for i in range(4)
    ]
    bias = everyone[:, 4 * each : 6 * each].reshape(1, -1)

    cond_in = condition.astype(f32)
    onehot = (task_ids[:, None] == jnp.arange(task_table.shape[0])[None, :]).astype(bf16)
    cond_in = cond_in + jnp.dot(onehot, task_table, preferred_element_type=f32)
    embedded = mish_act(cond_in).astype(bf16)

    offsets = [(dx, dy, r) for dx in range(nx) for dy in range(ny) for r in range(nz)]

    def around_me(sign):
        return jnp.stack(
            [
                flat(
                    (
                        (position[0] + sign * r) % nz,
                        (position[1] + sign * dy) % ny,
                        (position[2] + sign * dx) % nx,
                    ),
                    sizes,
                )
                for dx, dy, r in offsets
            ]
        )

    def ordered(value, order):
        return value.reshape(-1, count, film_rows)[:, order].reshape(-1, count * film_rows)

    behind, ahead = around_me(-1), around_me(1)
    film_cut = film_rows // 32 * 16 if film_rows >= 32 else film_rows // 2
    film_first, film_second = gather_pieces(film_weight, film_cut, sizes)
    film_all = jnp.concatenate(
        [
            jnp.concatenate([film_first[dx][dy], film_second[dx][dy]], axis=1)
            for dx in range(nx)
            for dy in range(ny)
        ]
    ).reshape(count * film_rows, film_width)
    film_own = jnp.dot(ordered(embedded, behind), film_all, preferred_element_type=f32)
    film_own = film_own + own_columns(bias, film_width)
    film_parts = around(film_own)
    order = (own - jnp.arange(shards)) % shards
    film_out = jnp.stack(film_parts)[order]
    film_out = jnp.moveaxis(film_out, 0, 1).reshape(samples, 2 * channels)
    scale = own_columns(film_out[:, :channels], width)
    shifting = own_columns(film_out[:, channels:], width)

    timed, upstream = to_time(features, out_grad, grad_mask)
    turned_a = turn(place, [timed], sizes)
    upstream = own_columns(upstream, width)
    residual = own_columns(timed, width)
    cut_a, cut_b = HALF + 1, HALF
    pieces_a = gather_pieces(conv_first, cut_a, sizes)
    pieces_b = gather_pieces(conv_second, cut_b, sizes)

    column = pl.BlockSpec((samples, tile), lambda n, k, *_: (0, n))
    vector = pl.BlockSpec((1, tile), lambda n, k, *_: (0, n))
    pair = pl.BlockSpec((2, tile), lambda n, k, *_: (0, n))
    field = pl.BlockSpec((HORIZON, samples, tile), lambda n, k, *_: (0, 0, n))
    spreads = pl.BlockSpec((tile // GROUP, samples, GROUP), lambda n, k, *_: (n, 0, 0))
    films = pl.BlockSpec((2, samples, tile), lambda n, k, *_: (0, 0, n))
    field_shape = (HORIZON, samples, width)
    pair_shape = jax.ShapeDtypeStruct((2, width), f32)
    spread_shape = jax.ShapeDtypeStruct((width // GROUP, samples, GROUP), f32)

    unit_a, spread_a, lifted, *quarters_a = conv_call(
        first_body,
        "conv_first",
        place,
        sizes,
        cut_a,
        [timed],
        pieces_a,
        [scale, shifting, gain_a, shift_a],
        [column, column, vector, vector],
        [jax.ShapeDtypeStruct(field_shape, f32), spread_shape, jax.ShapeDtypeStruct(field_shape, bf16)],
        [field, spreads, field],
    )
    lifted_all = around(lifted)
    turned_b = turn(place, lifted_all, sizes)
    block_own, grad_second, sums_b, *quarters_b = conv_call(
        second_body,
        "conv_second",
        place,
        sizes,
        cut_b,
        lifted_all,
        pieces_b,
        [residual, upstream, gain_b, shift_b],
        [field, field, vector, vector],
        [jax.ShapeDtypeStruct(field_shape, bf16), jax.ShapeDtypeStruct(field_shape, bf16), pair_shape],
        [field, field, pair],
    )
    quarters_a = [quarters_a[0]] + [swap(quarters_a[r], r) for r in range(1, shards)]
    quarters_b = [quarters_b[0]] + [swap(quarters_b[r], r) for r in range(1, shards)]
    block_out = from_time(place, around(block_own))

    grad_conv_second = conv_weight_grad(turned_b, grad_second, sizes, cut_b)
    grad_first, grad_film, sums_a = back_call(
        lifted_back_body,
        "lifted_back",
        place,
        around(grad_second),
        quarters_b,
        [unit_a, spread_a, scale, gain_a, shift_a],
        [field, spreads, column, vector, vector],
        [
            jax.ShapeDtypeStruct(field_shape, bf16),
            jax.ShapeDtypeStruct((2, samples, width), f32),
            pair_shape,
        ],
        [field, films, pair],
    )
    grad_conv_first = conv_weight_grad(turned_a, grad_first, sizes, cut_a)
    grad_features_own = back_call(
        features_back_body,
        "features_back",
        place,
        around(grad_first),
        quarters_a,
        [upstream],
        [field],
        jax.ShapeDtypeStruct(field_shape, bf16),
        field,
    )
    grad_features = from_time(place, around(grad_features_own))

    low_parts = jnp.stack(around(grad_film.astype(bf16)))[order]
    low = jnp.moveaxis(low_parts, 0, 2).reshape(2, samples, channels)
    low = jnp.moveaxis(low, 0, 1).reshape(samples, 2 * channels)
    low_own = own_columns(low, film_width)
    film_grad = lax.dot_general(
        ordered(embedded, ahead), low_own, (((0,), (0,)), ((), ())), preferred_element_type=f32
    ).reshape(nx, ny, nz, film_rows, film_width)
    part = film_grad[:, :, :, :film_cut]
    first = scatter_first(
        part[:, 0], [part[:, dy].astype(bf16) for dy in range(1, ny)], sizes
    )
    part = film_grad[:, :, :, film_cut:]
    second = scatter_second(part[0], [part[dx].astype(bf16) for dx in range(1, nx)], sizes)
    grad_film_weight = scatter_lines(first, second, sizes)

    grad_embedded = lax.dot_general(
        low_own, film_all, (((1,), (1,)), ((), ())), preferred_element_type=f32
    )
    grad_cond = grad_embedded * mish_slope(ordered(cond_in, behind))
    grad_table = lax.dot_general(
        onehot.astype(f32), grad_cond, (((0,), (0,)), ((), ())), precision=lax.Precision.HIGHEST
    )
    inverse = jnp.zeros((count,), behind.dtype).at[behind].set(jnp.arange(count))
    grad_table = ordered(grad_table, inverse)

    sums = jnp.concatenate([sums_a, sums_b, jnp.sum(grad_film, axis=1)])
    sums = lax.dynamic_update_slice(jnp.zeros((6, channels), f32), sums, (0, own * width)).reshape(-1)
    condition_width = grad_table.shape[1]
    sum_rows = -(-sums.shape[0] // condition_width)
    sums = jnp.pad(sums, (0, sum_rows * condition_width - sums.shape[0]))
    total = jnp.concatenate([grad_table, sums.reshape(sum_rows, condition_width)])
    total = lax.psum(total, ("dp", "shard"))
    task_count = grad_table.shape[0]
    grad_table = total[:task_count]
    sums = total[task_count:].reshape(-1)[: 6 * channels].reshape(6, channels)
    index = me * shards + own
    small = [lax.dynamic_slice(sums[i], (index * each,), (each,)) for i in range(4)]
    grad_film_bias = lax.dynamic_slice(sums[4:].reshape(-1), (index * 2 * each,), (2 * each,))
    return (
        block_out,
        grad_features,
        grad_conv_first,
        grad_conv_second,
        grad_film_weight,
        small[0],
        small[1],
        small[2],
        small[3],
        grad_film_bias,
        grad_table,
    )


def solution(mesh):
    return jax.shard_map(
        local,
        mesh=mesh,
        in_specs=(
            P("dp", None),
            P("dp", None),
            P("dp"),
            P(None, "dp", "shard"),
            P(None, "dp", "shard"),
            P("dp", "shard"),
            P(("dp", "shard")),
            P(("dp", "shard")),
            P(("dp", "shard")),
            P(("dp", "shard")),
            P(("dp", "shard")),
            P(),
            P("dp", None),
            P("dp"),
        ),
        out_specs=(
            P("dp", None),
            P("dp", None),
            P(None, "dp", "shard"),
            P(None, "dp", "shard"),
            P("dp", "shard"),
            P(("dp", "shard")),
            P(("dp", "shard")),
            P(("dp", "shard")),
            P(("dp", "shard")),
            P(("dp", "shard")),
            P(),
        ),
        check_vma=False,
    )
```

```python
import functools

import jax
import jax.numpy as jnp
from jax import lax
from jax.experimental import pallas as pl
from jax.experimental.pallas import tpu as pltpu
from jax.sharding import PartitionSpec as P

KERNEL = 5
HALF = KERNEL // 2
HORIZON = 16
GROUP = 128
EPSILON = 1e-05
BLOCK = 16
VMEM_LIMIT = 48 * 1024 * 1024
f32 = jnp.float32
bf16 = jnp.bfloat16


def mish_parts(v):
    w = jnp.exp(jnp.minimum(v, 20.0))
    n = w * (w + 2.0)
    r = 1.0 / (n + 2.0)
    return w, r, n * r


def mish_act(v):
    return v * mish_parts(v)[2]


def mish_slope(v):
    w, r, t = mish_parts(v)
    return t + v * (4.0 * w * (1.0 + w)) * (r * r)


def digits(count):
    bits = count.bit_length() - 1
    small = bits // 3
    return (1 << (bits - 2 * small), 1 << small, 1 << small)


def coordinates(index, sizes):
    _, ny, nx = sizes
    return (index // (ny * nx), (index // nx) % ny, index % nx)


def flat(position, sizes):
    _, ny, nx = sizes
    return (position[0] * ny + position[1]) * nx + position[2]


def move(value, sizes, axis, by):
    count = sizes[0] * sizes[1] * sizes[2]
    pairs = []
    for source in range(count):
        position = list(coordinates(source, sizes))
        position[axis] = (position[axis] + by) % sizes[axis]
        pairs.append((source, flat(position, sizes)))
    return lax.ppermute(value, "dp", pairs)


def swap(value, by):
    count = lax.axis_size("shard")
    return lax.ppermute(value, "shard", [(i, (i + by) % count) for i in range(count)])


def around(value):
    return [value] + [swap(value, r) for r in range(1, lax.axis_size("shard"))]


def trade(value, sizes, axis, mask):
    count = sizes[0] * sizes[1] * sizes[2]
    pairs = []
    for source in range(count):
        position = list(coordinates(source, sizes))
        position[axis] ^= mask
        pairs.append((source, flat(position, sizes)))
    return lax.ppermute(value, "dp", pairs)


def line_groups(sizes):
    nz, ny, nx = sizes
    return [[flat((z, y, x), sizes) for z in range(nz)] for y in range(ny) for x in range(nx)]


def gather_lines(own, cut, sizes):
    lines = lax.all_gather(own, "dp", axis=0, tiled=False, axis_index_groups=line_groups(sizes))
    return lines[:, :cut], lines[:, cut:]


def move_lines(own, cut, sizes):
    lines = [own] + [move(own, sizes, 0, r) for r in range(1, sizes[0])]
    return jnp.stack([line[:cut] for line in lines]), jnp.stack([line[cut:] for line in lines])


def gather_planes(first, second, sizes):
    _, ny, nx = sizes
    first_x = [first] + [move(first, sizes, 2, r) for r in range(1, nx)]
    second_y = [second] + [move(second, sizes, 1, r) for r in range(1, ny)]
    first_all = [[part] + [move(part, sizes, 1, r) for r in range(1, ny)] for part in first_x]
    by_y = [[part] + [move(part, sizes, 2, r) for r in range(1, nx)] for part in second_y]
    return (
        [first_all[dx][dy] for dx in range(nx) for dy in range(ny)],
        [by_y[dy][dx] for dx in range(nx) for dy in range(ny)],
    )


def scatter_planes(keep, sends, sizes, order):
    near, far = order
    got = [move(sends[r], sizes, near, r + 1).astype(f32) for r in range(sizes[near] - 1)]
    sums = [keep[r] + sum(part[r] for part in got) for r in range(sizes[far])]
    total = sums[0]
    for r in range(1, sizes[far]):
        total = total + move(sums[r].astype(bf16), sizes, far, r).astype(f32)
    return total


def scatter_lines(first, second, sizes):
    def whole(r):
        return jnp.concatenate([first[r], second[r]], axis=0)

    total = whole(0)
    for r in range(1, sizes[0]):
        total = total + move(whole(r).astype(bf16), sizes, 0, r).astype(f32)
    return total


def sum_everywhere(value, sizes):
    shards = lax.axis_size("shard")
    own = lax.axis_index("shard")
    rows = value.shape[0] // shards

    def part(r):
        return lax.dynamic_slice_in_dim(value, (own + r) % shards * rows, rows, 0)

    total = part(0)
    for r in range(1, shards):
        total = total + swap(part(r), r)
    for axis in (2, 1, 0):
        mask = 1
        while mask < sizes[axis]:
            total = total + trade(total, sizes, axis, mask)
            mask *= 2
    return in_order(around(total)).reshape(value.shape)


def in_order(parts):
    shards = len(parts)
    own = lax.axis_index("shard")
    if shards == 2:
        mine = own == 0
        return jnp.stack([jnp.where(mine, parts[0], parts[1]), jnp.where(mine, parts[1], parts[0])])
    return jnp.stack(parts)[(own - jnp.arange(shards)) % shards]


def cost(flops, bytes_accessed, transcendentals=0):
    return pl.CostEstimate(
        flops=int(flops), bytes_accessed=int(bytes_accessed), transcendentals=int(transcendentals)
    )


def params(dims):
    return pltpu.CompilerParams(
        dimension_semantics=("arbitrary",) * dims, vmem_limit_bytes=VMEM_LIMIT
    )


def regroup_matrix(masked=None):
    side = BLOCK * HORIZON
    row = lax.broadcasted_iota(jnp.int32, (side, side), 0)
    column = lax.broadcasted_iota(jnp.int32, (side, side), 1)
    picked = column == (row % BLOCK) * HORIZON + row // BLOCK
    value = picked.astype(f32)
    if masked is not None:
        value = value * masked
    return value.astype(bf16)


def to_time_body(features_ref, grads_ref, mask_ref, features_out, grads_out):
    channels = features_ref.shape[1]
    moved = jnp.dot(regroup_matrix(), features_ref[...], preferred_element_type=f32)
    features_out[...] = moved.astype(bf16).reshape(HORIZON, BLOCK, channels)
    moved = jnp.dot(
        regroup_matrix(mask_ref[0].astype(f32)), grads_ref[...], preferred_element_type=f32
    )
    grads_out[...] = moved.astype(bf16).reshape(HORIZON, BLOCK, channels)


def to_time(features, grads, mask):
    frames, channels = features.shape
    samples = frames // HORIZON
    steps = samples // BLOCK
    side = BLOCK * HORIZON
    rows = pl.BlockSpec((side, channels), lambda b: (b, 0))
    out = pl.BlockSpec((HORIZON, BLOCK, channels), lambda b: (0, b, 0))
    shape = jax.ShapeDtypeStruct((HORIZON, samples, channels), bf16)
    return pl.pallas_call(
        to_time_body,
        grid=(steps,),
        in_specs=[rows, rows, pl.BlockSpec((1, 1, side), lambda b: (b, 0, 0))],
        out_specs=[out, out],
        out_shape=[shape, shape],
        compiler_params=params(1),
        cost_estimate=cost(4 * frames * side * channels, 8 * frames * channels),
        name="to_time",
    )(features, grads, mask.reshape(steps, 1, side))


def from_time_body(place_ref, *refs):
    pieces, out = refs[:-1], refs[-1]
    count, width = len(pieces), pieces[0].shape[2]
    for r, piece in enumerate(pieces):
        rows = piece[...].reshape(HORIZON * BLOCK, width)
        moved = jnp.dot(regroup_matrix(), rows, preferred_element_type=f32).astype(bf16)
        column = pl.multiple_of(((place_ref[3] + count - r) % count) * width, width)
        out[:, pl.ds(column, width)] = moved


def from_time(place, pieces):
    horizon, samples, width = pieces[0].shape
    channels = width * len(pieces)
    frames = horizon * samples
    return pl.pallas_call(
        from_time_body,
        grid_spec=pltpu.PrefetchScalarGridSpec(
            num_scalar_prefetch=1,
            grid=(samples // BLOCK,),
            in_specs=[pl.BlockSpec((HORIZON, BLOCK, width), lambda b, _: (0, b, 0))] * len(pieces),
            out_specs=pl.BlockSpec((HORIZON * BLOCK, channels), lambda b, _: (b, 0)),
        ),
        out_shape=jax.ShapeDtypeStruct((frames, channels), bf16),
        compiler_params=params(1),
        cost_estimate=cost(2 * frames * 256 * channels, 4 * frames * channels),
        name="from_time",
    )(place, *pieces)


def turn_body(sizes, rows, place_ref, *refs):
    pieces, out = refs[:-1], refs[-1]
    count, width = len(pieces), pieces[0].shape[2]
    nz, ny, nx = sizes
    for r, piece in enumerate(pieces):
        shard = (place_ref[3] + count - r) % count
        for tile in range(width // GROUP):
            block = piece[:, :, tile * GROUP : (tile + 1) * GROUP]
            turned = block.reshape(-1, GROUP).T
            for j in range(GROUP // rows):
                owner = shard * (width // rows) + tile * (GROUP // rows) + j
                oz, oy, ox = coordinates(owner, sizes)
                dz = (oz - place_ref[0] + nz) % nz
                dy = (oy - place_ref[1] + ny) % ny
                dx = (ox - place_ref[2] + nx) % nx
                out[pl.ds((dx * ny + dy) * nz + dz, 1)] = turned[j * rows : (j + 1) * rows][None]


def turn(place, pieces, sizes):
    horizon, samples, width = pieces[0].shape
    count = sizes[0] * sizes[1] * sizes[2]
    channels = width * len(pieces)
    rows = channels // count
    frames = horizon * samples
    return pl.pallas_call(
        functools.partial(turn_body, sizes, rows),
        in_specs=[pl.BlockSpec(memory_space=pltpu.SMEM)]
        + [pl.BlockSpec(memory_space=pltpu.VMEM)] * len(pieces),
        out_specs=pl.BlockSpec(memory_space=pltpu.VMEM),
        out_shape=jax.ShapeDtypeStruct((count, rows, frames), bf16),
        compiler_params=pltpu.CompilerParams(vmem_limit_bytes=VMEM_LIMIT),
        cost_estimate=cost(0, 4 * frames * channels),
        name="turn",
    )(place, *pieces)


def zero_ends(padded):
    steps = padded.shape[0]
    zeros = jnp.zeros((HALF,) + padded.shape[1:], padded.dtype)
    padded[:HALF] = zeros
    padded[steps - HALF :] = zeros


def block_copies(sizes, ordered, place_ref, pieces, target, sems, base):
    nz, ny, nx = sizes
    rows = pieces[0].shape[-2]
    copies = []
    for dx in range(nx):
        for dy in range(ny):
            for r in range(nz):
                z = r if ordered else (place_ref[0] - r + nz) % nz
                owner = flat((z, (place_ref[1] - dy + ny) % ny, (place_ref[2] - dx + nx) % nx), sizes)
                at = pl.ds(pl.multiple_of(owner * target[1] + target[2], BLOCK), rows)
                copies.append(
                    pltpu.make_async_copy(
                        pieces[dx * ny + dy].at[r],
                        target[0].at[..., at, :],
                        sems.at[base + len(copies)],
                    )
                )
    return copies


def weight_copies(sizes, cut, place_ref, firsts, seconds, weight, sems):
    rows = firsts[0].shape[2]
    copies = block_copies(
        sizes, True, place_ref, firsts, (weight.at[pl.ds(0, cut)], rows, 0), sems, 0
    )
    return copies + block_copies(
        sizes,
        True,
        place_ref,
        seconds,
        (weight.at[pl.ds(cut, KERNEL - cut)], rows, 0),
        sems,
        len(copies),
    )


def column_copies(place_ref, pieces, target, sems, first_sem):
    count, width = len(pieces), pieces[0].shape[-1]
    copies = []
    for r, piece in enumerate(pieces):
        column = pl.multiple_of(((place_ref[3] + count - r) % count) * width, width)
        copies.append(
            pltpu.make_async_copy(
                piece, target.at[..., pl.ds(column, width)], sems.at[first_sem + r]
            )
        )
    return copies


def group_mean(value):
    return jnp.sum(jnp.sum(value, axis=0), axis=1, keepdims=True)[None] / (HORIZON * GROUP)


def norm_of(a):
    centre = a - group_mean(a)
    spread = lax.rsqrt(group_mean(centre * centre) + EPSILON)
    return centre * spread, spread


def norm_back(h, unit, spread):
    return spread * (h - group_mean(h) - unit * group_mean(h * unit))


def conv_blocks(padded, weight_of, order, body):
    samples, channels = padded.shape[1:]
    for b in range(samples // BLOCK):
        at = slice(b * BLOCK, (b + 1) * BLOCK)
        total = None
        for k in range(KERNEL):
            start = order(k)
            rows = padded[start : start + HORIZON, at, :].reshape(HORIZON * BLOCK, channels)
            part = weight_of(rows, k)
            total = part if total is None else total + part
        body(at, total.reshape(HORIZON, BLOCK, total.shape[1]))


def conv_front(sizes, cut, place_ref, inputs, firsts, seconds, quarters, padded, weight, sems):
    n = pl.program_id(0)
    count = len(quarters)
    height = weight.shape[2]
    base = len(firsts) * sizes[0] * 2 + len(inputs)

    def out_copies():
        return [
            pltpu.make_async_copy(
                weight.at[
                    :, pl.ds(pl.multiple_of(((place_ref[3] + r) % count) * height, height), height), :
                ],
                quarter,
                sems.at[base + r],
            )
            for r, quarter in enumerate(quarters)
        ]

    @pl.when(n == 0)
    def _():
        copies = weight_copies(sizes, cut, place_ref, firsts, seconds, weight, sems)
        copies += column_copies(
            place_ref, inputs, padded.at[pl.ds(HALF, HORIZON)], sems, len(copies)
        )
        for copy in copies:
            copy.start()
        zero_ends(padded)
        for copy in copies:
            copy.wait()
        for copy in out_copies():
            copy.start()

    def finish():
        @pl.when(n == pl.num_programs(0) - 1)
        def _():
            for copy in out_copies():
                copy.wait()

    return finish


def conv_weight(weight, tile):
    column = pl.ds(pl.multiple_of(pl.program_id(0) * tile, tile), tile)

    def apply(rows, k):
        return jnp.dot(rows, weight[k, :, column], preferred_element_type=f32)

    return apply


def groups_of(width):
    return [(g, slice(g * GROUP, (g + 1) * GROUP)) for g in range(width // GROUP)]


def first_body(sizes, cut, shards, place_ref, *refs):
    count = sizes[1] * sizes[2]
    inputs, firsts, seconds = refs[:1], refs[1 : 1 + count], refs[1 + count : 1 + 2 * count]
    scale, shifting, gain, shift = refs[1 + 2 * count : 5 + 2 * count]
    unit_out, spread_out, lifted_out = refs[5 + 2 * count : 8 + 2 * count]
    quarters = refs[8 + 2 * count : 8 + 2 * count + shards]
    padded, weight, sems = refs[8 + 2 * count + shards :]
    tile = unit_out.shape[2]
    finish = conv_front(
        sizes, cut, place_ref, inputs, firsts, seconds, quarters, padded, weight, sems
    )

    def body(at, a):
        for group, lanes in groups_of(tile):
            unit, spread = norm_of(a[:, :, lanes])
            unit_out[:, at, lanes] = unit
            spread_out[group, at, :] = jnp.broadcast_to(spread[0], (BLOCK, GROUP))
            mixed = mish_act(unit * gain[:, lanes][None] + shift[:, lanes][None])
            lifted = scale[at, lanes][None] * mixed + shifting[at, lanes][None]
            lifted_out[:, at, lanes] = lifted.astype(bf16)

    conv_blocks(padded, conv_weight(weight, tile), lambda k: k, body)
    finish()


def second_body(sizes, cut, shards, place_ref, *refs):
    count = sizes[1] * sizes[2]
    inputs, refs = refs[:shards], refs[shards:]
    firsts, seconds = refs[:count], refs[count : 2 * count]
    features, upstream, gain, shift = refs[2 * count : 4 + 2 * count]
    block_out, grad_out, sums_out = refs[4 + 2 * count : 7 + 2 * count]
    quarters = refs[7 + 2 * count : 7 + 2 * count + shards]
    padded, weight, sems = refs[7 + 2 * count + shards :]
    tile = block_out.shape[2]
    finish = conv_front(
        sizes, cut, place_ref, inputs, firsts, seconds, quarters, padded, weight, sems
    )
    sums_out[...] = jnp.zeros_like(sums_out)

    def body(at, a):
        for _, lanes in groups_of(tile):
            unit, spread = norm_of(a[:, :, lanes])
            gain_here = gain[:, lanes][None]
            normed = unit * gain_here + shift[:, lanes][None]
            w, r, t = mish_parts(normed)
            block = features[:, at, lanes].astype(f32) + normed * t
            block_out[:, at, lanes] = block.astype(bf16)
            slope = t + normed * (4.0 * w * (1.0 + w)) * (r * r)
            grad = upstream[:, at, lanes].astype(f32) * slope
            sums_out[0:1, lanes] += jnp.sum(jnp.sum(grad * unit, axis=0), axis=0, keepdims=True)
            sums_out[1:2, lanes] += jnp.sum(jnp.sum(grad, axis=0), axis=0, keepdims=True)
            grad_out[:, at, lanes] = norm_back(grad * gain_here, unit, spread).astype(bf16)

    conv_blocks(padded, conv_weight(weight, tile), lambda k: k, body)
    finish()


def conv_call(body, name, place, sizes, cut, inputs, pieces, extras, extra_specs, outs, out_specs):
    shards = lax.axis_size("shard")
    horizon, samples, _ = inputs[0].shape
    channels = inputs[0].shape[2] * len(inputs)
    frames = horizon * samples
    firsts, seconds = pieces
    width = firsts[0].shape[3]
    tile = min(256, width)
    quarter = jax.ShapeDtypeStruct((KERNEL, width, width), bf16)
    anywhere = pl.BlockSpec(memory_space=pl.ANY)
    copies = 2 * len(firsts) * sizes[0] + len(inputs) + shards
    return pl.pallas_call(
        functools.partial(body, sizes, cut, shards),
        grid_spec=pltpu.PrefetchScalarGridSpec(
            num_scalar_prefetch=1,
            grid=(width // tile,),
            in_specs=[anywhere] * (len(inputs) + 2 * len(firsts)) + extra_specs,
            out_specs=out_specs + [anywhere] * shards,
            scratch_shapes=[
                pltpu.VMEM((HORIZON + 2 * HALF, samples, channels), bf16),
                pltpu.VMEM((KERNEL, channels, width), bf16),
                pltpu.SemaphoreType.DMA((copies,)),
            ],
        ),
        out_shape=outs + [quarter] * shards,
        compiler_params=params(1),
        cost_estimate=cost(
            2 * KERNEL * frames * channels * width, 24 * frames * width + 10 * channels * width
        ),
        name=name,
    )(place, *inputs, *firsts, *seconds, *extras)


def back_front(place_ref, grads, quarters, padded, weight, sems):
    @pl.when(pl.program_id(0) == 0)
    def _():
        copies = column_copies(place_ref, grads, padded.at[pl.ds(HALF, HORIZON)], sems, 0)
        copies += column_copies(place_ref, quarters, weight, sems, len(copies))
        for copy in copies:
            copy.start()
        zero_ends(padded)
        for copy in copies:
            copy.wait()


def back_weight(weight, tile):
    at = pl.ds(pl.multiple_of(pl.program_id(0) * tile, tile), tile)

    def apply(rows, k):
        return lax.dot_general(
            rows, weight[k, at, :], (((1,), (1,)), ((), ())), preferred_element_type=f32
        )

    return apply


def lifted_back_body(shards, place_ref, *refs):
    grads, quarters, refs = refs[:shards], refs[shards : 2 * shards], refs[2 * shards :]
    unit_in, spread_in, scale, gain, shift = refs[:5]
    grad_out, film_out, sums_out = refs[5:8]
    padded, weight, sems = refs[8:]
    tile = grad_out.shape[2]
    back_front(place_ref, grads, quarters, padded, weight, sems)
    sums_out[...] = jnp.zeros_like(sums_out)

    def body(at, a):
        for group, lanes in groups_of(tile):
            grad_lifted = a[:, :, lanes]
            unit = unit_in[:, at, lanes]
            spread = spread_in[group, at, :][None]
            gain_here = gain[:, lanes][None]
            normed = unit * gain_here + shift[:, lanes][None]
            w, r, t = mish_parts(normed)
            film_out[0, at, lanes] = jnp.sum(grad_lifted * (normed * t), axis=0)
            film_out[1, at, lanes] = jnp.sum(grad_lifted, axis=0)
            slope = t + normed * (4.0 * w * (1.0 + w)) * (r * r)
            grad = grad_lifted * scale[at, lanes][None] * slope
            sums_out[0:1, lanes] += jnp.sum(jnp.sum(grad * unit, axis=0), axis=0, keepdims=True)
            sums_out[1:2, lanes] += jnp.sum(jnp.sum(grad, axis=0), axis=0, keepdims=True)
            grad_out[:, at, lanes] = norm_back(grad * gain_here, unit, spread).astype(bf16)

    conv_blocks(padded, back_weight(weight, tile), lambda k: KERNEL - 1 - k, body)


def features_back_body(shards, place_ref, *refs):
    grads, quarters, refs = refs[:shards], refs[shards : 2 * shards], refs[2 * shards :]
    upstream, grad_out, padded, weight, sems = refs
    tile = grad_out.shape[2]
    back_front(place_ref, grads, quarters, padded, weight, sems)

    def body(at, a):
        grad_out[:, at, :] = (a + upstream[:, at, :].astype(f32)).astype(bf16)

    conv_blocks(padded, back_weight(weight, tile), lambda k: KERNEL - 1 - k, body)


def back_call(body, name, place, grads, quarters, extras, extra_specs, outs, out_specs):
    shards = len(grads)
    horizon, samples, width = grads[0].shape
    channels = width * shards
    frames = horizon * samples
    tile = min(256, width)
    anywhere = pl.BlockSpec(memory_space=pl.ANY)
    return pl.pallas_call(
        functools.partial(body, shards),
        grid_spec=pltpu.PrefetchScalarGridSpec(
            num_scalar_prefetch=1,
            grid=(width // tile,),
            in_specs=[anywhere] * (2 * shards) + extra_specs,
            out_specs=out_specs,
            scratch_shapes=[
                pltpu.VMEM((HORIZON + 2 * HALF, samples, channels), bf16),
                pltpu.VMEM((KERNEL, width, channels), bf16),
                pltpu.SemaphoreType.DMA((2 * shards,)),
            ],
        ),
        out_shape=outs,
        compiler_params=params(1),
        cost_estimate=cost(
            2 * KERNEL * frames * channels * width, 24 * frames * width + 10 * channels * width
        ),
        name=name,
    )(place, *grads, *quarters, *extras)


def weight_grad_body(sizes, start, taps, order, half, place_ref, turned, grads, *refs):
    nz = sizes[0]
    near, far = order
    if half is None:
        keep, send, padded = refs
    else:
        embedded, low, keep, send, padded = refs
    rows, frames = turned.shape[2:]
    width = grads.shape[2]
    step = pl.program_id(0)
    away = step // sizes[far] + 1
    across = step % sizes[far]
    stays = away == sizes[near]

    @pl.when(step == 0)
    def _():
        zero_ends(padded)
        padded[HALF : HALF + HORIZON] = grads[...]

    lhs = turned[0].reshape(nz * rows, frames)
    parts = []
    for k in range(start, start + taps):
        at = KERNEL - 1 - k
        rhs = padded[at : at + HORIZON].reshape(frames, width)
        part = jnp.dot(lhs, rhs, preferred_element_type=f32)
        parts.append((k - start, part.reshape(nz, rows, width)))

    extra = []
    if half is not None:
        depth = embedded.shape[0] // (sizes[0] * sizes[1] * sizes[2])
        offset = [0, 0, 0]
        offset[near] = away % sizes[near]
        offset[far] = across
        for r in range(nz):
            there = [(place_ref[axis] + offset[axis]) % sizes[axis] for axis in range(3)]
            there[0] = (place_ref[0] + r) % nz
            at = pl.ds(pl.multiple_of(flat(there, sizes) * depth, BLOCK), depth)
            extra.append(jnp.dot(embedded[at, :], low[...], preferred_element_type=f32))

    def store(out, dtype):
        for k, part in parts:
            out[:, k * rows : (k + 1) * rows, :] = part.astype(dtype)
        for r, part in enumerate(extra):
            out[r, taps * rows :, :] = part.astype(dtype)

    @pl.when(stays)
    def _():
        store(keep.at[0], f32)

    @pl.when(jnp.logical_not(stays))
    def _():
        store(send.at[0, 0], bf16)


def weight_grad(place, turned, grads, sizes, start, taps, order, film=None):
    nz, ny, nx = sizes
    near, far = order
    _, rows, frames = turned.shape
    horizon, samples, width = grads.shape
    height = taps * rows
    turned = turned.reshape(nx * ny, nz, rows, frames)
    extras, specs, half = [], [], None
    if film is not None:
        embedded, low, half = film
        height += embedded.shape[0] // (nx * ny * nz)
        extras = [embedded, low]
        specs = [
            pl.BlockSpec(embedded.shape, lambda s, _: (0, 0)),
            pl.BlockSpec((samples, width), lambda s, _: (0, half)),
        ]

    def source(s, _):
        away, across = (s // sizes[far] + 1) % sizes[near], s % sizes[far]
        dx, dy = (across, away) if near == 1 else (away, across)
        return (dx * ny + dy, 0, 0, 0)

    leaving = (sizes[near] - 1) * sizes[far]

    def kept(s, _):
        return (jnp.maximum(s - leaving, 0), 0, 0, 0)

    def sent(s, _):
        last = jnp.minimum(s, leaving - 1)
        return (last // sizes[far], last % sizes[far], 0, 0, 0)

    return pl.pallas_call(
        functools.partial(weight_grad_body, sizes, start, taps, order, half),
        grid_spec=pltpu.PrefetchScalarGridSpec(
            num_scalar_prefetch=1,
            grid=(nx * ny,),
            in_specs=[
                pl.BlockSpec((1, nz, rows, frames), source),
                pl.BlockSpec(grads.shape, lambda s, _: (0, 0, 0)),
            ]
            + specs,
            out_specs=[
                pl.BlockSpec((1, nz, height, width), kept),
                pl.BlockSpec((1, 1, nz, height, width), sent),
            ],
            scratch_shapes=[pltpu.VMEM((HORIZON + 2 * HALF, samples, width), bf16)],
        ),
        out_shape=[
            jax.ShapeDtypeStruct((sizes[far], nz, height, width), f32),
            jax.ShapeDtypeStruct((sizes[near] - 1, sizes[far], nz, height, width), bf16),
        ],
        compiler_params=params(1),
        cost_estimate=cost(
            2 * taps * nx * ny * nz * rows * frames * width,
            2 * nx * ny * nz * rows * frames + 6 * taps * nx * ny * nz * rows * width,
        ),
        name="weight_grad",
    )(place, turned, grads, *extras)


def conv_weight_grad(place, turned, grads, sizes, cut, film=None):
    halves = (None, None) if film is None else (film + (0,), film + (1,))
    keep, send = weight_grad(place, turned, grads, sizes, 0, cut, (1, 2), halves[0])
    first = scatter_planes(keep, send, sizes, (1, 2))
    keep, send = weight_grad(place, turned, grads, sizes, cut, KERNEL - cut, (2, 1), halves[1])
    second = scatter_planes(keep, send, sizes, (2, 1))
    return scatter_lines(first, second, sizes)


def film_body(sizes, rows, place_ref, embedded, *refs):
    count = sizes[1] * sizes[2]
    firsts, seconds = refs[:count], refs[count : 2 * count]
    out, weight_out, weight, sems = refs[2 * count :]
    samples = embedded.shape[0]
    cut = firsts[0].shape[1]
    depth = cut + seconds[0].shape[1]
    copies = block_copies(sizes, False, place_ref, firsts, (weight, depth, 0), sems, 0)
    copies += block_copies(
        sizes, False, place_ref, seconds, (weight, depth, cut), sems, len(copies)
    )
    for copy in copies:
        copy.start()
    for copy in copies:
        copy.wait()
    back = pltpu.make_async_copy(weight, weight_out, sems.at[len(copies)])
    back.start()
    out[:samples, :] = jnp.dot(embedded[...], weight[...], preferred_element_type=f32)
    edge = rows // BLOCK * BLOCK
    for d in range(sizes[0] * count):
        block = weight[d * depth + edge : d * depth + edge + BLOCK, :].astype(f32)
        out[samples + d : samples + d + 1, :] = block[rows - edge : rows - edge + 1, :]
    back.wait()


def film_call(place, embedded, pieces, sizes, rows):
    firsts, seconds = pieces
    samples, deep = embedded.shape
    width = firsts[0].shape[2]
    count = sizes[0] * sizes[1] * sizes[2]
    anywhere = pl.BlockSpec(memory_space=pl.ANY)
    whole = pl.BlockSpec(memory_space=pltpu.VMEM)
    return pl.pallas_call(
        functools.partial(film_body, sizes, rows),
        in_specs=[pl.BlockSpec(memory_space=pltpu.SMEM), whole] + [anywhere] * (2 * len(firsts)),
        out_specs=[whole, anywhere],
        out_shape=[
            jax.ShapeDtypeStruct((samples + count, width), f32),
            jax.ShapeDtypeStruct((deep, width), bf16),
        ],
        scratch_shapes=[
            pltpu.VMEM((deep, width), bf16),
            pltpu.SemaphoreType.DMA((2 * count + 1,)),
        ],
        compiler_params=pltpu.CompilerParams(vmem_limit_bytes=VMEM_LIMIT),
        cost_estimate=cost(2 * samples * deep * width, 4 * deep * width),
        name="film",
    )(place, embedded, *firsts, *seconds)


def table_body(low, weight, cond_in, onehot, out):
    grad = lax.dot_general(
        low[...], weight[...], (((1,), (1,)), ((), ())), preferred_element_type=f32
    )
    rest = grad * mish_slope(cond_in[...])
    total = jnp.zeros(out.shape, f32)
    for _ in range(3):
        part = rest.astype(bf16)
        rest = rest - part.astype(f32)
        total = total + jnp.dot(onehot[...], part, preferred_element_type=f32)
    out[...] = total


def table_call(low, weight, cond_in, onehot):
    return pl.pallas_call(
        table_body,
        in_specs=[pl.BlockSpec(memory_space=pltpu.VMEM)] * 4,
        out_specs=pl.BlockSpec(memory_space=pltpu.VMEM),
        out_shape=jax.ShapeDtypeStruct((onehot.shape[0], weight.shape[0]), f32),
        compiler_params=pltpu.CompilerParams(vmem_limit_bytes=VMEM_LIMIT),
        cost_estimate=cost(2 * low.size * weight.shape[0], 2 * weight.size),
        name="table_grad",
    )(low, weight, cond_in, onehot)


def local(
    features,
    condition,
    task_ids,
    conv_first,
    conv_second,
    film_weight,
    norm_gain_first,
    norm_shift_first,
    norm_gain_second,
    norm_shift_second,
    film_bias,
    task_table,
    out_grad,
    grad_mask,
):
    count, shards = lax.axis_size("dp"), lax.axis_size("shard")
    sizes = digits(count)
    nz, ny, nx = sizes
    me, own = lax.axis_index("dp"), lax.axis_index("shard")
    position = coordinates(me, sizes)
    place = jnp.stack([position[0], position[1], position[2], own]).astype(jnp.int32)
    samples = condition.shape[0]
    channels = features.shape[1]
    width = channels // shards
    tile = min(256, width)
    film_rows, film_width = film_weight.shape

    def own_columns(value, each):
        return lax.dynamic_slice_in_dim(value, own * each, each, value.ndim - 1)

    each = norm_gain_first.shape[0]
    tasks = task_table.shape[0]
    depth = -(-(film_rows + 1) // BLOCK) * BLOCK
    film_cut = depth // (2 * BLOCK) * BLOCK

    def deep(value):
        blocks = value.reshape(-1, count, film_rows)
        return jnp.pad(blocks, ((0, 0), (0, 0), (0, depth - film_rows))).reshape(-1, count * depth)

    vectors = jnp.concatenate(
        [norm_gain_first, norm_shift_first, norm_gain_second, norm_shift_second, film_bias]
    )
    vectors = jnp.pad(vectors, (0, film_width - vectors.shape[0]))
    film_block = jnp.concatenate(
        [
            film_weight,
            vectors[None],
            jnp.zeros((depth - film_rows - 1, film_width), bf16),
        ]
    )
    film_pieces = gather_planes(*move_lines(film_block, film_cut, sizes), sizes)
    lines_a = gather_lines(conv_first, HALF + 1, sizes)
    lines_b = gather_lines(conv_second, HALF + 1, sizes)
    onehot = (task_ids[:, None] == jnp.arange(tasks)[None, :]).astype(bf16)
    cond_in = condition.astype(f32) + jnp.dot(onehot, task_table, preferred_element_type=f32)
    cond_in = deep(cond_in)
    embedded = mish_act(cond_in).astype(bf16)
    film_own, film_all = film_call(place, embedded, film_pieces, sizes, film_rows)
    film_out = in_order(around(film_own))
    small = film_out[:, samples:]
    small = jnp.moveaxis(small, 0, 1).reshape(count * shards, film_width)
    gain_a, shift_a, gain_b, shift_b = [
        own_columns(small[:, i * each : (i + 1) * each].reshape(1, -1), width) for i in range(4)
    ]
    bias = small[:, 4 * each : 6 * each].reshape(1, -1)
    film_out = jnp.moveaxis(film_out[:, :samples], 0, 1).reshape(samples, 2 * channels) + bias
    scale = own_columns(film_out[:, :channels], width)
    shifting = own_columns(film_out[:, channels:], width)

    timed, upstream = to_time(features, out_grad, grad_mask)
    turned_a = turn(place, [timed], sizes)
    upstream = own_columns(upstream, width)
    residual = own_columns(timed, width)
    cut_a = cut_b = HALF + 1
    pieces_a = gather_planes(*lines_a, sizes)
    pieces_b = gather_planes(*lines_b, sizes)

    column = pl.BlockSpec((samples, tile), lambda n, _: (0, n))
    vector = pl.BlockSpec((1, tile), lambda n, _: (0, n))
    pair = pl.BlockSpec((2, tile), lambda n, _: (0, n))
    field = pl.BlockSpec((HORIZON, samples, tile), lambda n, _: (0, 0, n))
    spreads = pl.BlockSpec((tile // GROUP, samples, GROUP), lambda n, _: (n, 0, 0))
    films = pl.BlockSpec((2, samples, tile), lambda n, _: (0, 0, n))
    field_shape = (HORIZON, samples, width)
    pair_shape = jax.ShapeDtypeStruct((2, width), f32)
    spread_shape = jax.ShapeDtypeStruct((width // GROUP, samples, GROUP), f32)

    unit_a, spread_a, lifted, *quarters_a = conv_call(
        first_body,
        "conv_first",
        place,
        sizes,
        cut_a,
        [timed],
        pieces_a,
        [scale, shifting, gain_a, shift_a],
        [column, column, vector, vector],
        [jax.ShapeDtypeStruct(field_shape, f32), spread_shape, jax.ShapeDtypeStruct(field_shape, bf16)],
        [field, spreads, field],
    )
    lifted_all = around(lifted)
    turned_b = turn(place, lifted_all, sizes)
    block_own, grad_second, sums_b, *quarters_b = conv_call(
        second_body,
        "conv_second",
        place,
        sizes,
        cut_b,
        lifted_all,
        pieces_b,
        [residual, upstream, gain_b, shift_b],
        [field, field, vector, vector],
        [jax.ShapeDtypeStruct(field_shape, bf16), jax.ShapeDtypeStruct(field_shape, bf16), pair_shape],
        [field, field, pair],
    )
    quarters_a = [quarters_a[0]] + [swap(quarters_a[r], r) for r in range(1, shards)]
    quarters_b = [quarters_b[0]] + [swap(quarters_b[r], r) for r in range(1, shards)]
    block_out = from_time(place, around(block_own))

    rows_b = conv_weight_grad(place, turned_b, grad_second, sizes, cut_b)
    grad_conv_second = rows_b.reshape(conv_second.shape)
    grad_first, grad_film, sums_a = back_call(
        lifted_back_body,
        "lifted_back",
        place,
        around(grad_second),
        quarters_b,
        [unit_a, spread_a, scale, gain_a, shift_a],
        [field, spreads, column, vector, vector],
        [
            jax.ShapeDtypeStruct(field_shape, bf16),
            jax.ShapeDtypeStruct((2, samples, width), f32),
            pair_shape,
        ],
        [field, films, pair],
    )
    low = in_order(around(grad_film.astype(bf16)))
    low = jnp.moveaxis(low, 0, 2).reshape(2, samples, channels)
    low_own = own_columns(jnp.moveaxis(low, 0, 1).reshape(samples, 2 * channels), film_width)
    rows_a = conv_weight_grad(
        place, turned_a, grad_first, sizes, cut_a, (embedded.T, low_own)
    )
    block_rows = conv_first.shape[1]
    ends = [cut_a * block_rows, cut_a * block_rows + depth, KERNEL * block_rows + depth]
    grad_conv_first = jnp.concatenate([rows_a[: ends[0]], rows_a[ends[1] : ends[2]]])
    grad_conv_first = grad_conv_first.reshape(conv_first.shape)
    grad_film_weight = jnp.concatenate(
        [rows_a[ends[0] : ends[0] + film_rows], rows_a[ends[2] : ends[2] + film_rows]], axis=1
    )
    grad_features_own = back_call(
        features_back_body,
        "features_back",
        place,
        around(grad_first),
        quarters_a,
        [upstream],
        [field],
        jax.ShapeDtypeStruct(field_shape, bf16),
        field,
    )
    grad_features = from_time(place, around(grad_features_own))

    task_rows = -(-tasks // BLOCK) * BLOCK
    onehot = jnp.pad(onehot.T, ((0, task_rows - tasks), (0, 0)))
    grad_table = table_call(low_own, film_all, cond_in, onehot)[:tasks]
    sums = jnp.concatenate([sums_a, sums_b, jnp.sum(grad_film, axis=1)])
    sums = lax.dynamic_update_slice(jnp.zeros((6, channels), f32), sums, (0, own * width)).reshape(-1)
    wide = grad_table.shape[1]
    rows = -(-(tasks + -(-sums.shape[0] // wide)) // 8) * 8
    sums = jnp.pad(sums, (0, (rows - tasks) * wide - sums.shape[0])).reshape(rows - tasks, wide)
    total = sum_everywhere(jnp.concatenate([grad_table, sums]), sizes)
    grad_table = total[:tasks].reshape(tasks, count, depth)[:, :, :film_rows].reshape(tasks, -1)
    sums = total[tasks:].reshape(-1)[: 6 * channels].reshape(6, channels)
    index = me * shards + own
    small = [lax.dynamic_slice(sums[i], (index * each,), (each,)) for i in range(4)]
    grad_film_bias = lax.dynamic_slice(sums[4:].reshape(-1), (index * 2 * each,), (2 * each,))
    return (
        block_out,
        grad_features,
        grad_conv_first,
        grad_conv_second,
        grad_film_weight,
        small[0],
        small[1],
        small[2],
        small[3],
        grad_film_bias,
        grad_table,
    )


def solution(mesh):
    return jax.shard_map(
        local,
        mesh=mesh,
        in_specs=(
            P("dp", None),
            P("dp", None),
            P("dp"),
            P(None, "dp", "shard"),
            P(None, "dp", "shard"),
            P("dp", "shard"),
            P(("dp", "shard")),
            P(("dp", "shard")),
            P(("dp", "shard")),
            P(("dp", "shard")),
            P(("dp", "shard")),
            P(),
            P("dp", None),
            P("dp"),
        ),
        out_specs=(
            P("dp", None),
            P("dp", None),
            P(None, "dp", "shard"),
            P(None, "dp", "shard"),
            P("dp", "shard"),
            P(("dp", "shard")),
            P(("dp", "shard")),
            P(("dp", "shard")),
            P(("dp", "shard")),
            P(("dp", "shard")),
            P(),
        ),
        check_vma=False,
    )
```

```python
import functools

import jax
import jax.numpy as jnp
from jax import lax
from jax.experimental import pallas as pl
from jax.experimental.pallas import tpu as pltpu
from jax.sharding import PartitionSpec as P

KERNEL = 5
HALF = KERNEL // 2
HORIZON = 16
GROUP = 128
EPSILON = 1e-05
BLOCK = 16
VMEM_LIMIT = 48 * 1024 * 1024
SHORT = pl.CostEstimate(flops=1, bytes_accessed=1, transcendentals=0)
f32 = jnp.float32
bf16 = jnp.bfloat16


def mish_parts(v):
    w = jnp.exp(jnp.minimum(v, 20.0))
    n = w * (w + 2.0)
    r = 1.0 / (n + 2.0)
    return w, r, n * r


def mish_act(v):
    return v * mish_parts(v)[2]


def mish_slope(v):
    w, r, t = mish_parts(v)
    return t + v * (4.0 * w * (1.0 + w)) * (r * r)


def digits(count):
    bits = count.bit_length() - 1
    small = bits // 3
    return (1 << (bits - 2 * small), 1 << small, 1 << small)


def coordinates(index, sizes):
    _, ny, nx = sizes
    return (index // (ny * nx), (index // nx) % ny, index % nx)


def flat(position, sizes):
    _, ny, nx = sizes
    return (position[0] * ny + position[1]) * nx + position[2]


def move(value, sizes, axis, by):
    count = sizes[0] * sizes[1] * sizes[2]
    pairs = []
    for source in range(count):
        position = list(coordinates(source, sizes))
        position[axis] = (position[axis] + by) % sizes[axis]
        pairs.append((source, flat(position, sizes)))
    return lax.ppermute(value, "dp", pairs)


def swap(value, by):
    count = lax.axis_size("shard")
    return lax.ppermute(value, "shard", [(i, (i + by) % count) for i in range(count)])


def around(value):
    return [value] + [swap(value, r) for r in range(1, lax.axis_size("shard"))]


def in_order(parts, own):
    count = len(parts)
    if count == 2:
        mine = own == 0
        return jnp.stack([jnp.where(mine, parts[0], parts[1]), jnp.where(mine, parts[1], parts[0])])
    return jnp.stack(parts)[(own - jnp.arange(count)) % count]


def trade(value, sizes, axis, mask):
    count = sizes[0] * sizes[1] * sizes[2]
    pairs = []
    for source in range(count):
        position = list(coordinates(source, sizes))
        position[axis] ^= mask
        pairs.append((source, flat(position, sizes)))
    return lax.ppermute(value, "dp", pairs)


def line_groups(sizes):
    nz, ny, nx = sizes
    return [[flat((z, y, x), sizes) for z in range(nz)] for y in range(ny) for x in range(nx)]


def move_lines(own, sizes):
    return jnp.stack([own] + [move(own, sizes, 0, r) for r in range(1, sizes[0])])


def line_masks(count):
    masks = [1 << bit for bit in reversed(range(count.bit_length() - 1))]
    order = [0]
    for mask in masks:
        order = order + [other ^ mask for other in order]
    return masks, order


def line_place(other, count):
    bits = count.bit_length() - 1
    return sum(((other >> bit) & 1) << (bits - 1 - bit) for bit in range(bits))


def double_lines(own, sizes):
    lines, steps = own[None], []
    for mask in line_masks(sizes[0])[0]:
        steps.append(trade(lines, sizes, 0, mask))
        lines = jnp.concatenate([lines, steps[-1]])
    return lines, steps


def halve_lines(parts, sizes):
    for mask in reversed(line_masks(sizes[0])[0]):
        half = parts.shape[0] // 2
        parts = parts[:half] + trade(parts[half:].astype(bf16), sizes, 0, mask).astype(f32)
    return parts[0]


def gather_sides(lines, sizes):
    return (
        [move(lines, sizes, 2, r) for r in range(1, sizes[2])],
        [move(lines, sizes, 1, r) for r in range(1, sizes[1])],
    )


def gather_corners(lines, sides, cut, sizes, *ready):
    by_x, by_y = sides
    rest = lines.shape[1] - cut
    pieces = [(lines, 0, 0, 0)]
    pieces += [(part, 0, dx + 1, 0) for dx, part in enumerate(by_x)]
    pieces += [(part, 0, 0, dy + 1) for dy, part in enumerate(by_y)]
    tops = [cut_rows(part, 0, cut, *ready) for part in by_x]
    ends = [cut_rows(part, cut, rest, *ready) for part in by_y]
    for dx in range(1, sizes[2]):
        for dy in range(1, sizes[1]):
            pieces.append((move(ends[dy - 1], sizes, 2, dx), cut, dx, dy))
            pieces.append((move(tops[dx - 1], sizes, 1, dy), 0, dx, dy))
    return pieces


def scatter_near(sends, sizes, order):
    return [move(sends[r], sizes, order[0], r + 1) for r in range(sizes[order[0]] - 1)]


def add_near(keep, got, *ready):
    got = [after(part, *ready).astype(f32) if ready else part.astype(f32) for part in got]
    return [keep[r] + sum(part[r] for part in got) for r in range(keep.shape[0])]


def scatter_far(own, leaving, sizes, order):
    total = own
    for r, part in enumerate(leaving):
        total = total + move(part, sizes, order[1], r + 1).astype(f32)
    return total


def sum_shards(value):
    shards = lax.axis_size("shard")
    own = lax.axis_index("shard")
    rows = value.shape[0] // shards

    def part(r):
        return lax.dynamic_slice_in_dim(value, (own + r) % shards * rows, rows, 0)

    total = part(0)
    for r in range(1, shards):
        total = total + swap(part(r), r)
    return total


def sum_along(total, sizes, axis):
    mask = 1
    while mask < sizes[axis]:
        total = total + trade(total, sizes, axis, mask)
        mask *= 2
    return total


def nothing(*_):
    pass


def after(value, *ready):
    anywhere = pl.BlockSpec(memory_space=pl.ANY)
    return pl.pallas_call(
        nothing,
        in_specs=[anywhere] * (1 + len(ready)),
        out_specs=anywhere,
        out_shape=jax.ShapeDtypeStruct(value.shape, value.dtype),
        input_output_aliases={0: 0},
        cost_estimate=SHORT,
        name="after",
    )(value, *ready)


def cut_rows(value, start, rows, *ready):
    return after(value[:, start : start + rows], *ready)


def params(dims):
    return pltpu.CompilerParams(
        dimension_semantics=("arbitrary",) * dims, vmem_limit_bytes=VMEM_LIMIT
    )


def regroup_matrix(masked=None):
    side = BLOCK * HORIZON
    row = lax.broadcasted_iota(jnp.int32, (side, side), 0)
    column = lax.broadcasted_iota(jnp.int32, (side, side), 1)
    picked = column == (row % BLOCK) * HORIZON + row // BLOCK
    value = picked.astype(f32)
    if masked is not None:
        value = value * masked
    return value.astype(bf16)


def to_time_body(features_ref, grads_ref, mask_ref, features_out, grads_out):
    channels = features_ref.shape[1]
    moved = jnp.dot(regroup_matrix(), features_ref[...], preferred_element_type=f32)
    features_out[...] = moved.astype(bf16).reshape(HORIZON, BLOCK, channels)
    moved = jnp.dot(
        regroup_matrix(mask_ref[0].astype(f32)), grads_ref[...], preferred_element_type=f32
    )
    grads_out[...] = moved.astype(bf16).reshape(HORIZON, BLOCK, channels)


def to_time(features, grads, mask):
    frames, channels = features.shape
    samples = frames // HORIZON
    steps = samples // BLOCK
    side = BLOCK * HORIZON
    rows = pl.BlockSpec((side, channels), lambda b: (b, 0))
    out = pl.BlockSpec((HORIZON, BLOCK, channels), lambda b: (0, b, 0))
    shape = jax.ShapeDtypeStruct((HORIZON, samples, channels), bf16)
    return pl.pallas_call(
        to_time_body,
        grid=(steps,),
        in_specs=[rows, rows, pl.BlockSpec((1, 1, side), lambda b: (b, 0, 0))],
        out_specs=[out, out],
        out_shape=[shape, shape],
        compiler_params=params(1),
        cost_estimate=SHORT,
        name="to_time",
    )(features, grads, mask.reshape(steps, 1, side))


def from_time_body(place_ref, *refs):
    pieces, out = refs[:-1], refs[-1]
    count, width = len(pieces), pieces[0].shape[2]
    for r, piece in enumerate(pieces):
        rows = piece[...].reshape(HORIZON * BLOCK, width)
        moved = jnp.dot(regroup_matrix(), rows, preferred_element_type=f32).astype(bf16)
        column = pl.multiple_of(((place_ref[3] + count - r) % count) * width, width)
        out[:, pl.ds(column, width)] = moved


def from_time(place, pieces):
    horizon, samples, width = pieces[0].shape
    channels = width * len(pieces)
    return pl.pallas_call(
        from_time_body,
        grid_spec=pltpu.PrefetchScalarGridSpec(
            num_scalar_prefetch=1,
            grid=(samples // BLOCK,),
            in_specs=[pl.BlockSpec((HORIZON, BLOCK, width), lambda b, _: (0, b, 0))] * len(pieces),
            out_specs=pl.BlockSpec((HORIZON * BLOCK, channels), lambda b, _: (b, 0)),
        ),
        out_shape=jax.ShapeDtypeStruct((horizon * samples, channels), bf16),
        compiler_params=params(1),
        cost_estimate=SHORT,
        name="from_time",
    )(place, *pieces)


def turn_body(sizes, rows, ordered, place_ref, *refs):
    pieces, out = refs[:-1], refs[-1]
    count, width = len(pieces), pieces[0].shape[2]
    nz, ny, nx = sizes
    for r, piece in enumerate(pieces):
        shard = (place_ref[3] + count - r) % count
        for tile in range(width // GROUP):
            block = piece[:, :, tile * GROUP : (tile + 1) * GROUP]
            turned = block.reshape(-1, GROUP).T
            for j in range(GROUP // rows):
                owner = shard * (width // rows) + tile * (GROUP // rows) + j
                oz, oy, ox = coordinates(owner, sizes)
                dz = oz if ordered else line_place(oz ^ place_ref[0], nz)
                dy = (oy - place_ref[1] + ny) % ny
                dx = (ox - place_ref[2] + nx) % nx
                out[pl.ds((dx * ny + dy) * nz + dz, 1)] = turned[j * rows : (j + 1) * rows][None]


def turn(place, pieces, sizes, ordered):
    horizon, samples, width = pieces[0].shape
    count = sizes[0] * sizes[1] * sizes[2]
    rows = len(pieces) * width // count
    return pl.pallas_call(
        functools.partial(turn_body, sizes, rows, ordered),
        in_specs=[pl.BlockSpec(memory_space=pltpu.SMEM)]
        + [pl.BlockSpec(memory_space=pltpu.VMEM)] * len(pieces),
        out_specs=pl.BlockSpec(memory_space=pltpu.VMEM),
        out_shape=jax.ShapeDtypeStruct((count, rows, horizon * samples), bf16),
        compiler_params=pltpu.CompilerParams(vmem_limit_bytes=VMEM_LIMIT),
        cost_estimate=SHORT,
        name="turn",
    )(place, *pieces)


def zero_ends(padded):
    steps = padded.shape[0]
    zeros = jnp.zeros((HALF,) + padded.shape[1:], padded.dtype)
    padded[:HALF] = zeros
    padded[steps - HALF :] = zeros


def block_copies(sizes, paired, place_ref, pieces, where, spot, sems):
    nz, ny, nx = sizes
    copies = []
    for piece, (start, dx, dy) in zip(pieces, where):
        for r in range(nz):
            z = place_ref[0] ^ line_masks(nz)[1][r] if paired else (place_ref[0] - r + nz) % nz
            owner = flat((z, (place_ref[1] - dy + ny) % ny, (place_ref[2] - dx + nx) % nx), sizes)
            copies.append(
                pltpu.make_async_copy(
                    piece.at[r], spot(owner, start, piece.shape[1]), sems.at[len(copies)]
                )
            )
    return copies


def weight_copies(sizes, paired, place_ref, pieces, where, weight, sems):
    rows = pieces[0].shape[2]

    def spot(owner, start, taps):
        at = pl.ds(pl.multiple_of(owner * rows, rows), rows)
        return weight.at[pl.ds(start, taps), at, :]

    return block_copies(sizes, paired, place_ref, pieces, where, spot, sems)


def column_copies(place_ref, pieces, target, sems, first_sem):
    count, width = len(pieces), pieces[0].shape[-1]
    copies = []
    for r, piece in enumerate(pieces):
        column = pl.multiple_of(((place_ref[3] + count - r) % count) * width, width)
        copies.append(
            pltpu.make_async_copy(
                piece, target.at[..., pl.ds(column, width)], sems.at[first_sem + r]
            )
        )
    return copies


def group_mean(value):
    return jnp.sum(jnp.sum(value, axis=0), axis=1, keepdims=True)[None] / (HORIZON * GROUP)


def norm_of(a):
    centre = a - group_mean(a)
    spread = lax.rsqrt(group_mean(centre * centre) + EPSILON)
    return centre * spread, spread


def norm_back(h, unit, spread):
    return spread * (h - group_mean(h) - unit * group_mean(h * unit))


def conv_blocks(padded, weight_of, order, body):
    samples, channels = padded.shape[1:]
    for b in range(samples // BLOCK):
        at = slice(b * BLOCK, (b + 1) * BLOCK)
        total = None
        for k in range(KERNEL):
            start = order(k)
            rows = padded[start : start + HORIZON, at, :].reshape(HORIZON * BLOCK, channels)
            part = weight_of(rows, k)
            total = part if total is None else total + part
        body(at, total.reshape(HORIZON, BLOCK, total.shape[1]))


def conv_front(sizes, paired, where, place_ref, inputs, pieces, quarters, padded, weight, sems):
    n = pl.program_id(0)
    count = len(quarters)
    height = weight.shape[2]
    base = len(pieces) * sizes[0] + len(inputs)

    def out_copies():
        return [
            pltpu.make_async_copy(
                weight.at[
                    :, pl.ds(pl.multiple_of(((place_ref[3] + r) % count) * height, height), height), :
                ],
                quarter,
                sems.at[base + r],
            )
            for r, quarter in enumerate(quarters)
        ]

    @pl.when(n == 0)
    def _():
        copies = weight_copies(sizes, paired, place_ref, pieces, where, weight, sems)
        copies += column_copies(
            place_ref, inputs, padded.at[pl.ds(HALF, HORIZON)], sems, len(copies)
        )
        for copy in copies:
            copy.start()
        zero_ends(padded)
        for copy in copies:
            copy.wait()
        for copy in out_copies():
            copy.start()

    def finish():
        @pl.when(n == pl.num_programs(0) - 1)
        def _():
            for copy in out_copies():
                copy.wait()

    return finish


def conv_weight(weight, tile):
    column = pl.ds(pl.multiple_of(pl.program_id(0) * tile, tile), tile)

    def apply(rows, k):
        return jnp.dot(rows, weight[k, :, column], preferred_element_type=f32)

    return apply


def groups_of(width):
    return [(g, slice(g * GROUP, (g + 1) * GROUP)) for g in range(width // GROUP)]


def first_body(sizes, paired, where, shards, waits, place_ref, *refs):
    inputs, refs = refs[:1], refs[1:]
    pieces, refs = refs[: len(where)], refs[len(where) :]
    scale, shifting, gain, shift = refs[:4]
    refs = refs[4 + waits :]
    unit_out, spread_out, lifted_out = refs[:3]
    quarters = refs[3 : 3 + shards]
    padded, weight, sems = refs[3 + shards :]
    tile = unit_out.shape[2]
    finish = conv_front(
        sizes, paired, where, place_ref, inputs, pieces, quarters, padded, weight, sems
    )

    def body(at, a):
        for group, lanes in groups_of(tile):
            unit, spread = norm_of(a[:, :, lanes])
            unit_out[:, at, lanes] = unit
            spread_out[group, at, :] = jnp.broadcast_to(spread[0], (BLOCK, GROUP))
            mixed = mish_act(unit * gain[:, lanes][None] + shift[:, lanes][None])
            lifted = scale[at, lanes][None] * mixed + shifting[at, lanes][None]
            lifted_out[:, at, lanes] = lifted.astype(bf16)

    conv_blocks(padded, conv_weight(weight, tile), lambda k: k, body)
    finish()


def second_body(sizes, paired, where, shards, waits, place_ref, *refs):
    inputs, refs = refs[:shards], refs[shards:]
    pieces, refs = refs[: len(where)], refs[len(where) :]
    features, upstream, gain, shift = refs[:4]
    refs = refs[4 + waits :]
    block_out, grad_out, sums_out = refs[:3]
    quarters = refs[3 : 3 + shards]
    padded, weight, sems = refs[3 + shards :]
    tile = block_out.shape[2]
    finish = conv_front(
        sizes, paired, where, place_ref, inputs, pieces, quarters, padded, weight, sems
    )
    sums_out[...] = jnp.zeros_like(sums_out)

    def body(at, a):
        for _, lanes in groups_of(tile):
            unit, spread = norm_of(a[:, :, lanes])
            gain_here = gain[:, lanes][None]
            normed = unit * gain_here + shift[:, lanes][None]
            w, r, t = mish_parts(normed)
            block = features[:, at, lanes].astype(f32) + normed * t
            block_out[:, at, lanes] = block.astype(bf16)
            slope = t + normed * (4.0 * w * (1.0 + w)) * (r * r)
            grad = upstream[:, at, lanes].astype(f32) * slope
            sums_out[0:1, lanes] += jnp.sum(jnp.sum(grad * unit, axis=0), axis=0, keepdims=True)
            sums_out[1:2, lanes] += jnp.sum(jnp.sum(grad, axis=0), axis=0, keepdims=True)
            grad_out[:, at, lanes] = norm_back(grad * gain_here, unit, spread).astype(bf16)

    conv_blocks(padded, conv_weight(weight, tile), lambda k: k, body)
    finish()


def conv_call(
    body, name, place, sizes, paired, inputs, pieces, extras, extra_specs, outs, out_specs, ready
):
    shards = lax.axis_size("shard")
    _, samples, depth = inputs[0].shape
    count = len(inputs)
    channels = count * depth
    arrays = [piece[0] for piece in pieces]
    where = tuple(piece[1:] for piece in pieces)
    width = arrays[0].shape[3]
    tile = min(256, width)
    quarter = jax.ShapeDtypeStruct((KERNEL, width, width), bf16)
    anywhere = pl.BlockSpec(memory_space=pl.ANY)
    return pl.pallas_call(
        functools.partial(body, sizes, paired, where, shards, len(ready)),
        grid_spec=pltpu.PrefetchScalarGridSpec(
            num_scalar_prefetch=1,
            grid=(width // tile,),
            in_specs=[anywhere] * (count + len(arrays)) + extra_specs + [anywhere] * len(ready),
            out_specs=out_specs + [anywhere] * shards,
            scratch_shapes=[
                pltpu.VMEM((HORIZON + 2 * HALF, samples, channels), bf16),
                pltpu.VMEM((KERNEL, channels, width), bf16),
                pltpu.SemaphoreType.DMA((len(arrays) * sizes[0] + count + shards,)),
            ],
        ),
        out_shape=outs + [quarter] * shards,
        compiler_params=params(1),
        cost_estimate=SHORT,
        name=name,
    )(place, *inputs, *arrays, *extras, *ready)


def back_front(place_ref, grads, quarters, padded, weight, sems):
    @pl.when(pl.program_id(0) == 0)
    def _():
        copies = column_copies(place_ref, grads, padded.at[pl.ds(HALF, HORIZON)], sems, 0)
        copies += column_copies(place_ref, quarters, weight, sems, len(copies))
        for copy in copies:
            copy.start()
        zero_ends(padded)
        for copy in copies:
            copy.wait()


def back_weight(weight, tile):
    at = pl.ds(pl.multiple_of(pl.program_id(0) * tile, tile), tile)

    def apply(rows, k):
        return lax.dot_general(
            rows, weight[k, at, :], (((1,), (1,)), ((), ())), preferred_element_type=f32
        )

    return apply


def lifted_back_body(shards, place_ref, *refs):
    grads, quarters, refs = refs[:shards], refs[shards : 2 * shards], refs[2 * shards :]
    unit_in, spread_in, scale, gain, shift = refs[:5]
    grad_out, film_out, sums_out, padded, weight, sems = refs[-6:]
    tile = unit_in.shape[2]
    back_front(place_ref, grads, quarters, padded, weight, sems)
    sums_out[...] = jnp.zeros_like(sums_out)

    def body(at, a):
        for group, lanes in groups_of(tile):
            grad_lifted = a[:, :, lanes]
            unit = unit_in[:, at, lanes]
            spread = spread_in[group, at, :][None]
            gain_here = gain[:, lanes][None]
            normed = unit * gain_here + shift[:, lanes][None]
            w, r, t = mish_parts(normed)
            for row, film in enumerate((grad_lifted * (normed * t), grad_lifted)):
                film = jnp.sum(film, axis=0)
                sums_out[2 + row : 3 + row, lanes] += jnp.sum(film, axis=0, keepdims=True)
                film_out[row, at, lanes] = film.astype(bf16)
            slope = t + normed * (4.0 * w * (1.0 + w)) * (r * r)
            grad = grad_lifted * scale[at, lanes][None] * slope
            sums_out[0:1, lanes] += jnp.sum(jnp.sum(grad * unit, axis=0), axis=0, keepdims=True)
            sums_out[1:2, lanes] += jnp.sum(jnp.sum(grad, axis=0), axis=0, keepdims=True)
            grad_out[:, at, lanes] = norm_back(grad * gain_here, unit, spread).astype(bf16)

    conv_blocks(padded, back_weight(weight, tile), lambda k: KERNEL - 1 - k, body)


def features_back_body(shards, place_ref, *refs):
    grads, quarters, refs = refs[:shards], refs[shards : 2 * shards], refs[2 * shards :]
    upstream = refs[0]
    grad_out, padded, weight, sems = refs[-4:]
    tile = upstream.shape[2]
    back_front(place_ref, grads, quarters, padded, weight, sems)

    def body(at, a):
        grad_out[:, at, :] = (a + upstream[:, at, :].astype(f32)).astype(bf16)

    conv_blocks(padded, back_weight(weight, tile), lambda k: KERNEL - 1 - k, body)


def back_call(body, name, place, grads, quarters, extras, extra_specs, outs, out_specs):
    shards = len(grads)
    _, samples, width = grads[0].shape
    channels = width * shards
    tile = min(256, width)
    anywhere = pl.BlockSpec(memory_space=pl.ANY)
    return pl.pallas_call(
        functools.partial(body, shards),
        grid_spec=pltpu.PrefetchScalarGridSpec(
            num_scalar_prefetch=1,
            grid=(width // tile,),
            in_specs=[anywhere] * (2 * shards) + extra_specs,
            out_specs=out_specs,
            scratch_shapes=[
                pltpu.VMEM((HORIZON + 2 * HALF, samples, channels), bf16),
                pltpu.VMEM((KERNEL, width, channels), bf16),
                pltpu.SemaphoreType.DMA((2 * shards,)),
            ],
        ),
        out_shape=outs,
        compiler_params=params(1),
        cost_estimate=SHORT,
        name=name,
    )(place, *grads, *quarters, *extras)


def weight_grad_body(sizes, start, taps, order, place_ref, turned, grads, *refs):
    nz = sizes[0]
    near, far = order
    keep, send, padded = refs[-3:]
    rows, frames = turned.shape[2:]
    width = grads.shape[2]
    step = pl.program_id(0)
    stays = step // sizes[far] + 1 == sizes[near]

    @pl.when(step == 0)
    def _():
        zero_ends(padded)
        padded[HALF : HALF + HORIZON] = grads[...]

    lhs = turned[0].reshape(nz * rows, frames)

    def store(out, dtype):
        for k in range(taps):
            at = KERNEL - 1 - start - k
            rhs = padded[at : at + HORIZON].reshape(frames, width)
            part = jnp.dot(lhs, rhs, preferred_element_type=f32).reshape(nz, rows, width)
            out[:, k * rows : (k + 1) * rows, :] = part.astype(dtype)

    @pl.when(stays)
    def _():
        store(keep.at[0], f32)

    @pl.when(jnp.logical_not(stays))
    def _():
        store(send.at[0, 0], bf16)


def weight_grad(place, turned, grads, sizes, start, taps, order, *ready):
    nz, ny, nx = sizes
    near, far = order
    _, rows, frames = turned.shape
    _, samples, width = grads.shape
    height = taps * rows
    turned = turned.reshape(nx * ny, nz, rows, frames)

    def source(s, _):
        away, across = (s // sizes[far] + 1) % sizes[near], s % sizes[far]
        dx, dy = (across, away) if near == 1 else (away, across)
        return (dx * ny + dy, 0, 0, 0)

    leaving = (sizes[near] - 1) * sizes[far]

    def kept(s, _):
        return (jnp.maximum(s - leaving, 0), 0, 0, 0)

    def sent(s, _):
        last = jnp.minimum(s, leaving - 1)
        return (last // sizes[far], last % sizes[far], 0, 0, 0)

    return pl.pallas_call(
        functools.partial(weight_grad_body, sizes, start, taps, order),
        grid_spec=pltpu.PrefetchScalarGridSpec(
            num_scalar_prefetch=1,
            grid=(nx * ny,),
            in_specs=[
                pl.BlockSpec((1, nz, rows, frames), source),
                pl.BlockSpec(grads.shape, lambda s, _: (0, 0, 0)),
            ]
            + [pl.BlockSpec(memory_space=pl.ANY)] * len(ready),
            out_specs=[
                pl.BlockSpec((1, nz, height, width), kept),
                pl.BlockSpec((1, 1, nz, height, width), sent),
            ],
            scratch_shapes=[pltpu.VMEM((HORIZON + 2 * HALF, samples, width), bf16)],
        ),
        out_shape=[
            jax.ShapeDtypeStruct((sizes[far], nz, height, width), f32),
            jax.ShapeDtypeStruct((sizes[near] - 1, sizes[far], nz, height, width), bf16),
        ],
        compiler_params=params(1),
        cost_estimate=SHORT,
        name="weight_grad",
    )(place, turned, grads, *ready)


def film_body(sizes, rows, place_ref, embedded, *refs):
    nz, ny, _ = sizes
    pieces = refs[:ny]
    out, weight_out, weight, sems = refs[ny:]
    parts, samples, deep = embedded.shape
    depth = deep // (nz * ny)
    copies = []
    for dy, piece in enumerate(pieces):
        for z in range(nz):
            there = place_ref[0] ^ line_masks(nz)[1][z]
            owner = there * ny + (place_ref[1] - dy + ny) % ny
            at = pl.ds(pl.multiple_of(owner * depth, BLOCK), depth)
            copies.append(
                pltpu.make_async_copy(piece.at[z], weight.at[at, :], sems.at[len(copies)])
            )
    for copy in copies:
        copy.start()
    for copy in copies:
        copy.wait()
    back = pltpu.make_async_copy(weight, weight_out, sems.at[len(copies)])
    back.start()
    for part in range(parts):
        out[part, :samples, :] = jnp.dot(
            embedded[part], weight[...], preferred_element_type=f32
        )
    edge = rows // BLOCK * BLOCK
    for owner in range(nz * ny):
        block = weight[owner * depth + edge : owner * depth + edge + BLOCK, :].astype(f32)
        for part in range(parts):
            at = samples + owner
            out[part, at : at + 1, :] = block[rows - edge : rows - edge + 1, :]
    back.wait()


def film_call(place, embedded, pieces, sizes, rows):
    nz, ny, nx = sizes
    _, samples, deep = embedded.shape
    width = pieces[0].shape[2]
    anywhere = pl.BlockSpec(memory_space=pl.ANY)
    whole = pl.BlockSpec(memory_space=pltpu.VMEM)
    return pl.pallas_call(
        functools.partial(film_body, sizes, rows),
        in_specs=[pl.BlockSpec(memory_space=pltpu.SMEM), whole] + [anywhere] * ny,
        out_specs=[whole, anywhere],
        out_shape=[
            jax.ShapeDtypeStruct((nx, samples + nz * ny, width), f32),
            jax.ShapeDtypeStruct((deep, width), bf16),
        ],
        scratch_shapes=[
            pltpu.VMEM((deep, width), bf16),
            pltpu.SemaphoreType.DMA((nz * ny + 1,)),
        ],
        compiler_params=pltpu.CompilerParams(vmem_limit_bytes=VMEM_LIMIT),
        cost_estimate=SHORT,
        name="film",
    )(place, embedded, *pieces)


def film_back_body(sizes, place_ref, turned, low, weight, cond_in, onehot, keep, send, table):
    nz, ny, _ = sizes
    depth = turned.shape[0] // (nz * ny)
    for dy in range(ny):
        for r in range(nz):
            owner = (place_ref[0] ^ line_masks(nz)[1][r]) * ny + (place_ref[1] + dy) % ny
            at = pl.ds(pl.multiple_of(owner * depth, BLOCK), depth)
            part = jnp.dot(turned[at, :], low[...], preferred_element_type=f32)
            if dy == 0:
                keep[r] = part
            else:
                send[dy - 1, r] = part.astype(bf16)
    grad = lax.dot_general(
        low[...], weight[...], (((1,), (1,)), ((), ())), preferred_element_type=f32
    )
    rest = grad * mish_slope(cond_in[...])
    total = jnp.zeros(table.shape, f32)
    for _ in range(3):
        part = rest.astype(bf16)
        rest = rest - part.astype(f32)
        total = total + jnp.dot(onehot[...], part, preferred_element_type=f32)
    table[...] = total


def film_back(place, turned, low, weight, cond_in, onehot, sizes):
    nz, ny, _ = sizes
    deep, width = weight.shape
    depth = deep // (nz * ny)
    whole = pl.BlockSpec(memory_space=pltpu.VMEM)
    return pl.pallas_call(
        functools.partial(film_back_body, sizes),
        in_specs=[pl.BlockSpec(memory_space=pltpu.SMEM)] + [whole] * 5,
        out_specs=[whole] * 3,
        out_shape=[
            jax.ShapeDtypeStruct((nz, depth, width), f32),
            jax.ShapeDtypeStruct((ny - 1, nz, depth, width), bf16),
            jax.ShapeDtypeStruct((onehot.shape[0], deep), f32),
        ],
        compiler_params=pltpu.CompilerParams(vmem_limit_bytes=VMEM_LIMIT),
        cost_estimate=SHORT,
        name="film_back",
    )(place, turned, low, weight, cond_in, onehot)


def local(
    features,
    condition,
    task_ids,
    conv_first,
    conv_second,
    film_weight,
    norm_gain_first,
    norm_shift_first,
    norm_gain_second,
    norm_shift_second,
    film_bias,
    task_table,
    out_grad,
    grad_mask,
):
    count, shards = lax.axis_size("dp"), lax.axis_size("shard")
    sizes = digits(count)
    nz, ny, nx = sizes
    me, own = lax.axis_index("dp"), lax.axis_index("shard")
    position = coordinates(me, sizes)
    place = jnp.stack([position[0], position[1], position[2], own]).astype(jnp.int32)
    samples = condition.shape[0]
    channels = features.shape[1]
    width = channels // shards
    tile = min(256, width)
    film_rows, film_width = film_weight.shape

    def own_columns(value, each):
        return lax.dynamic_slice_in_dim(value, own * each, each, value.ndim - 1)

    each = norm_gain_first.shape[0]
    tasks = task_table.shape[0]
    depth = -(-(film_rows + 1) // BLOCK) * BLOCK
    vectors = jnp.concatenate(
        [norm_gain_first, norm_shift_first, norm_gain_second, norm_shift_second, film_bias]
    )
    vectors = jnp.pad(vectors, (0, film_width - vectors.shape[0]))
    film_block = jnp.concatenate(
        [
            film_weight,
            vectors[None],
            jnp.zeros((depth - film_rows - 1, film_width), bf16),
        ]
    )

    def columns_of(value, fill, dx):
        blocks = value.reshape(-1, nz * ny, nx, film_rows)
        blocks = lax.dynamic_index_in_dim(blocks, (position[2] + dx) % nx, 2, keepdims=False)
        if fill is not None:
            fill = jnp.broadcast_to(fill[:, None, None], blocks.shape[:2] + (1,))
            blocks = jnp.concatenate([blocks, fill], axis=2)
        rest = depth - blocks.shape[2]
        return jnp.pad(blocks, ((0, 0), (0, 0), (0, rest))).reshape(-1, nz * ny * depth)

    numbers = task_ids.astype(bf16)
    conditions = [columns_of(condition, numbers, 0)] + [
        move(columns_of(condition, numbers, dx), sizes, 2, dx) for dx in range(1, nx)
    ]
    conditions = jnp.concatenate(conditions).astype(f32)
    onehot = (conditions[:, film_rows : film_rows + 1] == jnp.arange(tasks, dtype=f32)[None]).astype(
        bf16
    )
    inside = (jnp.arange(conditions.shape[1]) % depth < film_rows)[None]
    cond_in = jnp.where(inside, conditions, 0.0) + jnp.dot(
        onehot, columns_of(task_table, None, 0), preferred_element_type=f32
    )
    embedded = mish_act(cond_in).astype(bf16)
    onehot = jnp.pad(onehot.T, ((0, -(-tasks // BLOCK) * BLOCK - tasks), (0, 0)))

    timed, upstream = to_time(features, out_grad, grad_mask)
    turned_a = turn(place, [timed], sizes, False)
    upstream = own_columns(upstream, width)
    residual = own_columns(timed, width)

    lines_a = after(move_lines(conv_first, sizes), timed, turned_a, embedded)
    sides_a = gather_sides(lines_a, sizes)
    film_lines = double_lines(after(film_block, timed), sizes)[0]
    lines_b, steps_b = double_lines(after(conv_second, film_lines), sizes)
    film_lines = after(film_lines, sides_a[1][0], steps_b[0])
    film_pieces = [film_lines] + [move(film_lines, sizes, 1, r) for r in range(1, ny)]
    pieces_a = gather_corners(lines_a, sides_a, HALF, sizes)
    sides_b = gather_sides(after(lines_b, pieces_a[-2][0], pieces_a[-1][0]), sizes)

    film_parts, film_map = film_call(
        place,
        after(embedded.reshape(nx, samples, -1), lines_b),
        film_pieces,
        sizes,
        film_rows,
    )
    film_parts = [film_parts[0]] + [
        move(film_parts[dx], sizes, 2, nx - dx) for dx in range(1, nx)
    ]
    small = jnp.stack([part[samples:, : 6 * each] for part in film_parts])
    film_own = sum(part[:samples] for part in film_parts)
    film_out = in_order(around(film_own), own)
    small = in_order(around(small), own)
    small = in_order([small[:, (nx - r) % nx] for r in range(nx)], position[2])
    small = small.transpose(2, 0, 1, 3).reshape(count * shards, 6 * each)
    gain_a, shift_a, gain_b, shift_b = [
        own_columns(small[:, i * each : (i + 1) * each].reshape(1, -1), width) for i in range(4)
    ]
    bias = small[:, 4 * each : 6 * each].reshape(1, -1)
    film_out = jnp.moveaxis(film_out, 0, 1).reshape(samples, 2 * channels) + bias
    scale = own_columns(film_out[:, :channels], width)
    shifting = own_columns(film_out[:, channels:], width)

    column = pl.BlockSpec((samples, tile), lambda n, _: (0, n))
    vector = pl.BlockSpec((1, tile), lambda n, _: (0, n))
    pair = pl.BlockSpec((2, tile), lambda n, _: (0, n))
    field = pl.BlockSpec((HORIZON, samples, tile), lambda n, _: (0, 0, n))
    spreads = pl.BlockSpec((tile // GROUP, samples, GROUP), lambda n, _: (n, 0, 0))
    films = pl.BlockSpec((2, samples, tile), lambda n, _: (0, 0, n))
    fours = pl.BlockSpec((4, tile), lambda n, _: (0, n))
    low_shape = jax.ShapeDtypeStruct((HORIZON, samples, width), bf16)
    field_shape = jax.ShapeDtypeStruct((HORIZON, samples, width), f32)
    pair_shape = jax.ShapeDtypeStruct((2, width), f32)
    spread_shape = jax.ShapeDtypeStruct((width // GROUP, samples, GROUP), f32)

    unit_a, spread_a, lifted, *quarters_a = conv_call(
        first_body,
        "conv_first",
        place,
        sizes,
        False,
        [timed],
        pieces_a,
        [scale, shifting, gain_a, shift_a],
        [column, column, vector, vector],
        [field_shape, spread_shape, low_shape],
        [field, spreads, field],
        [turned_a],
    )
    pieces_b = gather_corners(lines_b, sides_b, HALF + 1, sizes, spread_a)
    quarters_a = [quarters_a[0]] + [swap(quarters_a[r], r) for r in range(1, shards)]
    lifted = around(lifted)
    turned_b = turn(place, lifted, sizes, True)
    block_own, grad_second, sums_b, *quarters_b = conv_call(
        second_body,
        "conv_second",
        place,
        sizes,
        True,
        lifted,
        pieces_b,
        [residual, upstream, gain_b, shift_b],
        [field, field, vector, vector],
        [low_shape, low_shape, pair_shape],
        [field, field, pair],
        [turned_b],
    )
    block_all = around(block_own)
    quarters_b = [quarters_b[0]] + [swap(quarters_b[r], r) for r in range(1, shards)]

    yx, xy = (1, 2), (2, 1)
    cut = HALF
    near_b = [
        weight_grad(place, turned_b, grad_second, sizes, 0, cut, yx),
        weight_grad(place, turned_b, grad_second, sizes, cut, KERNEL - cut, xy),
    ]
    grad_first, low, sums_a = back_call(
        lifted_back_body,
        "lifted_back",
        place,
        around(grad_second),
        quarters_b,
        [unit_a, spread_a, scale, gain_a, shift_a, *quarters_a[1:]],
        [field, spreads, column, vector, vector]
        + [pl.BlockSpec(memory_space=pl.ANY)] * (shards - 1),
        [
            low_shape,
            jax.ShapeDtypeStruct((2, samples, width), bf16),
            jax.ShapeDtypeStruct((4, width), f32),
        ],
        [field, films, fours],
    )
    low = in_order(around(low), own).transpose(2, 1, 0, 3).reshape(samples, 2 * channels)
    low_own = own_columns(low, film_width)
    first_b = add_near(near_b[0][0], scatter_near(near_b[0][1], sizes, yx), sums_a)
    second_b = add_near(near_b[1][0], scatter_near(near_b[1][1], sizes, xy), sums_a)
    leaving = [[part.astype(bf16) for part in parts[1:]] for parts in (first_b, second_b)]
    cut = HALF + 1
    ready = leaving[0] + leaving[1] + block_all[1:]
    near_a = [weight_grad(place, turned_a, grad_first, sizes, 0, cut, yx, *ready)]
    low_own = after(low_own, near_a[0][0])
    lows = [low_own] + [move(low_own, sizes, 2, dx) for dx in range(1, nx)]
    first_b = scatter_far(first_b[0], leaving[0], sizes, yx)
    second_b = scatter_far(second_b[0], leaving[1], sizes, xy)
    whole_b = jnp.concatenate([first_b, second_b], axis=1).astype(bf16)
    grad_first_all = around(grad_first)
    ready = lows[1:] + grad_first_all[1:] + [whole_b]
    near_a.append(
        weight_grad(place, turned_a, grad_first, sizes, cut, KERNEL - cut, xy, *ready)
    )
    grad_conv_second = lax.psum_scatter(
        whole_b, "dp", scatter_dimension=0, tiled=False, axis_index_groups=line_groups(sizes)
    )
    grad_conv_second = grad_conv_second.astype(f32).reshape(conv_second.shape)

    film_keep, film_send, grad_table = film_back(
        place,
        embedded.T,
        after(jnp.concatenate(lows), near_a[1][0]),
        film_map,
        cond_in,
        onehot,
        sizes,
    )
    sums = jnp.concatenate([sums_a[:2], sums_b, sums_a[2:]])
    sums = lax.dynamic_update_slice(jnp.zeros((6, channels), f32), sums, (0, own * width)).reshape(-1)
    wide = grad_table.shape[1]
    rows = -(-(tasks + -(-sums.shape[0] // wide)) // 8) * 8
    sums = jnp.pad(sums, (0, (rows - tasks) * wide - sums.shape[0])).reshape(rows - tasks, wide)
    total = sum_along(sum_shards(jnp.concatenate([grad_table[:tasks], sums])), sizes, 0)

    got_a = scatter_near(near_a[0][1], sizes, yx)
    got_b = scatter_near(near_a[1][1], sizes, xy)
    first_a = add_near(near_a[0][0], got_a, *got_b)
    second_a = add_near(near_a[1][0], got_b)
    leaving = [[part.astype(bf16) for part in parts[1:]] for parts in (first_a, second_a)]
    grad_own = back_call(
        features_back_body,
        "features_back",
        place,
        grad_first_all,
        quarters_a,
        [upstream, total],
        [field, pl.BlockSpec(memory_space=pl.ANY)],
        low_shape,
        field,
    )
    first_a = scatter_far(first_a[0], leaving[0], sizes, yx)
    second_a = scatter_far(second_a[0], leaving[1], sizes, xy)
    film_keep = film_keep + sum(
        move(film_send[dy - 1], sizes, 1, dy).astype(f32) for dy in range(1, ny)
    )
    grad_conv_first = jnp.concatenate(
        [halve_lines(first_a, sizes), halve_lines(second_a, sizes)]
    ).reshape(conv_first.shape)
    grad_film_weight = halve_lines(film_keep, sizes)[:film_rows]
    total = sum_along(after(total, second_a), sizes, 1)
    totals = [total] + [move(total, sizes, 2, r) for r in range(1, nx)]
    totals = in_order(totals, position[2])
    totals = in_order(around(totals), own)
    totals = jnp.moveaxis(totals, 0, 1).reshape(nx, rows, wide)
    block_out = from_time(place, block_all)
    grad_features = from_time(place, around(grad_own))

    grad_table = totals[:, :tasks].reshape(nx, tasks, nz * ny, depth)[..., :film_rows]
    grad_table = grad_table.transpose(1, 2, 0, 3).reshape(tasks, -1)
    sums = totals[0, tasks:]
    for x in range(1, nx):
        sums = sums + totals[x, tasks:]
    sums = sums.reshape(-1)[: 6 * channels].reshape(6, channels)
    index = me * shards + own
    small = [lax.dynamic_slice(sums[i], (index * each,), (each,)) for i in range(4)]
    grad_film_bias = lax.dynamic_slice(sums[4:].reshape(-1), (index * 2 * each,), (2 * each,))
    return (
        block_out,
        grad_features,
        grad_conv_first,
        grad_conv_second,
        grad_film_weight,
        small[0],
        small[1],
        small[2],
        small[3],
        grad_film_bias,
        grad_table,
    )


def solution(mesh):
    return jax.shard_map(
        local,
        mesh=mesh,
        in_specs=(
            P("dp", None),
            P("dp", None),
            P("dp"),
            P(None, "dp", "shard"),
            P(None, "dp", "shard"),
            P("dp", "shard"),
            P(("dp", "shard")),
            P(("dp", "shard")),
            P(("dp", "shard")),
            P(("dp", "shard")),
            P(("dp", "shard")),
            P(),
            P("dp", None),
            P("dp"),
        ),
        out_specs=(
            P("dp", None),
            P("dp", None),
            P(None, "dp", "shard"),
            P(None, "dp", "shard"),
            P("dp", "shard"),
            P(("dp", "shard")),
            P(("dp", "shard")),
            P(("dp", "shard")),
            P(("dp", "shard")),
            P(("dp", "shard")),
            P(),
        ),
        check_vma=False,
    )
```

```python
import functools

import jax
import jax.numpy as jnp
from jax import lax
from jax.experimental import pallas as pl
from jax.experimental.pallas import tpu as pltpu
from jax.sharding import PartitionSpec as P

KERNEL = 5
HALF = KERNEL // 2
HORIZON = 16
GROUP = 128
EPSILON = 1e-05
BLOCK = 16
VMEM_LIMIT = 48 * 1024 * 1024
SHORT = pl.CostEstimate(flops=1, bytes_accessed=1, transcendentals=0)


def lasting(microseconds):
    flops = int(microseconds * 5.175e+08)
    return pl.CostEstimate(flops=flops, bytes_accessed=1, transcendentals=0)


f32 = jnp.float32
bf16 = jnp.bfloat16


def mish_parts(v):
    w = jnp.exp(jnp.minimum(v, 20.0))
    n = w * (w + 2.0)
    r = 1.0 / (n + 2.0)
    return w, r, n * r


def mish_act(v):
    return v * mish_parts(v)[2]


def mish_slope(v):
    w, r, t = mish_parts(v)
    return t + v * (4.0 * w * (1.0 + w)) * (r * r)


def digits(count):
    bits = count.bit_length() - 1
    small = bits // 3
    return (1 << (bits - 2 * small), 1 << small, 1 << small)


def coordinates(index, sizes):
    _, ny, nx = sizes
    return (index // (ny * nx), (index // nx) % ny, index % nx)


def flat(position, sizes):
    _, ny, nx = sizes
    return (position[0] * ny + position[1]) * nx + position[2]


def move(value, sizes, axis, by):
    count = sizes[0] * sizes[1] * sizes[2]
    pairs = []
    for source in range(count):
        position = list(coordinates(source, sizes))
        position[axis] = (position[axis] + by) % sizes[axis]
        pairs.append((source, flat(position, sizes)))
    return lax.ppermute(value, "dp", pairs)


def swap(value, by):
    count = lax.axis_size("shard")
    return lax.ppermute(value, "shard", [(i, (i + by) % count) for i in range(count)])


def around(value):
    return [value] + [swap(value, r) for r in range(1, lax.axis_size("shard"))]


def in_order(parts, own):
    count = len(parts)
    if count == 2:
        mine = own == 0
        return jnp.stack([jnp.where(mine, parts[0], parts[1]), jnp.where(mine, parts[1], parts[0])])
    return jnp.stack(parts)[(own - jnp.arange(count)) % count]


def trade(value, sizes, axis, mask):
    count = sizes[0] * sizes[1] * sizes[2]
    pairs = []
    for source in range(count):
        position = list(coordinates(source, sizes))
        position[axis] ^= mask
        pairs.append((source, flat(position, sizes)))
    return lax.ppermute(value, "dp", pairs)


def line_groups(sizes):
    nz, ny, nx = sizes
    return [[flat((z, y, x), sizes) for z in range(nz)] for y in range(ny) for x in range(nx)]


def move_lines(own, sizes):
    return jnp.stack([own] + [move(own, sizes, 0, r) for r in range(1, sizes[0])])


def line_masks(count):
    masks = [1 << bit for bit in reversed(range(count.bit_length() - 1))]
    order = [0]
    for mask in masks:
        order = order + [other ^ mask for other in order]
    return masks, order


def line_place(other, count):
    bits = count.bit_length() - 1
    return sum(((other >> bit) & 1) << (bits - 1 - bit) for bit in range(bits))


def double_lines(own, sizes):
    lines = own[None]
    for mask in line_masks(sizes[0])[0]:
        lines = jnp.concatenate([lines, trade(lines, sizes, 0, mask)])
    return lines


def gather_sides(lines, sizes):
    return (
        [move(lines, sizes, 2, r) for r in range(1, sizes[2])],
        [move(lines, sizes, 1, r) for r in range(1, sizes[1])],
    )


def gather_corners(lines, sides, sizes, *ready):
    by_x, by_y = sides
    half = lines.shape[-1] // 2
    pieces = [(lines, 0, 0, 0)]
    pieces += [(part, 0, dx + 1, 0) for dx, part in enumerate(by_x)]
    pieces += [(part, 0, 0, dy + 1) for dy, part in enumerate(by_y)]
    lefts = [after(part[..., :half], *ready) for part in by_x]
    rights = [after(part[..., half:], *ready) for part in by_y]
    for dx in range(1, sizes[2]):
        for dy in range(1, sizes[1]):
            pieces.append((move(rights[dy - 1], sizes, 2, dx), half, dx, dy))
            pieces.append((move(lefts[dx - 1], sizes, 1, dy), 0, dx, dy))
    return pieces


def scatter_step(parts, sizes, axis):
    return [move(part, sizes, axis, r + 1) for r, part in enumerate(parts)]


def add_near(keep, got):
    sums = [keep[r] + sum(part[r].astype(f32) for part in got) for r in range(keep.shape[0])]
    return sums[0], [part.astype(bf16) for part in sums[1:]]


def add_far(own, got):
    for part in got:
        own = own + part.astype(f32)
    return own


def add_halves(own, got):
    half = own.shape[0] // 2
    stay = add_far(own[:half], [part[:half] for part in got])
    return stay, add_far(own[half:], [part[half:] for part in got]).astype(bf16)


def sum_shards(value, *ready):
    shards = lax.axis_size("shard")
    own = lax.axis_index("shard")
    rows = value.shape[0] // shards

    def part(r):
        return lax.dynamic_slice_in_dim(value, (own + r) % shards * rows, rows, 0)

    total = part(0)
    for r in range(1, shards):
        total = total + after(swap(part(r), r), *ready)
    return total


def sum_along(total, sizes, axis, *ready):
    steps = sizes[axis].bit_length() - 1
    for step in range(steps):
        got = trade(total, sizes, axis, 1 << step)
        total = total + after(got, *ready[min(step, len(ready) - 1)])
    return total


def nothing(*_):
    pass


def after(value, *ready):
    anywhere = pl.BlockSpec(memory_space=pl.ANY)
    return pl.pallas_call(
        nothing,
        in_specs=[anywhere] * (1 + len(ready)),
        out_specs=anywhere,
        out_shape=jax.ShapeDtypeStruct(value.shape, value.dtype),
        input_output_aliases={0: 0},
        cost_estimate=SHORT,
        name="after",
    )(value, *ready)


def params(dims):
    return pltpu.CompilerParams(
        dimension_semantics=("arbitrary",) * dims, vmem_limit_bytes=VMEM_LIMIT
    )


def regroup_matrix():
    side = BLOCK * HORIZON
    row = lax.broadcasted_iota(jnp.int32, (side, side), 0)
    column = lax.broadcasted_iota(jnp.int32, (side, side), 1)
    return (column == (row % BLOCK) * HORIZON + row // BLOCK).astype(bf16)


def to_time_body(matrix, features_ref, grads_ref, mask_ref, features_out, grads_out):
    channels = features_ref.shape[1]
    moved = jnp.dot(matrix[...], features_ref[...], preferred_element_type=f32)
    features_out[...] = moved.astype(bf16).reshape(HORIZON, BLOCK, channels)
    masked = matrix[...] * mask_ref[0].astype(bf16)
    moved = jnp.dot(masked, grads_ref[...], preferred_element_type=f32)
    grads_out[...] = moved.astype(bf16).reshape(HORIZON, BLOCK, channels)


def to_time(matrix, features, grads, mask):
    frames, channels = features.shape
    samples = frames // HORIZON
    steps = samples // BLOCK
    side = BLOCK * HORIZON
    square = pl.BlockSpec((side, side), lambda b: (0, 0))
    rows = pl.BlockSpec((side, channels), lambda b: (b, 0))
    out = pl.BlockSpec((HORIZON, BLOCK, channels), lambda b: (0, b, 0))
    shape = jax.ShapeDtypeStruct((HORIZON, samples, channels), bf16)
    return pl.pallas_call(
        to_time_body,
        grid=(steps,),
        in_specs=[square, rows, rows, pl.BlockSpec((1, 1, side), lambda b: (b, 0, 0))],
        out_specs=[out, out],
        out_shape=[shape, shape],
        compiler_params=params(1),
        cost_estimate=lasting(7),
        name="to_time",
    )(matrix, features, grads, mask.reshape(steps, 1, side))


def from_time_body(count, place_ref, matrix, *refs):
    pieces, out = refs[:-1], refs[-1]
    width = pieces[0].shape[2]
    moved = []
    for piece in pieces:
        rows = piece[...].reshape(HORIZON * BLOCK, width)
        moved.append(jnp.dot(matrix[...], rows, preferred_element_type=f32).astype(bf16))
    for own in range(count):

        @pl.when(place_ref[3] == own)
        def _(own=own):
            for r, rows in enumerate(moved):
                column = (own - r) % count * width
                out[:, column : column + width] = rows


def from_time(place, matrix, pieces):
    horizon, samples, width = pieces[0].shape
    count = len(pieces)
    channels = width * count
    return pl.pallas_call(
        functools.partial(from_time_body, count),
        grid_spec=pltpu.PrefetchScalarGridSpec(
            num_scalar_prefetch=1,
            grid=(samples // BLOCK,),
            in_specs=[pl.BlockSpec(matrix.shape, lambda b, _: (0, 0))]
            + [pl.BlockSpec((horizon, BLOCK, width), lambda b, _: (0, b, 0))] * count,
            out_specs=pl.BlockSpec((horizon * BLOCK, channels), lambda b, _: (b, 0)),
        ),
        out_shape=jax.ShapeDtypeStruct((horizon * samples, channels), bf16),
        compiler_params=params(1),
        cost_estimate=SHORT,
        name="from_time",
    )(place, matrix, *pieces)


def turn_body(sizes, rows, ordered, place_ref, *refs):
    pieces, out = refs[:-1], refs[-1]
    count, width = len(pieces), pieces[0].shape[2]
    nz, ny, nx = sizes
    for r, piece in enumerate(pieces):
        shard = (place_ref[3] + count - r) % count
        for tile in range(width // GROUP):
            block = piece[:, :, tile * GROUP : (tile + 1) * GROUP]
            turned = block.reshape(-1, GROUP).T
            for j in range(GROUP // rows):
                owner = shard * (width // rows) + tile * (GROUP // rows) + j
                oz, oy, ox = coordinates(owner, sizes)
                dz = oz if ordered else line_place(oz ^ place_ref[0], nz)
                dy = (oy - place_ref[1] + ny) % ny
                dx = (ox - place_ref[2] + nx) % nx
                out[pl.ds((dx * ny + dy) * nz + dz, 1)] = turned[j * rows : (j + 1) * rows][None]


def turn(place, pieces, sizes, ordered):
    horizon, samples, width = pieces[0].shape
    count = sizes[0] * sizes[1] * sizes[2]
    rows = len(pieces) * width // count
    return pl.pallas_call(
        functools.partial(turn_body, sizes, rows, ordered),
        in_specs=[pl.BlockSpec(memory_space=pltpu.SMEM)]
        + [pl.BlockSpec(memory_space=pltpu.VMEM)] * len(pieces),
        out_specs=pl.BlockSpec(memory_space=pltpu.VMEM),
        out_shape=jax.ShapeDtypeStruct((count, rows, horizon * samples), bf16),
        compiler_params=pltpu.CompilerParams(vmem_limit_bytes=VMEM_LIMIT),
        cost_estimate=lasting(3.5),
        name="turn",
    )(place, *pieces)


def zero_ends(padded):
    steps = padded.shape[0]
    zeros = jnp.zeros((HALF,) + padded.shape[1:], padded.dtype)
    padded[:HALF] = zeros
    padded[steps - HALF :] = zeros


def weight_copies(sizes, paired, place_ref, pieces, where, weight, sems):
    nz, ny, nx = sizes
    copies = []
    for piece, (column, dx, dy) in zip(pieces, where):
        _, _, rows, width = piece.shape
        for r in range(nz):
            z = place_ref[0] ^ line_masks(nz)[1][r] if paired else (place_ref[0] - r + nz) % nz
            owner = flat((z, (place_ref[1] - dy + ny) % ny, (place_ref[2] - dx + nx) % nx), sizes)
            at = pl.ds(pl.multiple_of(owner * rows, rows), rows)
            copies.append(
                pltpu.make_async_copy(
                    piece.at[r], weight.at[:, at, pl.ds(column, width)], sems.at[len(copies)]
                )
            )
    return copies


def column_copies(place_ref, pieces, target, sems, first_sem):
    count, width = len(pieces), pieces[0].shape[-1]
    copies = []
    for r, piece in enumerate(pieces):
        column = pl.multiple_of(((place_ref[3] + count - r) % count) * width, width)
        copies.append(
            pltpu.make_async_copy(
                piece, target.at[..., pl.ds(column, width)], sems.at[first_sem + r]
            )
        )
    return copies


def group_mean(value):
    return jnp.sum(jnp.sum(value, axis=0), axis=1, keepdims=True)[None] / (HORIZON * GROUP)


def norm_of(a):
    centre = a - group_mean(a)
    spread = lax.rsqrt(group_mean(centre * centre) + EPSILON)
    return centre * spread, spread


def norm_back(h, unit, spread):
    return spread * (h - group_mean(h) - unit * group_mean(h * unit))


def conv_blocks(padded, weight_of, order, body):
    samples, channels = padded.shape[1:]
    for b in range(samples // BLOCK):
        at = slice(b * BLOCK, (b + 1) * BLOCK)
        total = None
        for k in range(KERNEL):
            start = order(k)
            rows = padded[start : start + HORIZON, at, :].reshape(HORIZON * BLOCK, channels)
            part = weight_of(rows, k)
            total = part if total is None else total + part
        body(at, total.reshape(HORIZON, BLOCK, total.shape[1]))


def conv_front(sizes, paired, where, place_ref, inputs, pieces, quarters, padded, weight, sems):
    n = pl.program_id(0)
    count = len(quarters)
    height = weight.shape[2]
    base = len(pieces) * sizes[0] + len(inputs)

    def out_copies():
        return [
            pltpu.make_async_copy(
                weight.at[
                    :, pl.ds(pl.multiple_of(((place_ref[3] + r) % count) * height, height), height), :
                ],
                quarter,
                sems.at[base + r],
            )
            for r, quarter in enumerate(quarters)
        ]

    @pl.when(n == 0)
    def _():
        copies = weight_copies(sizes, paired, place_ref, pieces, where, weight, sems)
        copies += column_copies(
            place_ref, inputs, padded.at[pl.ds(HALF, HORIZON)], sems, len(copies)
        )
        for copy in copies:
            copy.start()
        zero_ends(padded)
        for copy in copies:
            copy.wait()
        for copy in out_copies():
            copy.start()

    def finish():
        @pl.when(n == pl.num_programs(0) - 1)
        def _():
            for copy in out_copies():
                copy.wait()

    return finish


def conv_weight(weight, tile):
    column = pl.ds(pl.multiple_of(pl.program_id(0) * tile, tile), tile)

    def apply(rows, k):
        return jnp.dot(rows, weight[k, :, column], preferred_element_type=f32)

    return apply


def groups_of(width):
    return [(g, slice(g * GROUP, (g + 1) * GROUP)) for g in range(width // GROUP)]


def first_body(sizes, paired, where, shards, waits, place_ref, *refs):
    inputs, refs = refs[:1], refs[1:]
    pieces, refs = refs[: len(where)], refs[len(where) :]
    scale, shifting, gain, shift = refs[:4]
    refs = refs[4 + waits :]
    unit_out, spread_out, lifted_out = refs[:3]
    quarters = refs[3 : 3 + shards]
    padded, weight, sems = refs[3 + shards :]
    tile = unit_out.shape[2]
    finish = conv_front(
        sizes, paired, where, place_ref, inputs, pieces, quarters, padded, weight, sems
    )

    def body(at, a):
        for group, lanes in groups_of(tile):
            unit, spread = norm_of(a[:, :, lanes])
            unit_out[:, at, lanes] = unit
            spread_out[group, at, :] = jnp.broadcast_to(spread[0], (BLOCK, GROUP))
            mixed = mish_act(unit * gain[:, lanes][None] + shift[:, lanes][None])
            lifted = scale[at, lanes][None] * mixed + shifting[at, lanes][None]
            lifted_out[:, at, lanes] = lifted.astype(bf16)

    conv_blocks(padded, conv_weight(weight, tile), lambda k: k, body)
    finish()


def second_body(sizes, paired, where, shards, waits, place_ref, *refs):
    inputs, refs = refs[:shards], refs[shards:]
    pieces, refs = refs[: len(where)], refs[len(where) :]
    features, upstream, gain, shift = refs[:4]
    refs = refs[4 + waits :]
    block_out, grad_out, sums_out = refs[:3]
    quarters = refs[3 : 3 + shards]
    padded, weight, sems = refs[3 + shards :]
    tile = block_out.shape[2]
    finish = conv_front(
        sizes, paired, where, place_ref, inputs, pieces, quarters, padded, weight, sems
    )
    sums_out[...] = jnp.zeros_like(sums_out)

    def body(at, a):
        for _, lanes in groups_of(tile):
            unit, spread = norm_of(a[:, :, lanes])
            gain_here = gain[:, lanes][None]
            normed = unit * gain_here + shift[:, lanes][None]
            w, r, t = mish_parts(normed)
            block = features[:, at, lanes].astype(f32) + normed * t
            block_out[:, at, lanes] = block.astype(bf16)
            slope = t + normed * (4.0 * w * (1.0 + w)) * (r * r)
            grad = upstream[:, at, lanes].astype(f32) * slope
            sums_out[0:1, lanes] += jnp.sum(jnp.sum(grad * unit, axis=0), axis=0, keepdims=True)
            sums_out[1:2, lanes] += jnp.sum(jnp.sum(grad, axis=0), axis=0, keepdims=True)
            grad_out[:, at, lanes] = norm_back(grad * gain_here, unit, spread).astype(bf16)

    conv_blocks(padded, conv_weight(weight, tile), lambda k: k, body)
    finish()


def conv_call(
    body, name, place, sizes, paired, inputs, pieces, extras, extra_specs, outs, out_specs, ready
):
    shards = lax.axis_size("shard")
    _, samples, depth = inputs[0].shape
    count = len(inputs)
    channels = count * depth
    arrays = [piece[0] for piece in pieces]
    where = tuple(piece[1:] for piece in pieces)
    width = arrays[0].shape[3]
    tile = min(256, width)
    quarter = jax.ShapeDtypeStruct((KERNEL, width, width), bf16)
    anywhere = pl.BlockSpec(memory_space=pl.ANY)
    return pl.pallas_call(
        functools.partial(body, sizes, paired, where, shards, len(ready)),
        grid_spec=pltpu.PrefetchScalarGridSpec(
            num_scalar_prefetch=1,
            grid=(width // tile,),
            in_specs=[anywhere] * (count + len(arrays)) + extra_specs + [anywhere] * len(ready),
            out_specs=out_specs + [anywhere] * shards,
            scratch_shapes=[
                pltpu.VMEM((HORIZON + 2 * HALF, samples, channels), bf16),
                pltpu.VMEM((KERNEL, channels, width), bf16),
                pltpu.SemaphoreType.DMA((len(arrays) * sizes[0] + count + shards,)),
            ],
        ),
        out_shape=outs + [quarter] * shards,
        compiler_params=params(1),
        cost_estimate=lasting(18),
        name=name,
    )(place, *inputs, *arrays, *extras, *ready)


def back_front(place_ref, grads, quarters, padded, weight, sems):
    @pl.when(pl.program_id(0) == 0)
    def _():
        copies = column_copies(place_ref, grads, padded.at[pl.ds(HALF, HORIZON)], sems, 0)
        copies += column_copies(place_ref, quarters, weight, sems, len(copies))
        for copy in copies:
            copy.start()
        zero_ends(padded)
        for copy in copies:
            copy.wait()


def back_weight(weight, tile):
    at = pl.ds(pl.multiple_of(pl.program_id(0) * tile, tile), tile)

    def apply(rows, k):
        return lax.dot_general(
            rows, weight[k, at, :], (((1,), (1,)), ((), ())), preferred_element_type=f32
        )

    return apply


def lifted_back_body(shards, place_ref, *refs):
    grads, quarters, refs = refs[:shards], refs[shards : 2 * shards], refs[2 * shards :]
    unit_in, spread_in, scale, gain, shift = refs[:5]
    grad_out, film_out, sums_out, padded, weight, sems = refs[-6:]
    tile = unit_in.shape[2]
    back_front(place_ref, grads, quarters, padded, weight, sems)
    sums_out[...] = jnp.zeros_like(sums_out)

    def body(at, a):
        for group, lanes in groups_of(tile):
            grad_lifted = a[:, :, lanes]
            unit = unit_in[:, at, lanes]
            spread = spread_in[group, at, :][None]
            gain_here = gain[:, lanes][None]
            normed = unit * gain_here + shift[:, lanes][None]
            w, r, t = mish_parts(normed)
            for row, film in enumerate((grad_lifted * (normed * t), grad_lifted)):
                film = jnp.sum(film, axis=0)
                sums_out[2 + row : 3 + row, lanes] += jnp.sum(film, axis=0, keepdims=True)
                film_out[row, at, lanes] = film.astype(bf16)
            slope = t + normed * (4.0 * w * (1.0 + w)) * (r * r)
            grad = grad_lifted * scale[at, lanes][None] * slope
            sums_out[0:1, lanes] += jnp.sum(jnp.sum(grad * unit, axis=0), axis=0, keepdims=True)
            sums_out[1:2, lanes] += jnp.sum(jnp.sum(grad, axis=0), axis=0, keepdims=True)
            grad_out[:, at, lanes] = norm_back(grad * gain_here, unit, spread).astype(bf16)

    conv_blocks(padded, back_weight(weight, tile), lambda k: KERNEL - 1 - k, body)


def features_back_body(shards, place_ref, *refs):
    grads, quarters, refs = refs[:shards], refs[shards : 2 * shards], refs[2 * shards :]
    upstream = refs[0]
    grad_out, padded, weight, sems = refs[-4:]
    tile = upstream.shape[2]
    back_front(place_ref, grads, quarters, padded, weight, sems)

    def body(at, a):
        grad_out[:, at, :] = (a + upstream[:, at, :].astype(f32)).astype(bf16)

    conv_blocks(padded, back_weight(weight, tile), lambda k: KERNEL - 1 - k, body)


def back_call(
    body, name, place, grads, quarters, extras, extra_specs, outs, out_specs, estimate
):
    shards = len(grads)
    _, samples, width = grads[0].shape
    channels = width * shards
    tile = min(256, width)
    anywhere = pl.BlockSpec(memory_space=pl.ANY)
    return pl.pallas_call(
        functools.partial(body, shards),
        grid_spec=pltpu.PrefetchScalarGridSpec(
            num_scalar_prefetch=1,
            grid=(width // tile,),
            in_specs=[anywhere] * (2 * shards) + extra_specs,
            out_specs=out_specs,
            scratch_shapes=[
                pltpu.VMEM((HORIZON + 2 * HALF, samples, channels), bf16),
                pltpu.VMEM((KERNEL, width, channels), bf16),
                pltpu.SemaphoreType.DMA((2 * shards,)),
            ],
        ),
        out_shape=outs,
        compiler_params=params(1),
        cost_estimate=lasting(estimate),
        name=name,
    )(place, *grads, *quarters, *extras)


def half_grad_body(sizes, along_y, half, turned, grads, *refs):
    nz, ny, nx = sizes
    keep, send, padded = refs[-3:]
    rows, frames = turned.shape[2:]
    width = keep.shape[3]
    step = pl.program_id(0)
    away = step // (nx if along_y else ny) + 1
    stays = away == (ny if along_y else nx)

    @pl.when(step == 0)
    def _():
        zero_ends(padded)
        padded[HALF : HALF + HORIZON] = grads[:, :, half * width : (half + 1) * width]

    lhs = turned[0].reshape(nz * rows, frames)

    def store(out):
        for k in range(KERNEL):
            at = KERNEL - 1 - k
            rhs = padded[at : at + HORIZON].reshape(frames, width)
            part = jnp.dot(lhs, rhs, preferred_element_type=f32).reshape(nz, rows, width)
            out[:, k * rows : (k + 1) * rows, :] = part.astype(out.dtype)

    @pl.when(stays)
    def _():
        store(keep.at[0])

    @pl.when(jnp.logical_not(stays))
    def _():
        store(send.at[0, 0])


def half_grad(estimate, turned, grads, sizes, along_y, half, *ready):
    nz, ny, nx = sizes
    near, far = (ny, nx) if along_y else (nx, ny)
    _, rows, frames = turned.shape
    _, samples, width = grads.shape
    height, width = KERNEL * rows, width // 2
    turned = turned.reshape(nx * ny, nz, rows, frames)
    leaving = (near - 1) * far

    def source(s):
        away, across = (s // far + 1) % near, s % far
        dx, dy = (across, away) if along_y else (away, across)
        return (dx * ny + dy, 0, 0, 0)

    def kept(s):
        return (jnp.maximum(s - leaving, 0), 0, 0, 0)

    def sent(s):
        last = jnp.minimum(s, leaving - 1)
        return (last // far, last % far, 0, 0, 0)

    return pl.pallas_call(
        functools.partial(half_grad_body, sizes, along_y, half),
        grid=(nx * ny,),
        in_specs=[
            pl.BlockSpec((1, nz, rows, frames), source),
            pl.BlockSpec(grads.shape, lambda s: (0, 0, 0)),
        ]
        + [pl.BlockSpec(memory_space=pl.ANY)] * len(ready),
        out_specs=[
            pl.BlockSpec((1, nz, height, width), kept),
            pl.BlockSpec((1, 1, nz, height, width), sent),
        ],
        out_shape=[
            jax.ShapeDtypeStruct((far, nz, height, width), f32),
            jax.ShapeDtypeStruct((near - 1, far, nz, height, width), bf16),
        ],
        scratch_shapes=[pltpu.VMEM((HORIZON + 2 * HALF, samples, width), bf16)],
        compiler_params=params(1),
        cost_estimate=estimate,
        name="half_grad",
    )(turned, grads, *ready)


def near_got(grads, sizes):
    _, send_left, _, send_right = grads
    left = scatter_step([send_left[r] for r in range(sizes[1] - 1)], sizes, 1)
    right = scatter_step([send_right[r] for r in range(sizes[2] - 1)], sizes, 2)
    return left, right


def near_sums(grads, got, *ready):
    keep_left, _, keep_right, _ = grads
    left = add_near(keep_left, [after(part, *ready) for part in got[0]])
    return left, add_near(keep_right, [after(part, *ready) for part in got[1]])


def far_got(near, sizes):
    (_, left), (_, right) = near
    return scatter_step(left, sizes, 2), scatter_step(right, sizes, 1)


def far_sums(near, got):
    (left, _), (right, _) = near
    return add_far(left, got[0]), add_far(right, got[1])


def film_body(sizes, rows, place_ref, embedded, *refs):
    nz, ny, _ = sizes
    pieces = refs[:ny]
    out, weight_out, weight, sems = refs[ny:]
    parts, samples, deep = embedded.shape
    depth = deep // (nz * ny)
    copies = []
    for dy, piece in enumerate(pieces):
        for z in range(nz):
            there = place_ref[0] ^ line_masks(nz)[1][z]
            owner = there * ny + (place_ref[1] - dy + ny) % ny
            at = pl.ds(pl.multiple_of(owner * depth, BLOCK), depth)
            copies.append(
                pltpu.make_async_copy(piece.at[z], weight.at[at, :], sems.at[len(copies)])
            )
    for copy in copies:
        copy.start()
    for copy in copies:
        copy.wait()
    back = pltpu.make_async_copy(weight, weight_out, sems.at[len(copies)])
    back.start()
    for part in range(parts):
        out[part, :samples, :] = jnp.dot(
            embedded[part], weight[...], preferred_element_type=f32
        )
    edge = rows // BLOCK * BLOCK
    for owner in range(nz * ny):
        block = weight[owner * depth + edge : owner * depth + edge + BLOCK, :].astype(f32)
        for part in range(parts):
            at = samples + owner
            out[part, at : at + 1, :] = block[rows - edge : rows - edge + 1, :]
    back.wait()


def film_call(place, embedded, pieces, sizes, rows):
    nz, ny, nx = sizes
    _, samples, deep = embedded.shape
    width = pieces[0].shape[2]
    anywhere = pl.BlockSpec(memory_space=pl.ANY)
    whole = pl.BlockSpec(memory_space=pltpu.VMEM)
    return pl.pallas_call(
        functools.partial(film_body, sizes, rows),
        in_specs=[pl.BlockSpec(memory_space=pltpu.SMEM), whole] + [anywhere] * ny,
        out_specs=[whole, anywhere],
        out_shape=[
            jax.ShapeDtypeStruct((nx, samples + nz * ny, width), f32),
            jax.ShapeDtypeStruct((deep, width), bf16),
        ],
        scratch_shapes=[
            pltpu.VMEM((deep, width), bf16),
            pltpu.SemaphoreType.DMA((nz * ny + 1,)),
        ],
        compiler_params=pltpu.CompilerParams(vmem_limit_bytes=VMEM_LIMIT),
        cost_estimate=lasting(3),
        name="film",
    )(place, embedded, *pieces)


def film_back_body(sizes, place_ref, turned, low, weight, cond_in, onehot, keep, send, table):
    nz, ny, _ = sizes
    depth = turned.shape[0] // (nz * ny)
    for dy in range(ny):
        for r in range(nz):
            owner = (place_ref[0] ^ line_masks(nz)[1][r]) * ny + (place_ref[1] + dy) % ny
            at = pl.ds(pl.multiple_of(owner * depth, BLOCK), depth)
            part = jnp.dot(turned[at, :], low[...], preferred_element_type=f32)
            if dy == 0:
                keep[r] = part
            else:
                send[dy - 1, r] = part.astype(bf16)
    grad = lax.dot_general(
        low[...], weight[...], (((1,), (1,)), ((), ())), preferred_element_type=f32
    )
    rest = grad * mish_slope(cond_in[...])
    total = jnp.zeros(table.shape, f32)
    for _ in range(3):
        part = rest.astype(bf16)
        rest = rest - part.astype(f32)
        total = total + jnp.dot(onehot[...], part, preferred_element_type=f32)
    table[...] = total


def film_back(place, turned, low, weight, cond_in, onehot, sizes):
    nz, ny, _ = sizes
    deep, width = weight.shape
    depth = deep // (nz * ny)
    whole = pl.BlockSpec(memory_space=pltpu.VMEM)
    return pl.pallas_call(
        functools.partial(film_back_body, sizes),
        in_specs=[pl.BlockSpec(memory_space=pltpu.SMEM)] + [whole] * 5,
        out_specs=[whole] * 3,
        out_shape=[
            jax.ShapeDtypeStruct((nz, depth, width), f32),
            jax.ShapeDtypeStruct((ny - 1, nz, depth, width), bf16),
            jax.ShapeDtypeStruct((onehot.shape[0], deep), f32),
        ],
        compiler_params=pltpu.CompilerParams(vmem_limit_bytes=VMEM_LIMIT),
        cost_estimate=lasting(2.5),
        name="film_back",
    )(place, turned, low, weight, cond_in, onehot)


def local(
    features,
    condition,
    task_ids,
    conv_first,
    conv_second,
    film_weight,
    norm_gain_first,
    norm_shift_first,
    norm_gain_second,
    norm_shift_second,
    film_bias,
    task_table,
    out_grad,
    grad_mask,
):
    count, shards = lax.axis_size("dp"), lax.axis_size("shard")
    sizes = digits(count)
    nz, ny, nx = sizes
    me, own = lax.axis_index("dp"), lax.axis_index("shard")
    position = coordinates(me, sizes)
    place = jnp.stack([position[0], position[1], position[2], own]).astype(jnp.int32)
    samples = condition.shape[0]
    channels = features.shape[1]
    width = channels // shards
    tile = min(256, width)
    film_rows, film_width = film_weight.shape

    def own_columns(value, each):
        return lax.dynamic_slice_in_dim(value, own * each, each, value.ndim - 1)

    each = norm_gain_first.shape[0]
    tasks = task_table.shape[0]
    depth = -(-(film_rows + 1) // BLOCK) * BLOCK
    vectors = jnp.concatenate(
        [norm_gain_first, norm_shift_first, norm_gain_second, norm_shift_second, film_bias]
    )
    vectors = jnp.pad(vectors, (0, film_width - vectors.shape[0]))
    film_block = jnp.concatenate(
        [
            film_weight,
            vectors[None],
            jnp.zeros((depth - film_rows - 1, film_width), bf16),
        ]
    )

    def columns_of(value, fill, dx):
        blocks = value.reshape(-1, nz * ny, nx, film_rows)
        blocks = lax.dynamic_index_in_dim(blocks, (position[2] + dx) % nx, 2, keepdims=False)
        if fill is not None:
            fill = jnp.broadcast_to(fill[:, None, None], blocks.shape[:2] + (1,))
            blocks = jnp.concatenate([blocks, fill], axis=2)
        rest = depth - blocks.shape[2]
        return jnp.pad(blocks, ((0, 0), (0, 0), (0, rest))).reshape(-1, nz * ny * depth)

    numbers = task_ids.astype(bf16)
    conditions = [columns_of(condition, numbers, 0)] + [
        move(columns_of(condition, numbers, dx), sizes, 2, dx) for dx in range(1, nx)
    ]
    conditions = jnp.concatenate(conditions).astype(f32)
    onehot = (conditions[:, film_rows : film_rows + 1] == jnp.arange(tasks, dtype=f32)[None]).astype(
        bf16
    )
    inside = (jnp.arange(conditions.shape[1]) % depth < film_rows)[None]
    cond_in = jnp.where(inside, conditions, 0.0) + jnp.dot(
        onehot, columns_of(task_table, None, 0), preferred_element_type=f32
    )
    embedded = mish_act(cond_in).astype(bf16)
    onehot = jnp.pad(onehot.T, ((0, -(-tasks // BLOCK) * BLOCK - tasks), (0, 0)))

    matrix = regroup_matrix()
    timed, upstream = to_time(matrix, features, out_grad, grad_mask)
    turned_a = turn(place, [timed], sizes, False)
    upstream = own_columns(upstream, width)
    residual = own_columns(timed, width)

    lines_a = after(move_lines(conv_first, sizes), timed, turned_a, embedded)
    sides_a = gather_sides(lines_a, sizes)
    film_lines = double_lines(after(film_block, timed), sizes)
    lines_b = double_lines(conv_second, sizes)
    film_lines = after(film_lines, *sides_a[0], *sides_a[1])
    film_pieces = [film_lines] + [move(film_lines, sizes, 1, r) for r in range(1, ny)]
    pieces_a = gather_corners(lines_a, sides_a, sizes)
    sides_b = gather_sides(after(lines_b, pieces_a[-2][0], pieces_a[-1][0]), sizes)

    film_parts, film_map = film_call(
        place,
        embedded.reshape(nx, samples, -1),
        film_pieces,
        sizes,
        film_rows,
    )
    film_parts = [film_parts[0]] + [
        move(after(film_parts[dx], lines_b), sizes, 2, nx - dx) for dx in range(1, nx)
    ]
    small = jnp.stack([part[samples:, : 6 * each] for part in film_parts])
    film_own = sum(part[:samples] for part in film_parts)
    film_out = in_order(around(film_own), own)
    small = in_order(around(small), own)
    small = in_order([small[:, (nx - r) % nx] for r in range(nx)], position[2])
    small = small.transpose(2, 0, 1, 3).reshape(count * shards, 6 * each)
    gain_a, shift_a, gain_b, shift_b = [
        own_columns(small[:, i * each : (i + 1) * each].reshape(1, -1), width) for i in range(4)
    ]
    bias = small[:, 4 * each : 6 * each].reshape(1, -1)
    film_out = jnp.moveaxis(film_out, 0, 1).reshape(samples, 2 * channels) + bias
    scale = own_columns(film_out[:, :channels], width)
    shifting = own_columns(film_out[:, channels:], width)

    column = pl.BlockSpec((samples, tile), lambda n, _: (0, n))
    vector = pl.BlockSpec((1, tile), lambda n, _: (0, n))
    pair = pl.BlockSpec((2, tile), lambda n, _: (0, n))
    field = pl.BlockSpec((HORIZON, samples, tile), lambda n, _: (0, 0, n))
    spreads = pl.BlockSpec((tile // GROUP, samples, GROUP), lambda n, _: (n, 0, 0))
    films = pl.BlockSpec((2, samples, tile), lambda n, _: (0, 0, n))
    fours = pl.BlockSpec((4, tile), lambda n, _: (0, n))
    low_shape = jax.ShapeDtypeStruct((HORIZON, samples, width), bf16)
    field_shape = jax.ShapeDtypeStruct((HORIZON, samples, width), f32)
    pair_shape = jax.ShapeDtypeStruct((2, width), f32)
    spread_shape = jax.ShapeDtypeStruct((width // GROUP, samples, GROUP), f32)

    unit_a, spread_a, lifted, *quarters_a = conv_call(
        first_body,
        "conv_first",
        place,
        sizes,
        False,
        [timed],
        pieces_a,
        [scale, shifting, gain_a, shift_a],
        [column, column, vector, vector],
        [field_shape, spread_shape, low_shape],
        [field, spreads, field],
        [turned_a],
    )
    pieces_b = gather_corners(lines_b, sides_b, sizes, spread_a)
    quarters_a = [quarters_a[0]] + [swap(quarters_a[r], r) for r in range(1, shards)]
    lifted = around(lifted)
    turned_b = turn(place, lifted, sizes, True)
    block_own, grad_second, sums_b, *quarters_b = conv_call(
        second_body,
        "conv_second",
        place,
        sizes,
        True,
        lifted,
        pieces_b,
        [residual, upstream, gain_b, shift_b],
        [field, field, vector, vector],
        [low_shape, low_shape, pair_shape],
        [field, field, pair],
        [turned_b],
    )
    block_all = around(block_own)
    quarters_b = [quarters_b[0]] + [swap(quarters_b[r], r) for r in range(1, shards)]

    grads_b = half_grad(lasting(7.5), turned_b, grad_second, sizes, True, 0)
    grads_b += half_grad(lasting(7.5), turned_b, grad_second, sizes, False, 1)
    grad_first, low, sums_a = back_call(
        lifted_back_body,
        "lifted_back",
        place,
        around(grad_second),
        quarters_b,
        [unit_a, spread_a, scale, gain_a, shift_a, *quarters_a[1:]],
        [field, spreads, column, vector, vector]
        + [pl.BlockSpec(memory_space=pl.ANY)] * (shards - 1),
        [
            low_shape,
            jax.ShapeDtypeStruct((2, samples, width), bf16),
            jax.ShapeDtypeStruct((4, width), f32),
        ],
        [field, films, fours],
        16,
    )
    low = in_order(around(low), own).transpose(2, 1, 0, 3).reshape(samples, 2 * channels)
    low_own = own_columns(low, film_width)
    lows = [low_own] + [move(low_own, sizes, 2, dx) for dx in range(1, nx)]
    block_all = [after(block_all[0], low_own)] + block_all[1:]
    block_out = from_time(place, matrix, block_all)
    got_near = near_got(grads_b, sizes)
    ready = lows[1:] + [block_out]
    near_left = add_near(grads_b[0], [after(part, *ready) for part in got_near[0]])
    near_right = add_near(grads_b[2], [after(part, *near_left[1]) for part in got_near[1]])
    near_b = (near_left, near_right)
    grad_first_all = around(grad_first)
    got_b = far_got(near_b, sizes)
    grads_a = half_grad(SHORT, turned_a, grad_first, sizes, True, 0, *near_left[1], *near_right[1])
    grads_a += half_grad(SHORT, turned_a, grad_first, sizes, False, 1, grads_a[0])
    got_b = tuple([after(part, grads_a[2]) for part in parts] for parts in got_b)
    whole_b = jnp.concatenate(far_sums(near_b, got_b), axis=2).astype(bf16)
    rows_b = lax.psum_scatter(
        whole_b, "dp", scatter_dimension=0, tiled=False, axis_index_groups=line_groups(sizes)
    )
    grad_conv_second = rows_b.astype(f32).reshape(conv_second.shape)
    film_keep, film_send, grad_table = film_back(
        place,
        embedded.T,
        after(jnp.concatenate(lows), whole_b),
        film_map,
        cond_in,
        onehot,
        sizes,
    )
    grad_own = back_call(
        features_back_body,
        "features_back",
        place,
        grad_first_all,
        quarters_a,
        [upstream, film_send],
        [field, pl.BlockSpec(memory_space=pl.ANY)],
        [low_shape],
        [field],
        2,
    )
    got_near = near_got(grads_a, sizes)
    near_left = add_near(grads_a[0], [after(part, *grad_own) for part in got_near[0]])
    near_right = add_near(grads_a[2], [after(part, *near_left[1]) for part in got_near[1]])
    got_a = far_got((near_left, near_right), sizes)
    film_got = [move(film_send[dy - 1], sizes, 1, dy) for dy in range(1, ny)]
    film_got = [after(part, *near_right[1]) for part in film_got]
    film_value = add_halves(film_keep, film_got)
    left = add_halves(near_left[0], [after(part, film_value[0]) for part in got_a[0]])
    ready = (left[0],)
    right = add_halves(near_right[0], [after(part, *ready) for part in got_a[1]])

    grad_all = around(grad_own[0])
    grad_all = [after(grad_all[0], right[0])] + grad_all[1:]
    grad_features = from_time(place, matrix, grad_all)
    masks = line_masks(nz)[0][::-1]
    values, film_ready = [left, right], right[0]
    for mask in masks[:-1]:
        got = [trade(value[1], sizes, 0, mask) for value in values]
        film_got = after(trade(film_value[1], sizes, 0, mask), film_ready)
        got[0] = after(got[0], grad_features, got[1], rows_b)
        values = [add_halves(value[0], [part]) for value, part in zip(values, got)]
        film_value = add_halves(film_value[0], [film_got])
        film_ready = values[1][0]

    sums = jnp.concatenate([sums_a[:2], sums_b, sums_a[2:]])
    sums = lax.dynamic_update_slice(jnp.zeros((6, channels), f32), sums, (0, own * width)).reshape(-1)
    wide = grad_table.shape[1]
    rows = -(-(tasks + -(-sums.shape[0] // wide)) // 8) * 8
    sums = jnp.pad(sums, (0, (rows - tasks) * wide - sums.shape[0])).reshape(rows - tasks, wide)
    total = sum_shards(jnp.concatenate([grad_table[:tasks], sums]), *near_left[1])
    total = sum_along(total, sizes, 0, near_right[1], [left[0]])
    total = sum_along(total, sizes, 1, [right[0]])
    totals = [total] + [after(move(total, sizes, 2, r), values[0][0]) for r in range(1, nx)]
    totals = in_order(totals, position[2])
    totals = in_order(around(totals), own)
    totals = jnp.moveaxis(totals, 0, 1).reshape(nx, rows, wide)

    grad_table = totals[:, :tasks].reshape(nx, tasks, nz * ny, depth)[..., :film_rows]
    grad_table = grad_table.transpose(1, 2, 0, 3).reshape(tasks, -1)
    sums = totals[0, tasks:]
    for x in range(1, nx):
        sums = sums + totals[x, tasks:]
    sums = sums.reshape(-1)[: 6 * channels].reshape(6, channels)

    got = [trade(value[1], sizes, 0, masks[-1]) for value in values]
    got[0] = after(got[0], got[1], grad_table, sums, grad_conv_second)
    film_got = trade(film_value[1], sizes, 0, masks[-1])
    grad_conv_first = [add_far(value[0], [part])[0] for value, part in zip(values, got)]
    grad_conv_first = jnp.concatenate(grad_conv_first, axis=1).reshape(conv_first.shape)
    grad_film_weight = add_far(film_value[0], [after(film_got, grad_table)])[0, :film_rows]
    index = me * shards + own
    small = [lax.dynamic_slice(sums[i], (index * each,), (each,)) for i in range(4)]
    grad_film_bias = lax.dynamic_slice(sums[4:].reshape(-1), (index * 2 * each,), (2 * each,))
    return (
        block_out,
        grad_features,
        grad_conv_first,
        grad_conv_second,
        grad_film_weight,
        small[0],
        small[1],
        small[2],
        small[3],
        grad_film_bias,
        grad_table,
    )


def solution(mesh):
    return jax.shard_map(
        local,
        mesh=mesh,
        in_specs=(
            P("dp", None),
            P("dp", None),
            P("dp"),
            P(None, "dp", "shard"),
            P(None, "dp", "shard"),
            P("dp", "shard"),
            P(("dp", "shard")),
            P(("dp", "shard")),
            P(("dp", "shard")),
            P(("dp", "shard")),
            P(("dp", "shard")),
            P(),
            P("dp", None),
            P("dp"),
        ),
        out_specs=(
            P("dp", None),
            P("dp", None),
            P(None, "dp", "shard"),
            P(None, "dp", "shard"),
            P("dp", "shard"),
            P(("dp", "shard")),
            P(("dp", "shard")),
            P(("dp", "shard")),
            P(("dp", "shard")),
            P(("dp", "shard")),
            P(),
        ),
        check_vma=False,
    )
```

```python
import functools

import jax
import jax.numpy as jnp
from jax import lax
from jax.experimental import pallas as pl
from jax.experimental.pallas import tpu as pltpu
from jax.sharding import PartitionSpec as P

KERNEL = 5
HALF = KERNEL // 2
HORIZON = 16
GROUP = 128
EPSILON = 1e-05
BLOCK = 16
VMEM_LIMIT = 48 * 1024 * 1024
SHORT = pl.CostEstimate(flops=1, bytes_accessed=1, transcendentals=0)


def lasting(microseconds):
    flops = int(microseconds * 5.175e+08)
    return pl.CostEstimate(flops=flops, bytes_accessed=1, transcendentals=0)


f32 = jnp.float32
bf16 = jnp.bfloat16


def mish_parts(v):
    w = jnp.exp(jnp.minimum(v, 20.0))
    n = w * (w + 2.0)
    r = 1.0 / (n + 2.0)
    return w, r, n * r


def mish_act(v):
    return v * mish_parts(v)[2]


def mish_slope(v):
    w, r, t = mish_parts(v)
    return t + v * (4.0 * w * (1.0 + w)) * (r * r)


def digits(count):
    bits = count.bit_length() - 1
    small = bits // 3
    return (1 << (bits - 2 * small), 1 << small, 1 << small)


def coordinates(index, sizes):
    _, ny, nx = sizes
    return (index // (ny * nx), (index // nx) % ny, index % nx)


def flat(position, sizes):
    _, ny, nx = sizes
    return (position[0] * ny + position[1]) * nx + position[2]


def move(value, sizes, axis, by):
    count = sizes[0] * sizes[1] * sizes[2]
    pairs = []
    for source in range(count):
        position = list(coordinates(source, sizes))
        position[axis] = (position[axis] + by) % sizes[axis]
        pairs.append((source, flat(position, sizes)))
    return lax.ppermute(value, "dp", pairs)


def swap(value, by):
    count = lax.axis_size("shard")
    return lax.ppermute(value, "shard", [(i, (i + by) % count) for i in range(count)])


def around(value):
    return [value] + [swap(value, r) for r in range(1, lax.axis_size("shard"))]


def in_order(parts, own):
    count = len(parts)
    if count == 2:
        mine = own == 0
        return jnp.stack([jnp.where(mine, parts[0], parts[1]), jnp.where(mine, parts[1], parts[0])])
    return jnp.stack(parts)[(own - jnp.arange(count)) % count]


def trade(value, sizes, axis, mask):
    count = sizes[0] * sizes[1] * sizes[2]
    pairs = []
    for source in range(count):
        position = list(coordinates(source, sizes))
        position[axis] ^= mask
        pairs.append((source, flat(position, sizes)))
    return lax.ppermute(value, "dp", pairs)


def line_groups(sizes):
    nz, ny, nx = sizes
    return [[flat((z, y, x), sizes) for z in range(nz)] for y in range(ny) for x in range(nx)]


def move_lines(own, sizes):
    return jnp.stack([own] + [move(own, sizes, 0, r) for r in range(1, sizes[0])])


def line_masks(count):
    masks = [1 << bit for bit in reversed(range(count.bit_length() - 1))]
    order = [0]
    for mask in masks:
        order = order + [other ^ mask for other in order]
    return masks, order


def line_place(other, count):
    bits = count.bit_length() - 1
    return sum(((other >> bit) & 1) << (bits - 1 - bit) for bit in range(bits))


def double_lines(own, sizes):
    lines, steps = own[None], []
    for mask in line_masks(sizes[0])[0]:
        steps.append(trade(lines, sizes, 0, mask))
        lines = jnp.concatenate([lines, steps[-1]])
    return lines, steps


def gather_sides(lines, sizes):
    return (
        [move(lines, sizes, 2, r) for r in range(1, sizes[2])],
        [move(lines, sizes, 1, r) for r in range(1, sizes[1])],
    )


def gather_corners(lines, sides, sizes, *ready):
    by_x, by_y = sides
    half = lines.shape[-1] // 2
    pieces = [(lines, 0, 0, 0)]
    pieces += [(part, 0, dx + 1, 0) for dx, part in enumerate(by_x)]
    pieces += [(part, 0, 0, dy + 1) for dy, part in enumerate(by_y)]
    lefts = [after(part[..., :half], *ready) for part in by_x]
    rights = [after(part[..., half:], *ready) for part in by_y]
    for dx in range(1, sizes[2]):
        for dy in range(1, sizes[1]):
            pieces.append((move(rights[dy - 1], sizes, 2, dx), half, dx, dy))
            pieces.append((move(lefts[dx - 1], sizes, 1, dy), 0, dx, dy))
    return pieces


def scatter_step(parts, sizes, axis):
    return [move(part, sizes, axis, r + 1) for r, part in enumerate(parts)]


def add_near(keep, got):
    sums = [
        keep[r].astype(f32) + sum(part[r].astype(f32) for part in got) for r in range(keep.shape[0])
    ]
    return sums[0], [part.astype(bf16) for part in sums[1:]]


def add_far(own, got):
    for part in got:
        own = own + part.astype(f32)
    return own


def add_halves(own, got):
    half = own.shape[0] // 2
    stay = add_far(own[:half], [part[:half] for part in got])
    return stay, add_far(own[half:], [part[half:] for part in got]).astype(bf16)


def sum_shards(value, *ready):
    shards = lax.axis_size("shard")
    own = lax.axis_index("shard")
    rows = value.shape[0] // shards

    def part(r):
        return lax.dynamic_slice_in_dim(value, (own + r) % shards * rows, rows, 0)

    total = part(0)
    for r in range(1, shards):
        total = total + after(swap(part(r), r), *ready)
    return total


def sum_along(total, sizes, axis, *ready):
    steps = sizes[axis].bit_length() - 1
    for step in range(steps):
        got = trade(total, sizes, axis, 1 << step)
        total = total + after(got, *ready[min(step, len(ready) - 1)])
    return total


def nothing(*_):
    pass


def after(value, *ready):
    anywhere = pl.BlockSpec(memory_space=pl.ANY)
    return pl.pallas_call(
        nothing,
        in_specs=[anywhere] * (1 + len(ready)),
        out_specs=anywhere,
        out_shape=jax.ShapeDtypeStruct(value.shape, value.dtype),
        input_output_aliases={0: 0},
        cost_estimate=SHORT,
        name="after",
    )(value, *ready)


def copy_body(source, *refs):
    refs[-1][...] = source[...]


def copied(value, *ready):
    whole = pl.BlockSpec(memory_space=pltpu.VMEM)
    return pl.pallas_call(
        copy_body,
        in_specs=[whole] + [pl.BlockSpec(memory_space=pl.ANY)] * len(ready),
        out_specs=whole,
        out_shape=jax.ShapeDtypeStruct(value.shape, value.dtype),
        cost_estimate=SHORT,
        name="copied",
    )(value, *ready)


def params(dims):
    return pltpu.CompilerParams(
        dimension_semantics=("arbitrary",) * dims, vmem_limit_bytes=VMEM_LIMIT
    )


def regroup_matrix():
    side = BLOCK * HORIZON
    row = lax.broadcasted_iota(jnp.int32, (side, side), 0)
    column = lax.broadcasted_iota(jnp.int32, (side, side), 1)
    return (column == (row % BLOCK) * HORIZON + row // BLOCK).astype(bf16)


def to_time_body(matrix, features_ref, grads_ref, mask_ref, features_out, grads_out):
    channels = features_ref.shape[1]
    moved = jnp.dot(matrix[...], features_ref[...], preferred_element_type=f32)
    features_out[...] = moved.astype(bf16).reshape(HORIZON, BLOCK, channels)
    masked = matrix[...] * mask_ref[0].astype(bf16)
    moved = jnp.dot(masked, grads_ref[...], preferred_element_type=f32)
    grads_out[...] = moved.astype(bf16).reshape(HORIZON, BLOCK, channels)


def to_time(matrix, features, grads, mask):
    frames, channels = features.shape
    samples = frames // HORIZON
    steps = samples // BLOCK
    side = BLOCK * HORIZON
    square = pl.BlockSpec((side, side), lambda b: (0, 0))
    rows = pl.BlockSpec((side, channels), lambda b: (b, 0))
    out = pl.BlockSpec((HORIZON, BLOCK, channels), lambda b: (0, b, 0))
    shape = jax.ShapeDtypeStruct((HORIZON, samples, channels), bf16)
    return pl.pallas_call(
        to_time_body,
        grid=(steps,),
        in_specs=[square, rows, rows, pl.BlockSpec((1, 1, side), lambda b: (b, 0, 0))],
        out_specs=[out, out],
        out_shape=[shape, shape],
        compiler_params=params(1),
        cost_estimate=lasting(7),
        name="to_time",
    )(matrix, features, grads, mask.reshape(steps, 1, side))


def from_time_body(count, place_ref, matrix, *refs):
    pieces, out = refs[:-1], refs[-1]
    width = pieces[0].shape[2]
    moved = []
    for piece in pieces:
        rows = piece[...].reshape(HORIZON * BLOCK, width)
        moved.append(jnp.dot(matrix[...], rows, preferred_element_type=f32).astype(bf16))
    for own in range(count):

        @pl.when(place_ref[3] == own)
        def _(own=own):
            for r, rows in enumerate(moved):
                column = (own - r) % count * width
                out[:, column : column + width] = rows


def from_time(place, matrix, pieces):
    horizon, samples, width = pieces[0].shape
    count = len(pieces)
    channels = width * count
    return pl.pallas_call(
        functools.partial(from_time_body, count),
        grid_spec=pltpu.PrefetchScalarGridSpec(
            num_scalar_prefetch=1,
            grid=(samples // BLOCK,),
            in_specs=[pl.BlockSpec(matrix.shape, lambda b, _: (0, 0))]
            + [pl.BlockSpec((horizon, BLOCK, width), lambda b, _: (0, b, 0))] * count,
            out_specs=pl.BlockSpec((horizon * BLOCK, channels), lambda b, _: (b, 0)),
        ),
        out_shape=jax.ShapeDtypeStruct((horizon * samples, channels), bf16),
        compiler_params=params(1),
        cost_estimate=SHORT,
        name="from_time",
    )(place, matrix, *pieces)


def turn_body(sizes, rows, ordered, place_ref, *refs):
    pieces, out = refs[:-1], refs[-1]
    count, width = len(pieces), pieces[0].shape[2]
    nz, ny, nx = sizes
    for r, piece in enumerate(pieces):
        shard = (place_ref[3] + count - r) % count
        for tile in range(width // GROUP):
            block = piece[:, :, tile * GROUP : (tile + 1) * GROUP]
            turned = block.reshape(-1, GROUP).T
            for j in range(GROUP // rows):
                owner = shard * (width // rows) + tile * (GROUP // rows) + j
                oz, oy, ox = coordinates(owner, sizes)
                dz = oz if ordered else line_place(oz ^ place_ref[0], nz)
                dy = (oy - place_ref[1] + ny) % ny
                dx = (ox - place_ref[2] + nx) % nx
                out[pl.ds((dx * ny + dy) * nz + dz, 1)] = turned[j * rows : (j + 1) * rows][None]


def turn(place, pieces, sizes, ordered):
    horizon, samples, width = pieces[0].shape
    count = sizes[0] * sizes[1] * sizes[2]
    rows = len(pieces) * width // count
    return pl.pallas_call(
        functools.partial(turn_body, sizes, rows, ordered),
        in_specs=[pl.BlockSpec(memory_space=pltpu.SMEM)]
        + [pl.BlockSpec(memory_space=pltpu.VMEM)] * len(pieces),
        out_specs=pl.BlockSpec(memory_space=pltpu.VMEM),
        out_shape=jax.ShapeDtypeStruct((count, rows, horizon * samples), bf16),
        compiler_params=pltpu.CompilerParams(vmem_limit_bytes=VMEM_LIMIT),
        cost_estimate=lasting(3.5),
        name="turn",
    )(place, *pieces)


def zero_ends(padded):
    steps = padded.shape[0]
    zeros = jnp.zeros((HALF,) + padded.shape[1:], padded.dtype)
    padded[:HALF] = zeros
    padded[steps - HALF :] = zeros


def weight_copies(sizes, paired, place_ref, pieces, where, weight, sems):
    nz, ny, nx = sizes
    copies = []
    for piece, (column, dx, dy) in zip(pieces, where):
        _, _, rows, width = piece.shape
        for r in range(nz):
            z = place_ref[0] ^ line_masks(nz)[1][r] if paired else (place_ref[0] - r + nz) % nz
            owner = flat((z, (place_ref[1] - dy + ny) % ny, (place_ref[2] - dx + nx) % nx), sizes)
            at = pl.ds(pl.multiple_of(owner * rows, rows), rows)
            copies.append(
                pltpu.make_async_copy(
                    piece.at[r], weight.at[:, at, pl.ds(column, width)], sems.at[len(copies)]
                )
            )
    return copies


def column_copies(place_ref, pieces, target, sems, first_sem):
    count, width = len(pieces), pieces[0].shape[-1]
    copies = []
    for r, piece in enumerate(pieces):
        column = pl.multiple_of(((place_ref[3] + count - r) % count) * width, width)
        copies.append(
            pltpu.make_async_copy(
                piece, target.at[..., pl.ds(column, width)], sems.at[first_sem + r]
            )
        )
    return copies


def group_mean(value):
    return jnp.sum(jnp.sum(value, axis=0), axis=1, keepdims=True)[None] / (HORIZON * GROUP)


def norm_of(a):
    centre = a - group_mean(a)
    spread = lax.rsqrt(group_mean(centre * centre) + EPSILON)
    return centre * spread, spread


def norm_back(h, unit, spread):
    return spread * (h - group_mean(h) - unit * group_mean(h * unit))


def conv_blocks(padded, weight_of, order, body):
    samples, channels = padded.shape[1:]
    for b in range(samples // BLOCK):
        at = slice(b * BLOCK, (b + 1) * BLOCK)
        total = None
        for k in range(KERNEL):
            start = order(k)
            rows = padded[start : start + HORIZON, at, :].reshape(HORIZON * BLOCK, channels)
            part = weight_of(rows, k)
            total = part if total is None else total + part
        body(at, total.reshape(HORIZON, BLOCK, total.shape[1]))


def conv_front(sizes, paired, where, place_ref, inputs, pieces, quarters, padded, weight, sems):
    n = pl.program_id(0)
    count = len(quarters)
    height = weight.shape[2]
    base = len(pieces) * sizes[0] + len(inputs)

    def out_copies():
        return [
            pltpu.make_async_copy(
                weight.at[
                    :, pl.ds(pl.multiple_of(((place_ref[3] + r) % count) * height, height), height), :
                ],
                quarter,
                sems.at[base + r],
            )
            for r, quarter in enumerate(quarters)
        ]

    @pl.when(n == 0)
    def _():
        copies = weight_copies(sizes, paired, place_ref, pieces, where, weight, sems)
        copies += column_copies(
            place_ref, inputs, padded.at[pl.ds(HALF, HORIZON)], sems, len(copies)
        )
        for copy in copies:
            copy.start()
        zero_ends(padded)
        for copy in copies:
            copy.wait()
        for copy in out_copies():
            copy.start()

    def finish():
        @pl.when(n == pl.num_programs(0) - 1)
        def _():
            for copy in out_copies():
                copy.wait()

    return finish


def conv_weight(weight, tile):
    column = pl.ds(pl.multiple_of(pl.program_id(0) * tile, tile), tile)

    def apply(rows, k):
        return jnp.dot(rows, weight[k, :, column], preferred_element_type=f32)

    return apply


def groups_of(width):
    return [(g, slice(g * GROUP, (g + 1) * GROUP)) for g in range(width // GROUP)]


def first_body(sizes, paired, where, shards, waits, place_ref, *refs):
    inputs, refs = refs[:1], refs[1:]
    pieces, refs = refs[: len(where)], refs[len(where) :]
    scale, shifting, gain, shift = refs[:4]
    refs = refs[4 + waits :]
    unit_out, spread_out, lifted_out = refs[:3]
    quarters = refs[3 : 3 + shards]
    padded, weight, sems = refs[3 + shards :]
    tile = unit_out.shape[2]
    finish = conv_front(
        sizes, paired, where, place_ref, inputs, pieces, quarters, padded, weight, sems
    )

    def body(at, a):
        for group, lanes in groups_of(tile):
            unit, spread = norm_of(a[:, :, lanes])
            unit_out[:, at, lanes] = unit
            spread_out[group, at, :] = jnp.broadcast_to(spread[0], (BLOCK, GROUP))
            mixed = mish_act(unit * gain[:, lanes][None] + shift[:, lanes][None])
            lifted = scale[at, lanes][None] * mixed + shifting[at, lanes][None]
            lifted_out[:, at, lanes] = lifted.astype(bf16)

    conv_blocks(padded, conv_weight(weight, tile), lambda k: k, body)
    finish()


def second_body(sizes, paired, where, shards, waits, place_ref, *refs):
    inputs, refs = refs[:shards], refs[shards:]
    pieces, refs = refs[: len(where)], refs[len(where) :]
    features, upstream, gain, shift = refs[:4]
    refs = refs[4 + waits :]
    block_out, grad_out, sums_out = refs[:3]
    quarters = refs[3 : 3 + shards]
    padded, weight, sems = refs[3 + shards :]
    tile = block_out.shape[2]
    finish = conv_front(
        sizes, paired, where, place_ref, inputs, pieces, quarters, padded, weight, sems
    )
    sums_out[...] = jnp.zeros_like(sums_out)

    def body(at, a):
        for _, lanes in groups_of(tile):
            unit, spread = norm_of(a[:, :, lanes])
            gain_here = gain[:, lanes][None]
            normed = unit * gain_here + shift[:, lanes][None]
            w, r, t = mish_parts(normed)
            block = features[:, at, lanes].astype(f32) + normed * t
            block_out[:, at, lanes] = block.astype(bf16)
            slope = t + normed * (4.0 * w * (1.0 + w)) * (r * r)
            grad = upstream[:, at, lanes].astype(f32) * slope
            sums_out[0:1, lanes] += jnp.sum(jnp.sum(grad * unit, axis=0), axis=0, keepdims=True)
            sums_out[1:2, lanes] += jnp.sum(jnp.sum(grad, axis=0), axis=0, keepdims=True)
            grad_out[:, at, lanes] = norm_back(grad * gain_here, unit, spread).astype(bf16)

    conv_blocks(padded, conv_weight(weight, tile), lambda k: k, body)
    finish()


def conv_call(
    body, name, place, sizes, paired, inputs, pieces, extras, extra_specs, outs, out_specs, ready
):
    shards = lax.axis_size("shard")
    _, samples, depth = inputs[0].shape
    count = len(inputs)
    channels = count * depth
    arrays = [piece[0] for piece in pieces]
    where = tuple(piece[1:] for piece in pieces)
    width = arrays[0].shape[3]
    tile = min(256, width)
    quarter = jax.ShapeDtypeStruct((KERNEL, width, width), bf16)
    anywhere = pl.BlockSpec(memory_space=pl.ANY)
    return pl.pallas_call(
        functools.partial(body, sizes, paired, where, shards, len(ready)),
        grid_spec=pltpu.PrefetchScalarGridSpec(
            num_scalar_prefetch=1,
            grid=(width // tile,),
            in_specs=[anywhere] * (count + len(arrays)) + extra_specs + [anywhere] * len(ready),
            out_specs=out_specs + [anywhere] * shards,
            scratch_shapes=[
                pltpu.VMEM((HORIZON + 2 * HALF, samples, channels), bf16),
                pltpu.VMEM((KERNEL, channels, width), bf16),
                pltpu.SemaphoreType.DMA((len(arrays) * sizes[0] + count + shards,)),
            ],
        ),
        out_shape=outs + [quarter] * shards,
        compiler_params=params(1),
        cost_estimate=lasting(18),
        name=name,
    )(place, *inputs, *arrays, *extras, *ready)


def back_front(place_ref, grads, quarters, padded, weight, sems):
    @pl.when(pl.program_id(0) == 0)
    def _():
        copies = column_copies(place_ref, grads, padded.at[pl.ds(HALF, HORIZON)], sems, 0)
        copies += column_copies(place_ref, quarters, weight, sems, len(copies))
        for copy in copies:
            copy.start()
        zero_ends(padded)
        for copy in copies:
            copy.wait()


def back_weight(weight, tile):
    at = pl.ds(pl.multiple_of(pl.program_id(0) * tile, tile), tile)

    def apply(rows, k):
        return lax.dot_general(
            rows, weight[k, at, :], (((1,), (1,)), ((), ())), preferred_element_type=f32
        )

    return apply


def lifted_back_body(shards, place_ref, *refs):
    grads, quarters, refs = refs[:shards], refs[shards : 2 * shards], refs[2 * shards :]
    unit_in, spread_in, scale, gain, shift = refs[:5]
    grad_out, film_out, sums_out, padded, weight, sems = refs[-6:]
    tile = unit_in.shape[2]
    back_front(place_ref, grads, quarters, padded, weight, sems)
    sums_out[...] = jnp.zeros_like(sums_out)

    def body(at, a):
        for group, lanes in groups_of(tile):
            grad_lifted = a[:, :, lanes]
            unit = unit_in[:, at, lanes]
            spread = spread_in[group, at, :][None]
            gain_here = gain[:, lanes][None]
            normed = unit * gain_here + shift[:, lanes][None]
            w, r, t = mish_parts(normed)
            for row, film in enumerate((grad_lifted * (normed * t), grad_lifted)):
                film = jnp.sum(film, axis=0)
                sums_out[2 + row : 3 + row, lanes] += jnp.sum(film, axis=0, keepdims=True)
                film_out[row, at, lanes] = film.astype(bf16)
            slope = t + normed * (4.0 * w * (1.0 + w)) * (r * r)
            grad = grad_lifted * scale[at, lanes][None] * slope
            sums_out[0:1, lanes] += jnp.sum(jnp.sum(grad * unit, axis=0), axis=0, keepdims=True)
            sums_out[1:2, lanes] += jnp.sum(jnp.sum(grad, axis=0), axis=0, keepdims=True)
            grad_out[:, at, lanes] = norm_back(grad * gain_here, unit, spread).astype(bf16)

    conv_blocks(padded, back_weight(weight, tile), lambda k: KERNEL - 1 - k, body)


def features_back_body(shards, place_ref, *refs):
    grads, quarters, refs = refs[:shards], refs[shards : 2 * shards], refs[2 * shards :]
    upstream = refs[0]
    grad_out, padded, weight, sems = refs[-4:]
    tile = upstream.shape[2]
    back_front(place_ref, grads, quarters, padded, weight, sems)

    def body(at, a):
        grad_out[:, at, :] = (a + upstream[:, at, :].astype(f32)).astype(bf16)

    conv_blocks(padded, back_weight(weight, tile), lambda k: KERNEL - 1 - k, body)


def back_call(
    body, name, place, grads, quarters, extras, extra_specs, outs, out_specs, estimate
):
    shards = len(grads)
    _, samples, width = grads[0].shape
    channels = width * shards
    tile = min(256, width)
    anywhere = pl.BlockSpec(memory_space=pl.ANY)
    return pl.pallas_call(
        functools.partial(body, shards),
        grid_spec=pltpu.PrefetchScalarGridSpec(
            num_scalar_prefetch=1,
            grid=(width // tile,),
            in_specs=[anywhere] * (2 * shards) + extra_specs,
            out_specs=out_specs,
            scratch_shapes=[
                pltpu.VMEM((HORIZON + 2 * HALF, samples, channels), bf16),
                pltpu.VMEM((KERNEL, width, channels), bf16),
                pltpu.SemaphoreType.DMA((2 * shards,)),
            ],
        ),
        out_shape=outs,
        compiler_params=params(1),
        cost_estimate=lasting(estimate),
        name=name,
    )(place, *grads, *quarters, *extras)


def half_grad_body(sizes, along_y, half, turned, grads, *refs):
    nz, ny, nx = sizes
    keep, send, padded = refs[-3:]
    rows, frames = turned.shape[2:]
    width = keep.shape[3]
    step = pl.program_id(0)
    away = step // (nx if along_y else ny) + 1
    stays = away == (ny if along_y else nx)

    @pl.when(step == 0)
    def _():
        zero_ends(padded)
        padded[HALF : HALF + HORIZON] = grads[:, :, half * width : (half + 1) * width]

    lhs = turned[0].reshape(nz * rows, frames)

    def store(out):
        for k in range(KERNEL):
            at = KERNEL - 1 - k
            rhs = padded[at : at + HORIZON].reshape(frames, width)
            part = jnp.dot(lhs, rhs, preferred_element_type=f32).reshape(nz, rows, width)
            out[:, k * rows : (k + 1) * rows, :] = part.astype(out.dtype)

    @pl.when(stays)
    def _():
        store(keep.at[0])

    @pl.when(jnp.logical_not(stays))
    def _():
        store(send.at[0, 0])


def half_grad(estimate, turned, grads, sizes, along_y, half, *ready):
    nz, ny, nx = sizes
    near, far = (ny, nx) if along_y else (nx, ny)
    _, rows, frames = turned.shape
    _, samples, width = grads.shape
    height, width = KERNEL * rows, width // 2
    turned = turned.reshape(nx * ny, nz, rows, frames)
    leaving = (near - 1) * far

    def source(s):
        away, across = (s // far + 1) % near, s % far
        dx, dy = (across, away) if along_y else (away, across)
        return (dx * ny + dy, 0, 0, 0)

    def kept(s):
        return (jnp.maximum(s - leaving, 0), 0, 0, 0)

    def sent(s):
        last = jnp.minimum(s, leaving - 1)
        return (last // far, last % far, 0, 0, 0)

    return pl.pallas_call(
        functools.partial(half_grad_body, sizes, along_y, half),
        grid=(nx * ny,),
        in_specs=[
            pl.BlockSpec((1, nz, rows, frames), source),
            pl.BlockSpec(grads.shape, lambda s: (0, 0, 0)),
        ]
        + [pl.BlockSpec(memory_space=pl.ANY)] * len(ready),
        out_specs=[
            pl.BlockSpec((1, nz, height, width), kept),
            pl.BlockSpec((1, 1, nz, height, width), sent),
        ],
        out_shape=[
            jax.ShapeDtypeStruct((far, nz, height, width), bf16),
            jax.ShapeDtypeStruct((near - 1, far, nz, height, width), bf16),
        ],
        scratch_shapes=[pltpu.VMEM((HORIZON + 2 * HALF, samples, width), bf16)],
        compiler_params=params(1),
        cost_estimate=estimate,
        name="half_grad",
    )(turned, grads, *ready)


def near_got(grads, sizes):
    _, send_left, _, send_right = grads
    left = scatter_step([send_left[r] for r in range(sizes[1] - 1)], sizes, 1)
    right = scatter_step([send_right[r] for r in range(sizes[2] - 1)], sizes, 2)
    return left, right


def near_sums(grads, got, *ready):
    keep_left, _, keep_right, _ = grads
    left = add_near(keep_left, [after(part, *ready) for part in got[0]])
    return left, add_near(keep_right, [after(part, *ready) for part in got[1]])


def far_got(near, sizes):
    (_, left), (_, right) = near
    return scatter_step(left, sizes, 2), scatter_step(right, sizes, 1)


def far_sums(near, got):
    (left, _), (right, _) = near
    return add_far(left, got[0]), add_far(right, got[1])


def film_body(sizes, rows, place_ref, embedded, *refs):
    nz, ny, _ = sizes
    pieces = refs[:ny]
    out, weight_out, weight, sems = refs[ny:]
    parts, samples, deep = embedded.shape
    depth = deep // (nz * ny)
    copies = []
    for dy, piece in enumerate(pieces):
        for z in range(nz):
            there = place_ref[0] ^ line_masks(nz)[1][z]
            owner = there * ny + (place_ref[1] - dy + ny) % ny
            at = pl.ds(pl.multiple_of(owner * depth, BLOCK), depth)
            copies.append(
                pltpu.make_async_copy(piece.at[z], weight.at[at, :], sems.at[len(copies)])
            )
    for copy in copies:
        copy.start()
    for copy in copies:
        copy.wait()
    back = pltpu.make_async_copy(weight, weight_out, sems.at[len(copies)])
    back.start()
    for part in range(parts):
        out[part, :samples, :] = jnp.dot(
            embedded[part], weight[...], preferred_element_type=f32
        )
    edge = rows // BLOCK * BLOCK
    for owner in range(nz * ny):
        block = weight[owner * depth + edge : owner * depth + edge + BLOCK, :].astype(f32)
        for part in range(parts):
            at = samples + owner
            out[part, at : at + 1, :] = block[rows - edge : rows - edge + 1, :]
    back.wait()


def film_call(place, embedded, pieces, sizes, rows):
    nz, ny, nx = sizes
    _, samples, deep = embedded.shape
    width = pieces[0].shape[2]
    anywhere = pl.BlockSpec(memory_space=pl.ANY)
    whole = pl.BlockSpec(memory_space=pltpu.VMEM)
    return pl.pallas_call(
        functools.partial(film_body, sizes, rows),
        in_specs=[pl.BlockSpec(memory_space=pltpu.SMEM), whole] + [anywhere] * ny,
        out_specs=[whole, anywhere],
        out_shape=[
            jax.ShapeDtypeStruct((nx, samples + nz * ny, width), f32),
            jax.ShapeDtypeStruct((deep, width), bf16),
        ],
        scratch_shapes=[
            pltpu.VMEM((deep, width), bf16),
            pltpu.SemaphoreType.DMA((nz * ny + 1,)),
        ],
        compiler_params=pltpu.CompilerParams(vmem_limit_bytes=VMEM_LIMIT),
        cost_estimate=lasting(3),
        name="film",
    )(place, embedded, *pieces)


def film_back_body(sizes, place_ref, turned, weight, cond_in, onehot, *refs):
    nz, ny, nx = sizes
    keep, send, table = refs[-3:]
    depth = turned.shape[0] // (nz * ny)
    low = [jnp.concatenate([part[j] for j in range(part.shape[0])], axis=1) for part in refs[:nx]]
    low = jnp.concatenate(low)
    for dy in range(ny):
        for r in range(nz):
            owner = (place_ref[0] ^ line_masks(nz)[1][r]) * ny + (place_ref[1] + dy) % ny
            at = pl.ds(pl.multiple_of(owner * depth, BLOCK), depth)
            part = jnp.dot(turned[at, :], low, preferred_element_type=f32)
            if dy == 0:
                keep[r] = part
            else:
                send[dy - 1, r] = part.astype(bf16)
    grad = lax.dot_general(
        low, weight[...], (((1,), (1,)), ((), ())), preferred_element_type=f32
    )
    rest = grad * mish_slope(cond_in[...])
    total = jnp.zeros(table.shape, f32)
    for _ in range(3):
        part = rest.astype(bf16)
        rest = rest - part.astype(f32)
        total = total + jnp.dot(onehot[...], part, preferred_element_type=f32)
    table[...] = total


def film_back(place, turned, lows, weight, cond_in, onehot, sizes, *ready):
    nz, ny, _ = sizes
    deep, width = weight.shape
    depth = deep // (nz * ny)
    whole = pl.BlockSpec(memory_space=pltpu.VMEM)
    return pl.pallas_call(
        functools.partial(film_back_body, sizes),
        in_specs=[pl.BlockSpec(memory_space=pltpu.SMEM)]
        + [whole] * (4 + len(lows))
        + [pl.BlockSpec(memory_space=pl.ANY)] * len(ready),
        out_specs=[whole] * 3,
        out_shape=[
            jax.ShapeDtypeStruct((nz, depth, width), f32),
            jax.ShapeDtypeStruct((ny - 1, nz, depth, width), bf16),
            jax.ShapeDtypeStruct((onehot.shape[0], deep), f32),
        ],
        compiler_params=pltpu.CompilerParams(vmem_limit_bytes=VMEM_LIMIT),
        cost_estimate=lasting(2.5),
        name="film_back",
    )(place, turned, weight, cond_in, onehot, *lows, *ready)


def local(
    features,
    condition,
    task_ids,
    conv_first,
    conv_second,
    film_weight,
    norm_gain_first,
    norm_shift_first,
    norm_gain_second,
    norm_shift_second,
    film_bias,
    task_table,
    out_grad,
    grad_mask,
):
    count, shards = lax.axis_size("dp"), lax.axis_size("shard")
    sizes = digits(count)
    nz, ny, nx = sizes
    me, own = lax.axis_index("dp"), lax.axis_index("shard")
    position = coordinates(me, sizes)
    place = jnp.stack([position[0], position[1], position[2], own]).astype(jnp.int32)
    samples = condition.shape[0]
    channels = features.shape[1]
    width = channels // shards
    tile = min(256, width)
    film_rows, film_width = film_weight.shape

    def own_columns(value, each):
        return lax.dynamic_slice_in_dim(value, own * each, each, value.ndim - 1)

    each = norm_gain_first.shape[0]
    tasks = task_table.shape[0]
    depth = -(-(film_rows + 1) // BLOCK) * BLOCK
    vectors = jnp.concatenate(
        [norm_gain_first, norm_shift_first, norm_gain_second, norm_shift_second, film_bias]
    )
    vectors = jnp.pad(vectors, (0, film_width - vectors.shape[0]))
    film_block = jnp.concatenate(
        [
            film_weight,
            vectors[None],
            jnp.zeros((depth - film_rows - 1, film_width), bf16),
        ]
    )

    def columns_of(value, fill, dx):
        blocks = value.reshape(-1, nz * ny, nx, film_rows)
        blocks = lax.dynamic_index_in_dim(blocks, (position[2] + dx) % nx, 2, keepdims=False)
        if fill is not None:
            fill = jnp.broadcast_to(fill[:, None, None], blocks.shape[:2] + (1,))
            blocks = jnp.concatenate([blocks, fill], axis=2)
        rest = depth - blocks.shape[2]
        return jnp.pad(blocks, ((0, 0), (0, 0), (0, rest))).reshape(-1, nz * ny * depth)

    numbers = task_ids.astype(bf16)
    conditions = [columns_of(condition, numbers, 0)] + [
        move(columns_of(condition, numbers, dx), sizes, 2, dx) for dx in range(1, nx)
    ]
    conditions = jnp.concatenate(conditions).astype(f32)
    onehot = (conditions[:, film_rows : film_rows + 1] == jnp.arange(tasks, dtype=f32)[None]).astype(
        bf16
    )
    inside = (jnp.arange(conditions.shape[1]) % depth < film_rows)[None]
    cond_in = jnp.where(inside, conditions, 0.0) + jnp.dot(
        onehot, columns_of(task_table, None, 0), preferred_element_type=f32
    )
    embedded = mish_act(cond_in).astype(bf16)
    onehot = jnp.pad(onehot.T, ((0, -(-tasks // BLOCK) * BLOCK - tasks), (0, 0)))

    matrix = regroup_matrix()
    timed, upstream = to_time(matrix, features, out_grad, grad_mask)
    turned_a = turn(place, [timed], sizes, False)
    upstream = own_columns(upstream, width)
    residual = own_columns(timed, width)

    lines_a = after(move_lines(conv_first, sizes), timed, turned_a, embedded)
    sides_a = gather_sides(lines_a, sizes)
    film_lines, film_steps = double_lines(after(film_block, timed), sizes)
    lines_b = double_lines(copied(conv_second, *film_steps[:1]), sizes)[0]
    film_lines = after(film_lines, *sides_a[0], *sides_a[1])
    film_pieces = [film_lines] + [move(film_lines, sizes, 1, r) for r in range(1, ny)]
    pieces_a = gather_corners(lines_a, sides_a, sizes)
    sides_b = gather_sides(after(lines_b, pieces_a[-2][0], pieces_a[-1][0]), sizes)

    film_parts, film_map = film_call(
        place,
        embedded.reshape(nx, samples, -1),
        film_pieces,
        sizes,
        film_rows,
    )
    film_parts = [film_parts[0]] + [
        move(after(film_parts[dx], lines_b), sizes, 2, nx - dx) for dx in range(1, nx)
    ]
    small = jnp.stack([part[samples:, : 6 * each] for part in film_parts])
    film_own = sum(part[:samples] for part in film_parts)
    film_out = in_order(around(film_own), own)
    small = in_order(around(small), own)
    small = in_order([small[:, (nx - r) % nx] for r in range(nx)], position[2])
    small = small.transpose(2, 0, 1, 3).reshape(count * shards, 6 * each)
    gain_a, shift_a, gain_b, shift_b = [
        own_columns(small[:, i * each : (i + 1) * each].reshape(1, -1), width) for i in range(4)
    ]
    bias = small[:, 4 * each : 6 * each].reshape(1, -1)
    film_out = jnp.moveaxis(film_out, 0, 1).reshape(samples, 2 * channels) + bias
    scale = own_columns(film_out[:, :channels], width)
    shifting = own_columns(film_out[:, channels:], width)

    column = pl.BlockSpec((samples, tile), lambda n, _: (0, n))
    vector = pl.BlockSpec((1, tile), lambda n, _: (0, n))
    pair = pl.BlockSpec((2, tile), lambda n, _: (0, n))
    field = pl.BlockSpec((HORIZON, samples, tile), lambda n, _: (0, 0, n))
    spreads = pl.BlockSpec((tile // GROUP, samples, GROUP), lambda n, _: (n, 0, 0))
    films = pl.BlockSpec((2, samples, tile), lambda n, _: (0, 0, n))
    fours = pl.BlockSpec((4, tile), lambda n, _: (0, n))
    low_shape = jax.ShapeDtypeStruct((HORIZON, samples, width), bf16)
    field_shape = jax.ShapeDtypeStruct((HORIZON, samples, width), f32)
    pair_shape = jax.ShapeDtypeStruct((2, width), f32)
    spread_shape = jax.ShapeDtypeStruct((width // GROUP, samples, GROUP), f32)

    unit_a, spread_a, lifted, *quarters_a = conv_call(
        first_body,
        "conv_first",
        place,
        sizes,
        False,
        [timed],
        pieces_a,
        [scale, shifting, gain_a, shift_a],
        [column, column, vector, vector],
        [field_shape, spread_shape, low_shape],
        [field, spreads, field],
        [turned_a],
    )
    pieces_b = gather_corners(lines_b, sides_b, sizes, spread_a)
    quarters_a = [quarters_a[0]] + [swap(quarters_a[r], r) for r in range(1, shards)]
    lifted = around(lifted)
    turned_b = turn(place, lifted, sizes, True)
    block_own, grad_second, sums_b, *quarters_b = conv_call(
        second_body,
        "conv_second",
        place,
        sizes,
        True,
        lifted,
        pieces_b,
        [residual, upstream, gain_b, shift_b],
        [field, field, vector, vector],
        [low_shape, low_shape, pair_shape],
        [field, field, pair],
        [turned_b],
    )
    block_all = around(block_own)
    quarters_b = [quarters_b[0]] + [swap(quarters_b[r], r) for r in range(1, shards)]

    grads_b = half_grad(lasting(7.5), turned_b, grad_second, sizes, True, 0)
    grads_b += half_grad(lasting(7.5), turned_b, grad_second, sizes, False, 1)
    grad_first, low, sums_a = back_call(
        lifted_back_body,
        "lifted_back",
        place,
        around(grad_second),
        quarters_b,
        [unit_a, spread_a, scale, gain_a, shift_a, *quarters_a[1:]],
        [field, spreads, column, vector, vector]
        + [pl.BlockSpec(memory_space=pl.ANY)] * (shards - 1),
        [
            low_shape,
            jax.ShapeDtypeStruct((2, samples, width), bf16),
            jax.ShapeDtypeStruct((4, width), f32),
        ],
        [field, films, fours],
        16,
    )
    if shards == 2:
        mine, other = (lax.dynamic_index_in_dim(low, row, 0, False) for row in (own, 1 - own))
        low_own = in_order([mine, swap(other, 1)], own)
    else:
        low = in_order(around(low), own).transpose(2, 1, 0, 3).reshape(samples, 2 * channels)
        low_own = own_columns(low, film_width)[None]
    lows = [low_own] + [move(low_own, sizes, 2, dx) for dx in range(1, nx)]
    block_all = [after(block_all[0], low_own)] + block_all[1:]
    block_out = from_time(place, matrix, block_all)
    got_near = near_got(grads_b, sizes)
    ready = lows[1:] + [block_out]
    near_left = add_near(grads_b[0], [after(part, *ready) for part in got_near[0]])
    near_right = add_near(grads_b[2], [after(part, *near_left[1]) for part in got_near[1]])
    near_b = (near_left, near_right)
    grad_first_all = around(grad_first)
    got_b = far_got(near_b, sizes)
    grads_a = half_grad(SHORT, turned_a, grad_first, sizes, True, 0, *near_left[1], *near_right[1])
    grads_a += half_grad(SHORT, turned_a, grad_first, sizes, False, 1, grads_a[0])
    got_b = tuple([after(part, grads_a[2]) for part in parts] for parts in got_b)
    whole_b = jnp.concatenate(far_sums(near_b, got_b), axis=2).astype(bf16)
    rows_b = lax.psum_scatter(
        whole_b, "dp", scatter_dimension=0, tiled=False, axis_index_groups=line_groups(sizes)
    )
    grad_conv_second = rows_b.astype(f32).reshape(conv_second.shape)
    film_keep, film_send, grad_table = film_back(
        place,
        embedded.T,
        lows,
        film_map,
        cond_in,
        onehot,
        sizes,
        whole_b,
    )
    grad_own = back_call(
        features_back_body,
        "features_back",
        place,
        grad_first_all,
        quarters_a,
        [upstream, film_send],
        [field, pl.BlockSpec(memory_space=pl.ANY)],
        [low_shape],
        [field],
        2,
    )
    got_near = near_got(grads_a, sizes)
    near_left = add_near(grads_a[0], [after(part, *grad_own) for part in got_near[0]])
    near_right = add_near(grads_a[2], [after(part, *near_left[1]) for part in got_near[1]])
    got_a = far_got((near_left, near_right), sizes)
    film_got = [move(film_send[dy - 1], sizes, 1, dy) for dy in range(1, ny)]
    film_got = [after(part, *near_right[1]) for part in film_got]
    film_value = add_halves(film_keep, film_got)
    left = add_halves(near_left[0], [after(part, film_value[0]) for part in got_a[0]])
    ready = (left[0],)
    right = add_halves(near_right[0], [after(part, *ready) for part in got_a[1]])

    grad_all = around(grad_own[0])
    masks = line_masks(nz)[0][::-1]
    values, film_ready = [left, right], right[0]
    for mask in masks[:-1]:
        got = [trade(value[1], sizes, 0, mask) for value in values]
        film_got = after(trade(film_value[1], sizes, 0, mask), film_ready)
        got[0] = after(got[0], got[1], rows_b)
        values = [add_halves(value[0], [part]) for value, part in zip(values, got)]
        film_value = add_halves(film_value[0], [film_got])
        film_ready = values[1][0]
    grad_all = [after(grad_all[0], values[0][0], values[1][0])] + grad_all[1:]
    grad_features = from_time(place, matrix, grad_all)

    sums = jnp.concatenate([sums_a[:2], sums_b, sums_a[2:]])
    sums = lax.dynamic_update_slice(jnp.zeros((6, channels), f32), sums, (0, own * width)).reshape(-1)
    wide = grad_table.shape[1]
    rows = -(-(tasks + -(-sums.shape[0] // wide)) // 8) * 8
    sums = jnp.pad(sums, (0, (rows - tasks) * wide - sums.shape[0])).reshape(rows - tasks, wide)
    total = sum_shards(jnp.concatenate([grad_table[:tasks], sums]), *near_left[1])
    total = sum_along(total, sizes, 0, near_right[1], [left[0]])
    total = sum_along(total, sizes, 1, [right[0]])
    totals = [total] + [after(move(total, sizes, 2, r), values[0][0]) for r in range(1, nx)]
    totals = in_order(totals, position[2])
    totals = in_order(around(totals), own)
    totals = jnp.moveaxis(totals, 0, 1).reshape(nx, rows, wide)

    grad_table = totals[:, :tasks].reshape(nx, tasks, nz * ny, depth)[..., :film_rows]
    grad_table = grad_table.transpose(1, 2, 0, 3).reshape(tasks, -1)
    sums = totals[0, tasks:]
    for x in range(1, nx):
        sums = sums + totals[x, tasks:]
    sums = sums.reshape(-1)[: 6 * channels].reshape(6, channels)

    index = me * shards + own
    small = [lax.dynamic_slice(sums[i], (index * each,), (each,)) for i in range(4)]
    grad_film_bias = lax.dynamic_slice(sums[4:].reshape(-1), (index * 2 * each,), (2 * each,))
    ready = [grad_features, grad_table, grad_conv_second, grad_film_bias, *small]
    got = [trade(value[1], sizes, 0, masks[-1]) for value in values]
    got[0] = after(got[0], got[1], *ready)
    film_got = trade(film_value[1], sizes, 0, masks[-1])
    grad_conv_first = [add_far(value[0], [part])[0] for value, part in zip(values, got)]
    grad_conv_first = jnp.concatenate(grad_conv_first, axis=1).reshape(conv_first.shape)
    grad_film_weight = add_far(film_value[0], [after(film_got, grad_table)])[0, :film_rows]
    return (
        block_out,
        grad_features,
        grad_conv_first,
        grad_conv_second,
        grad_film_weight,
        small[0],
        small[1],
        small[2],
        small[3],
        grad_film_bias,
        grad_table,
    )


def solution(mesh):
    return jax.shard_map(
        local,
        mesh=mesh,
        in_specs=(
            P("dp", None),
            P("dp", None),
            P("dp"),
            P(None, "dp", "shard"),
            P(None, "dp", "shard"),
            P("dp", "shard"),
            P(("dp", "shard")),
            P(("dp", "shard")),
            P(("dp", "shard")),
            P(("dp", "shard")),
            P(("dp", "shard")),
            P(),
            P("dp", None),
            P("dp"),
        ),
        out_specs=(
            P("dp", None),
            P("dp", None),
            P(None, "dp", "shard"),
            P(None, "dp", "shard"),
            P("dp", "shard"),
            P(("dp", "shard")),
            P(("dp", "shard")),
            P(("dp", "shard")),
            P(("dp", "shard")),
            P(("dp", "shard")),
            P(),
        ),
        check_vma=False,
    )
```
